128 devices in a mesh: dp: 4 (over y), item: 32 (over z, x, core).
Axes of the slice: x: 4, y: 4, z: 4, core: 2. Of those that a mesh axis runs over, the one named last changes fastest.
Arguments:
- queries: bfloat16 [131072, 256], P(('dp', 'item')), may hold values from -0.5 to 0.5
- item_table: float32 [131072, 256], P('item'), may hold values from -0.5 to 0.5
- adagrad_state: float32 [131072], P('item'), may hold values from 1 to 1000
- pos_owner: int32 [131072, 1], P(('dp', 'item')), may hold values from 0 to 31; in each aligned block of 1024 rows (0 to 1023, 1024 to 2047, ...) at most 96 rows name the same one
- pos_row: int32 [131072], P(('dp', 'item')), may hold values from 0 to 4095
- neg_rows: int32 [6144], P(('dp', 'item')), may hold values from 0 to 4095
Outputs:
- query_grad: bfloat16 [131072, 256], P(('dp', 'item'))
- example_loss: float32 [131072], P(('dp', 'item'))
- new_table: float32 [131072, 256], P('item')
- new_state: float32 [131072], P('item')
The draws below stay inside these ranges and needn't reach their ends.
Inputs may be any that keep to these rules, and one draw needn't show every extreme that they name: `pos_owner`: within the rows of one device (aligned blocks of 1024 examples) no shard is named more than 96 times; some device's block names one shard exactly 96 times.
All inputs are finite; a program needn't handle non-finite values.
Results may differ from the reference program's by a relative error of at most 0.0049.
Values may be sent and summed in bfloat16 or wider, within the bound.
A program may use at most 64 MiB of HBM per device.

```python
import math
import jax
import jax.numpy as jnp
import numpy as np
from jax import lax

D = 256
ROWS_DEV = 4096
EX_DEV = 1024
NEG_DEV = 48
CAP = 96
TABLE_ROWS = 131072
EXAMPLES = 131072
NEGS = 6144
N_ITEM = 32


def with_ends(values, stream_key, smallest, largest):
    dims = values.shape
    place = [jax.random.randint(jax.random.fold_in(stream_key, axis), (), 0, dims[axis]) for axis in range(len(dims))]
    values = values.at[tuple(place)].set(smallest)
    longest = dims.index(max(dims))
    place[longest] = (place[longest] + 1) % dims[longest]
    return values.at[tuple(place)].set(largest)


def shard_levels(key, dims, cuts, least, high):
    gain, own = 1.0, jax.random.fold_in(key, 6)
    for position, parts in cuts:
        steps = jnp.exp(jax.random.uniform(jax.random.fold_in(own, position), (parts,), jnp.float32, least / len(cuts), high / len(cuts)))
        gain = gain * jnp.repeat(steps, dims[position] // parts).reshape([-1 if axis == position else 1 for axis in range(len(dims))])
    return gain


def routed_block(rng, own, number, rows, number_of, top, most, skew):
    ranking = jax.random.permutation(rng, number_of)
    crowded, usual = portions_of(number_of, rows * top, most, skew, True), portions_of(number_of, rows * top, most, skew, False)
    places = jnp.arange(number_of)

    def named(sizes, turn):
        used = int((sizes > 0).sum())
        fixed = max(1, used // 4)
        shifted = fixed + (places - fixed + turn * (used - fixed)) % max(1, number_of - fixed)
        return jnp.zeros((number_of,), jnp.int32).at[ranking[jnp.where(places < fixed, places, shifted)]].set(jnp.asarray(sizes, jnp.int32))

    sizes = jnp.where(number % 4 == 0, named(crowded, number // 4), named(usual, number - number // 4 - 1))
    mixed = jax.random.permutation(jax.random.fold_in(own, 3), number_of)
    giver, sink = mixed[0:number_of // 2 * 2:2], mixed[1:number_of // 2 * 2:2]
    slack = jnp.minimum(sizes[giver] - 1, most - sizes[sink]) // 2
    slack = jnp.where((giver == ranking[0]) | (sink == ranking[0]) | (sizes[sink] == 0), 0, jnp.maximum(slack, 0))
    shifted = jax.random.randint(jax.random.fold_in(own, 4), (number_of // 2,), 0, 1 << 20) % (slack + 1)
    sizes = sizes.at[giver].add(-shifted).at[sink].add(shifted)
    items = jnp.searchsorted(jnp.cumsum(sizes), jnp.arange(rows * top), side="right").astype(jnp.int32)
    listing = items.reshape(top, rows).T
    listing = listing[jax.random.permutation(jax.random.fold_in(own, 1), rows)]
    turn = jax.random.randint(jax.random.fold_in(own, 2), (rows, 1), 0, top)
    return jnp.take_along_axis(listing, (jnp.arange(top)[None, :] + turn) % top, axis=1)


def portions_of(amount, total, limit, lean, full):
    weights = [(1 << 20) // math.isqrt(grade ** lean) + 1 for grade in range(1, amount + 1)]
    largest = limit if full else min(limit, max(-(-total // amount), total * weights[0] // sum(weights)))
    least = 1 if total - largest >= amount - 1 else 0
    holding, surplus = [largest] + [least] * (amount - 1), total - largest - least * (amount - 1)
    while surplus > 0:
        candidates = [i for i in range(1, amount) if holding[i] < largest] or [i for i in range(1, amount) if holding[i] < limit]
        mass, left = sum([weights[i] for i in candidates]), surplus
        for i in candidates:
            addition = min(limit - holding[i], max(1, left * weights[i] // mass), surplus)
            holding[i] = holding[i] + addition
            surplus = surplus - addition
    return np.array(holding)


def gaussian(rng, extent, deviation, most, cuts=(), kind=jnp.bfloat16):
    gain = shard_levels(rng, extent, cuts, -0.22, 0.18) if cuts else 1.0
    result = jax.random.normal(rng, extent, jnp.float32) * deviation * gain
    return jnp.minimum(jnp.maximum(result, -most), most).astype(kind)


def setup_inputs(seed: int = 0) -> dict:
    seeds = jax.random.split(jax.random.key(seed), 7)
    queries = gaussian(seeds[0], (EXAMPLES, D), 0.0625, 0.5, ((0, 128),))
    item_table = gaussian(seeds[1], (TABLE_ROWS, D), 0.0625, 0.5, ((0, 32),), jnp.float32)
    adagrad_state = jnp.clip(jnp.exp(math.log(1000.0) - 6.9077553 * jax.random.uniform(seeds[2], (TABLE_ROWS,), jnp.float32) ** shard_levels(seeds[2], (TABLE_ROWS,), ((0, 32),), -0.2, 0.2)), 1.0, 1000.0)
    pos_owner_keys = jax.random.split(jax.random.fold_in(seeds[3], 1), EXAMPLES // EX_DEV)
    pos_owner_turns = jax.random.permutation(jax.random.fold_in(seeds[3], 3), EXAMPLES // EX_DEV)
    pos_owner = jax.vmap(lambda own, number: routed_block(jax.random.fold_in(seeds[3], 2), own, number, EX_DEV, N_ITEM, 1, CAP, 2))(pos_owner_keys, pos_owner_turns).reshape((EXAMPLES, 1))
    pos_row = with_ends(jax.random.randint(seeds[4], (EXAMPLES,), 0, ROWS_DEV), jax.random.fold_in(seeds[4], 1), 0, ROWS_DEV - 1).astype(jnp.int32)
    neg_rows = with_ends(jax.random.randint(seeds[5], (NEGS,), 0, ROWS_DEV), jax.random.fold_in(seeds[5], 1), 0, ROWS_DEV - 1).astype(jnp.int32)
    return dict(queries=queries, item_table=item_table, adagrad_state=adagrad_state, pos_owner=pos_owner, pos_row=pos_row, neg_rows=neg_rows)


INV_TEMP = 20.0
LEARN_RATE = 0.05
EPSILON = 1e-06

def unit_rows(matrix):
    row_norm = jnp.sqrt(lax.optimization_barrier(jnp.sum(matrix * matrix, axis=-1, keepdims=True)) + EPSILON)
    return (matrix / row_norm, row_norm)

def reference(queries, item_table, adagrad_state, pos_owner, pos_row, neg_rows):
    query_f = queries.astype(jnp.float32)
    query_hat, query_norm = unit_rows(query_f)
    unit_table, table_norm = unit_rows(item_table)
    table_send = unit_table.astype(jnp.bfloat16)
    query_send = query_hat.astype(jnp.bfloat16)
    pos_gid = (pos_owner[:, 0] * ROWS_DEV + pos_row).astype(jnp.int32)
    neg_owner = jnp.arange(NEGS, dtype=jnp.int32) // NEG_DEV % N_ITEM
    neg_gid = (neg_owner * ROWS_DEV + neg_rows).astype(jnp.int32)
    neg_e = table_send[neg_gid]
    pos_e = table_send[pos_gid]
    blocks = EXAMPLES // EX_DEV

    def one_block(carry, pieces):
        q_send, q_hat, q_norm, p_e, p_gid = pieces
        scores = jnp.dot(q_send, neg_e.T, preferred_element_type=jnp.float32) * INV_TEMP
        allowed = neg_gid[None, :] != p_gid[:, None]
        s_pos = INV_TEMP * lax.optimization_barrier(jnp.sum(q_send.astype(jnp.float32) * p_e.astype(jnp.float32), axis=1))
        totals = jnp.exp(s_pos) + lax.optimization_barrier(jnp.sum(jnp.where(allowed, jnp.exp(scores), 0.0), axis=1))
        lse = jnp.log(totals)
        loss = lse - s_pos
        probs = jnp.where(allowed, jnp.exp(scores - lse[:, None]), 0.0).astype(jnp.bfloat16)
        p_pos = jnp.exp(s_pos - lse)
        g_q = INV_TEMP * ((p_pos - 1.0)[:, None] * p_e.astype(jnp.float32) + jnp.dot(probs, neg_e, preferred_element_type=jnp.float32))
        q_grad = ((g_q - q_hat * lax.optimization_barrier(jnp.sum(q_hat * g_q, axis=1, keepdims=True))) / q_norm).astype(jnp.bfloat16)
        g_pos = INV_TEMP * (p_pos - 1.0)[:, None] * q_hat
        carry = carry + INV_TEMP * jnp.dot(probs.T, q_send, preferred_element_type=jnp.float32)
        return (carry, (q_grad, loss, g_pos))
    pieces = (query_send.reshape(blocks, EX_DEV, D), query_hat.reshape(blocks, EX_DEV, D), query_norm.reshape(blocks, EX_DEV, 1), pos_e.reshape(blocks, EX_DEV, D), pos_gid.reshape(blocks, EX_DEV))
    g_neg, (q_grad, loss, g_pos) = lax.scan(one_block, jnp.zeros((NEGS, D), jnp.float32), pieces)
    g_unit = jnp.zeros((TABLE_ROWS, D), jnp.float32)
    g_unit = g_unit.at[pos_gid].add(g_pos.reshape(EXAMPLES, D))
    g_unit = g_unit.at[neg_gid].add(g_neg)
    g_row = (g_unit - unit_table * lax.optimization_barrier(jnp.sum(unit_table * g_unit, axis=1, keepdims=True))) / table_norm
    new_state = adagrad_state + lax.optimization_barrier(jnp.mean(g_row * g_row, axis=1))
    new_table = item_table - LEARN_RATE * g_row / jnp.sqrt(new_state)[:, None]
    return (q_grad.reshape(EXAMPLES, D), loss.reshape(EXAMPLES), new_table, new_state)
```

```python
import functools

import jax
import jax.numpy as jnp
from jax import lax
from jax.experimental import pallas as pl
from jax.experimental.pallas import tpu as pltpu
from jax.sharding import PartitionSpec as P

INV_TEMP = 20.0
LEARN_RATE = 0.05
EPSILON = 1e-06
LOG2E = 1.4426950408889634
BF, F32 = jnp.bfloat16, jnp.float32
LANES = 128


def dot(a, b):
    return jnp.dot(a, b, preferred_element_type=F32)


def iota(shape, dim):
    return lax.broadcasted_iota(jnp.int32, shape, dim).astype(F32)


def eye():
    return lax.broadcasted_iota(jnp.int32, (LANES, LANES), 0) == lax.broadcasted_iota(jnp.int32, (LANES, LANES), 1)


def row_to_col(row):
    parts = []
    for k in range(row.shape[1] // LANES):
        wide = jnp.broadcast_to(row[:, k * LANES : (k + 1) * LANES], (LANES, LANES))
        parts.append(jnp.sum(jnp.where(eye(), wide, 0.0), axis=1, keepdims=True))
    return parts[0] if len(parts) == 1 else jnp.concatenate(parts, axis=0)


def col_to_row(col):
    parts = []
    for k in range(col.shape[0] // LANES):
        wide = jnp.broadcast_to(col[k * LANES : (k + 1) * LANES], (LANES, LANES))
        parts.append(jnp.sum(jnp.where(eye(), wide, 0.0), axis=0, keepdims=True))
    return parts[0] if len(parts) == 1 else jnp.concatenate(parts, axis=1)


def main_kernel(
    n_dp, n_item,
    q_ref, table_ref, owner_ref, row_ref, neg_ref,
    grad_ref, loss_ref, g_ref, negsum_ref, negid_ref,
    tsend, qt, req_out, req_in, negbuf, nidbuf, found, returned, outbox, inbox, acc, ut, tot, et, part, sib_in, red_in, red_out, y_in,
    dense_f, rs_out, relay_in, rs_in, ag,
    req_s, req_r, neg_s, neg_r, nid_s, nid_r, pos_s, pos_r, g_s, g_r, sib_s, sib_r, red_s, red_r, y_s, y_r,
    rs_s, relay_r, rs_r, ag_s, ag_r,
):
    ex, width = q_ref.shape
    rows = table_ref.shape[0]
    chips = n_item // 2
    cap = 3 * ex // n_item
    neg = negbuf.shape[2]
    y, me = lax.axis_index("dp"), lax.axis_index("item")
    chip, core = me // 2, lax.rem(me, 2)
    sibling = chip * 2 + 1 - core
    up, far, down = lax.rem(y + 1, n_dp), lax.rem(y + 2, n_dp), lax.rem(y + 3, n_dp)

    def copy(src, dst, send, recv, **where):
        return pltpu.make_async_remote_copy(
            src_ref=src, dst_ref=dst, send_sem=send, recv_sem=recv, device_id=where, device_id_type=pl.DeviceIdType.MESH
        )

    barrier = pltpu.get_barrier_semaphore()

    @pl.loop(1, n_item)
    def _(off):
        pl.semaphore_signal(barrier, inc=1, device_id={"item": lax.rem(me + off, n_item)}, device_id_type=pl.DeviceIdType.MESH)

    @pl.loop(1, n_dp)
    def _(off):
        pl.semaphore_signal(barrier, inc=1, device_id={"dp": lax.rem(y + off, n_dp)}, device_id_type=pl.DeviceIdType.MESH)

    owner_c = owner_ref[...].astype(F32)
    row_r = row_ref[...].astype(F32)
    row_c = row_to_col(row_r)
    owner_r = col_to_row(owner_c)
    gid_r = owner_r * rows + row_r
    onehot_c = (owner_c == iota((ex, LANES), 1)).astype(F32)
    before = (iota((ex, ex), 1) < iota((ex, ex), 0)).astype(BF)
    slot_c = jnp.sum(dot(before, onehot_c.astype(BF)) * onehot_c, axis=1, keepdims=True)
    place_c = owner_c * cap + slot_c
    place_r = col_to_row(place_c)
    high_c = jnp.floor(row_c * (1.0 / 64.0))
    low_c = row_c - 64.0 * high_c
    at_slot = slot_c == iota((ex, LANES), 1)
    both = jnp.concatenate([jnp.where(at_slot, high_c, 0.0), jnp.where(at_slot, low_c, 0.0)], axis=1).astype(BF)
    owners_r = (owner_r == iota((n_item, ex), 0)).astype(BF)
    asked2 = dot(owners_r, both)
    asked = asked2[:, :LANES] * 64.0 + asked2[:, LANES:]
    for s in range(n_item):
        req_out[s] = asked[s : s + 1, :]

    tile = min(512, rows)

    @pl.loop(0, rows // tile)
    def _(k):
        at = pl.ds(pl.multiple_of(k * tile, tile), tile)
        t = table_ref[at, :]
        tsend[at, :] = (t / jnp.sqrt(jnp.sum(t * t, axis=1, keepdims=True) + EPSILON)).astype(BF)

    neg_row = neg_ref[...].astype(F32)
    neg_c = row_to_col(neg_row)[:neg]
    mine = y * 2 + core
    my_neg = jnp.zeros((neg, width), F32)
    for k in range(rows // tile):
        pick = (neg_c == iota((neg, tile), 1) + float(k * tile)).astype(BF)
        my_neg += dot(pick, tsend[k * tile : (k + 1) * tile, :])
    negbuf[mine, chip] = my_neg.astype(BF)
    nidbuf[mine, chip] = neg_row

    pl.semaphore_wait(barrier, n_item - 1 + n_dp - 1)

    req_in[me] = req_out[me]

    def req_copy(peer):
        return copy(req_out.at[peer], req_in.at[me], req_s.at[peer], req_r.at[me], item=peer)

    @pl.loop(1, n_item)
    def _(off):
        req_copy(lax.rem(me + off, n_item)).start()

    def plane_copies(peer_chip):
        to = peer_chip * 2 + core
        return (
            copy(negbuf.at[mine, chip], negbuf.at[mine, chip], neg_s.at[peer_chip], neg_r.at[chip], item=to),
            copy(nidbuf.at[mine, chip], nidbuf.at[mine, chip], nid_s.at[peer_chip], nid_r.at[chip], item=to),
        )

    @pl.loop(1, chips)
    def _(off):
        for c in plane_copies(lax.rem(chip + off, chips)):
            c.start()

    q = q_ref[...].astype(F32)
    q_norm = jnp.sqrt(jnp.sum(q * q, axis=1, keepdims=True) + EPSILON)
    acc[...] = q / q_norm
    qt[...] = jnp.transpose(acc[...]).astype(BF)

    def wait_recv(dst, send, recv, **where):
        copy(dst, dst, send, recv, **where).wait_recv()

    @pl.loop(1, chips)
    def _(off):
        src = lax.rem(chip + off, chips)
        wait_recv(negbuf.at[mine, src], neg_s.at[src], neg_r.at[src], item=src * 2 + core)
        wait_recv(nidbuf.at[mine, src], nid_s.at[src], nid_r.at[src], item=src * 2 + core)

    pieces = 2 * n_dp

    def y_copies(dest):
        at = chips + mine
        s_at = chips + dest
        return (
            copy(negbuf.at[mine], negbuf.at[mine], neg_s.at[s_at], neg_r.at[at], dp=dest),
            copy(nidbuf.at[mine], nidbuf.at[mine], nid_s.at[s_at], nid_r.at[at], dp=dest),
        )

    def sib_copies(piece):
        at = chips + pieces + piece
        return (
            copy(negbuf.at[piece], negbuf.at[piece], neg_s.at[at], neg_r.at[at], item=sibling),
            copy(nidbuf.at[piece], nidbuf.at[piece], nid_s.at[at], nid_r.at[at], item=sibling),
        )

    @pl.loop(1, n_dp)
    def _(off):
        for c in y_copies(lax.rem(y + off, n_dp)):
            c.start()

    for c in sib_copies(mine):
        c.start()

    @pl.loop(1, n_item)
    def _(off):
        src = lax.rem(me + off, n_item)
        wait_recv(req_in.at[src], req_s.at[src], req_r.at[src], item=src)

    batch = min(8, n_item)
    batches = n_item // batch

    def pos_copy(peer):
        return copy(found.at[peer], returned.at[me], pos_s.at[peer], pos_r.at[me], item=peer)

    @pl.loop(0, batches)
    def _(k):
        first = lax.rem(k + me // batch, batches) * batch
        ids = jnp.concatenate([row_to_col(req_in[first + s])[:cap] for s in range(batch)], axis=0)
        got = jnp.zeros((batch * cap, width), F32)
        for t in range(rows // tile):
            pick = (ids == iota((batch * cap, tile), 1) + float(t * tile)).astype(BF)
            got += dot(pick, tsend[t * tile : (t + 1) * tile, :])
        found[pl.ds(first, batch)] = got.astype(BF).reshape(batch, cap, width)
        for s in range(batch):

            @pl.when(first + s != me)
            def _():
                pos_copy(first + s).start()

    returned[me] = found[me]

    tot[...] = jnp.zeros_like(tot)
    ut[...] = jnp.zeros_like(ut)
    half = max(1, chips // 2)

    def pass1(piece):
        @pl.loop(0, chips // half)
        def _(h):
            first = h * half
            block = negbuf[piece, pl.ds(first, half)].reshape(half * neg, width)
            ids = jnp.concatenate(
                [
                    row_to_col(nidbuf[piece, first + z])[:neg]
                    + (((first + z) * 2 + lax.rem(piece, 2)) * rows).astype(F32)
                    for z in range(half)
                ],
                axis=0,
            )
            e = jnp.where(ids != gid_r, jnp.exp2(dot(block, qt[...]) * (INV_TEMP * LOG2E)), 0.0)
            tot[...] += jnp.sum(e.reshape(half * neg // 8, 8, ex), axis=0)
            eb = e.astype(BF)
            et[piece, pl.ds(first, half)] = eb.reshape(half, neg, ex)
            ut[...] += lax.dot_general(block, eb, (((0,), (0,)), ((), ())), preferred_element_type=F32)

    pass1(mine)

    @pl.loop(0, n_dp)
    def _(off):
        @pl.when(off > 0)
        def _():
            piece = lax.rem(y + off, n_dp) * 2 + core
            wait_recv(negbuf.at[piece], neg_s.at[chips + piece // 2], neg_r.at[chips + piece], dp=piece // 2)
            wait_recv(nidbuf.at[piece], nid_s.at[chips + piece // 2], nid_r.at[chips + piece], dp=piece // 2)
            for c in sib_copies(piece):
                c.start()
            pass1(piece)

    @pl.loop(0, n_dp)
    def _(off):
        piece = lax.rem(y + off, n_dp) * 2 + 1 - core
        at = chips + pieces + piece
        wait_recv(negbuf.at[piece], neg_s.at[at], neg_r.at[at], item=sibling)
        wait_recv(nidbuf.at[piece], nid_s.at[at], nid_r.at[at], item=sibling)
        pass1(piece)

    @pl.loop(1, n_item)
    def _(off):
        src = lax.rem(me + off, n_item)
        wait_recv(returned.at[src], pos_s.at[src], pos_r.at[src], item=src)

    q_hat = acc[...]
    pos_e = jnp.zeros((ex, width), F32)
    for k in range(batches):
        pick = (place_c == iota((ex, batch * cap), 1) + float(k * batch * cap)).astype(BF)
        pos_e += dot(pick, returned[k * batch : (k + 1) * batch].reshape(batch * cap, width))
    s_pos = INV_TEMP * jnp.sum(q_hat.astype(BF).astype(F32) * pos_e, axis=1, keepdims=True)
    neg_tot = row_to_col(jnp.sum(tot[...], axis=0, keepdims=True))
    lse = jnp.log(jnp.exp(s_pos) + neg_tot)
    loss_ref[...] = col_to_row(lse - s_pos)
    coef = jnp.exp(s_pos - lse) - 1.0
    inv_tot = jnp.exp(-lse)

    g_pos = (INV_TEMP * coef * q_hat).astype(BF)

    def g_copy(peer):
        return copy(outbox.at[peer], inbox.at[me], g_s.at[peer], g_r.at[me], item=peer)

    for k in range(batches):
        pick = (place_r == iota((batch * cap, ex), 0) + float(k * batch * cap)).astype(BF)
        outbox[k * batch : (k + 1) * batch] = dot(pick, g_pos).astype(BF).reshape(batch, cap, width)

    @pl.loop(1, n_item)
    def _(off):
        g_copy(lax.rem(me + off, n_item)).start()

    inbox[me] = outbox[me]

    q_scaled = (q_hat.astype(BF).astype(F32) * (INV_TEMP * inv_tot)).astype(BF)

    def pass2(side):
        @pl.loop(0, n_dp)
        def _(d):
            for h in range(chips // half):
                at = slice(h * half, (h + 1) * half)
                p = dot(et[d * 2 + side, at].reshape(half * neg, ex), q_scaled)
                p = p.astype(BF).reshape(half, neg, width)
                for z in range(half):
                    part[side, h * half + z, pl.ds(pl.multiple_of(d * neg, neg), neg), :] = p[z]

    pass2(1 - core)
    to_sib = copy(part.at[1 - core], sib_in, sib_s, sib_r, item=sibling)
    to_sib.start()
    pass2(core)

    g_q = INV_TEMP * (coef * pos_e + jnp.transpose(ut[...]) * inv_tot)
    grad_ref[...] = ((g_q - q_hat * jnp.sum(q_hat * g_q, axis=1, keepdims=True)) / q_norm).astype(BF)

    to_sib.wait_recv()

    @pl.loop(0, chips)
    def _(z):
        red_out[z] = (part[core, z].astype(F32) + sib_in[z].astype(F32)).astype(BF)

    @pl.loop(1, n_item)
    def _(off):
        src = lax.rem(me + off, n_item)
        wait_recv(inbox.at[src], g_s.at[src], g_r.at[src], item=src)

    def red_copy(peer_chip):
        return copy(red_out.at[peer_chip], red_in.at[chip], red_s.at[peer_chip], red_r.at[chip], item=peer_chip * 2 + core)

    @pl.loop(1, chips)
    def _(off):
        red_copy(lax.rem(chip + off, chips)).start()

    quarter = rows // n_dp
    hq = quarter // 2
    four = 4

    def dense(dest):
        dense_f[...] = jnp.zeros_like(dense_f)

        @pl.loop(0, n_item // four)
        def _(k):
            ids = jnp.concatenate([req_in[k * four + s][:, :cap] for s in range(four)], axis=1)
            base = (dest * quarter).astype(F32)
            pick = (ids == iota((quarter, four * cap), 0) + base).astype(BF)
            dense_f[...] += dot(pick, inbox[pl.ds(k * four, four)].reshape(four * cap, width))

    def rs_copies():
        return (
            copy(rs_out.at[0, 0], relay_in.at[0], rs_s.at[0, 0], relay_r.at[0], dp=up),
            copy(rs_out.at[0, 1], relay_in.at[1], rs_s.at[0, 1], relay_r.at[1], dp=down),
            copy(rs_out.at[1, 0], rs_in.at[0, 0], rs_s.at[1, 0], rs_r.at[0, 0], dp=up),
            copy(rs_out.at[1, 1], rs_in.at[0, 1], rs_s.at[1, 1], rs_r.at[0, 1], dp=up),
            copy(rs_out.at[2, 0], rs_in.at[1, 0], rs_s.at[2, 0], rs_r.at[1, 0], dp=down),
            copy(rs_out.at[2, 1], rs_in.at[1, 1], rs_s.at[2, 1], rs_r.at[1, 1], dp=down),
        )

    far0, far1, up0, up1, down0, down1 = rs_copies()
    dense(far)
    rs_out[0, 0] = dense_f[:hq, :].astype(BF)
    rs_out[0, 1] = dense_f[hq:, :].astype(BF)
    far0.start()
    far1.start()
    dense(up)
    rs_out[1, 1] = dense_f[hq:, :].astype(BF)
    up1.start()
    far0.wait_recv()
    rs_out[1, 0] = (dense_f[:hq, :] + relay_in[0].astype(F32)).astype(BF)
    up0.start()
    dense(down)
    rs_out[2, 0] = dense_f[:hq, :].astype(BF)
    down0.start()
    far1.wait_recv()
    rs_out[2, 1] = (dense_f[hq:, :] + relay_in[1].astype(F32)).astype(BF)
    down1.start()
    dense(y)

    total = red_out[chip].astype(F32)

    def add_red(off, total):
        src = lax.rem(chip + off, chips)
        wait_recv(red_in.at[src], red_s.at[src], red_r.at[src], item=src * 2 + core)
        return total + red_in[src].astype(F32)

    total = lax.fori_loop(1, chips, add_red, total)
    y_in[y] = total.astype(BF)

    def sum_copy(dest):
        return copy(y_in.at[y], y_in.at[y], y_s.at[dest], y_r.at[y], dp=dest)

    @pl.loop(1, n_dp)
    def _(off):
        sum_copy(lax.rem(y + off, n_dp)).start()

    up1.wait_recv()
    up0.wait_recv()
    down0.wait_recv()
    down1.wait_recv()
    for h in range(2):
        at = slice(h * hq, (h + 1) * hq)
        ag[y, h] = (dense_f[at, :] + rs_in[0, h].astype(F32) + rs_in[1, h].astype(F32)).astype(BF)

    def ag_copy(slot, h, way, dest):
        return copy(ag.at[slot, h], ag.at[slot, h], ag_s.at[way, h], ag_r.at[slot, h], dp=dest)

    for h in range(2):
        ag_copy(y, h, 0, up).start()
        ag_copy(y, h, 1, down).start()
    wait_recv(ag.at[down, 0], ag_s.at[0, 0], ag_r.at[down, 0], dp=down)
    ag_copy(down, 0, 2, up).start()
    wait_recv(ag.at[up, 1], ag_s.at[0, 1], ag_r.at[up, 1], dp=up)
    ag_copy(up, 1, 2, down).start()

    @pl.loop(1, n_dp)
    def _(off):
        src = lax.rem(y + off, n_dp)
        wait_recv(y_in.at[src], y_s.at[src], y_r.at[src], dp=src)

    sums = y_in[0].astype(F32)
    for d in range(1, n_dp):
        sums += y_in[d].astype(F32)
    negsum_ref[...] = sums
    for d in range(n_dp):
        negid_ref[d : d + 1, :] = nidbuf[d * 2 + core, chip]

    wait_recv(ag.at[down, 1], ag_s.at[0, 1], ag_r.at[down, 1], dp=down)
    wait_recv(ag.at[up, 0], ag_s.at[0, 0], ag_r.at[up, 0], dp=up)
    wait_recv(ag.at[far, 0], ag_s.at[0, 0], ag_r.at[far, 0], dp=down)
    wait_recv(ag.at[far, 1], ag_s.at[0, 1], ag_r.at[far, 1], dp=up)
    g_ref[...] = ag[...].reshape(rows, width)

    @pl.loop(1, n_item)
    def _(off):
        peer = lax.rem(me + off, n_item)
        req_copy(peer).wait_send()
        pos_copy(peer).wait_send()
        g_copy(peer).wait_send()

    @pl.loop(1, chips)
    def _(off):
        peer = lax.rem(chip + off, chips)
        for c in plane_copies(peer):
            c.wait_send()
        red_copy(peer).wait_send()

    @pl.loop(1, n_dp)
    def _(off):
        dest = lax.rem(y + off, n_dp)
        for c in y_copies(dest):
            c.wait_send()
        sum_copy(dest).wait_send()

    @pl.loop(0, n_dp)
    def _(d):
        for c in sib_copies(d * 2 + core):
            c.wait_send()

    to_sib.wait_send()
    for c in rs_copies():
        c.wait_send()
    for h in range(2):
        ag_copy(y, h, 0, up).wait_send()
        ag_copy(y, h, 1, down).wait_send()
    ag_copy(down, 0, 2, up).wait_send()
    ag_copy(up, 1, 2, down).wait_send()


def step_kernel(g_ref, negsum_ref, negid_ref, table_ref, state_ref, table_out, state_out):
    tile, width = g_ref.shape
    neg = negsum_ref.shape[0] // negid_ref.shape[0]
    base = (pl.program_id(0) * tile).astype(F32)
    g = g_ref[...].astype(F32)
    numbers = iota((tile, LANES), 0) + base
    ids = jnp.concatenate([negid_ref[d : d + 1, :][:, :neg] for d in range(negid_ref.shape[0])], axis=1)
    sums = negsum_ref[...]
    high = sums.astype(BF)
    pick = (ids == iota((tile, negsum_ref.shape[0]), 0) + base).astype(BF)
    g += dot(pick, high) + dot(pick, (sums - high.astype(F32)).astype(BF))
    t = table_ref[...]
    norm = jnp.sqrt(jnp.sum(t * t, axis=1, keepdims=True) + EPSILON)
    unit = t / norm
    g_row = (g - unit * jnp.sum(unit * g, axis=1, keepdims=True)) / norm
    mean = jnp.sum(g_row * g_row, axis=1, keepdims=True) * (1.0 / width)
    state_r = state_ref[...] + col_to_row(mean)
    state_out[...] = state_r
    table_out[...] = t - LEARN_RATE * g_row / jnp.sqrt(row_to_col(state_r))
    del numbers


def on_device(n_dp, n_item, queries, item_table, adagrad_state, pos_owner, pos_row, neg_rows):
    ex, width = queries.shape
    rows = item_table.shape[0]
    neg = neg_rows.shape[0]
    chips = n_item // 2
    cap = 3 * ex // n_item
    quarter = rows // n_dp
    vmem = pl.BlockSpec(memory_space=pltpu.VMEM)
    dma = pltpu.SemaphoreType.DMA
    negr = jnp.pad(neg_rows, (0, LANES - neg), constant_values=-1).reshape(1, LANES)
    n_neg = 2 * n_dp * chips * neg
    flops = 2 * width * (3 * n_neg * ex + 3 * n_item * cap * (rows + ex))
    grad, loss, g, negsum, negid = pl.pallas_call(
        functools.partial(main_kernel, n_dp, n_item),
        out_shape=(
            jax.ShapeDtypeStruct((ex, width), BF),
            jax.ShapeDtypeStruct((1, ex), F32),
            jax.ShapeDtypeStruct((rows, width), BF),
            jax.ShapeDtypeStruct((n_dp * neg, width), F32),
            jax.ShapeDtypeStruct((n_dp, LANES), F32),
        ),
        in_specs=[vmem] * 5,
        out_specs=(vmem,) * 5,
        scratch_shapes=[
            pltpu.VMEM((rows, width), BF),
            pltpu.VMEM((width, ex), BF),
            pltpu.VMEM((n_item, 1, LANES), F32),
            pltpu.VMEM((n_item, 1, LANES), F32),
            pltpu.VMEM((2 * n_dp, chips, neg, width), BF),
            pltpu.VMEM((2 * n_dp, chips, 1, LANES), F32),
            pltpu.VMEM((n_item, cap, width), BF),
            pltpu.VMEM((n_item, cap, width), BF),
            pltpu.VMEM((n_item, cap, width), BF),
            pltpu.VMEM((n_item, cap, width), BF),
            pltpu.VMEM((ex, width), F32),
            pltpu.VMEM((width, ex), F32),
            pltpu.VMEM((8, ex), F32),
            pltpu.VMEM((2 * n_dp, chips, neg, ex), BF),
            pltpu.VMEM((2, chips, n_dp * neg, width), BF),
            pltpu.VMEM((chips, n_dp * neg, width), BF),
            pltpu.VMEM((chips, n_dp * neg, width), BF),
            pltpu.VMEM((chips, n_dp * neg, width), BF),
            pltpu.VMEM((n_dp, n_dp * neg, width), BF),
            pltpu.VMEM((quarter, width), F32),
            pltpu.VMEM((3, 2, quarter // 2, width), BF),
            pltpu.VMEM((2, quarter // 2, width), BF),
            pltpu.VMEM((2, 2, quarter // 2, width), BF),
            pltpu.VMEM((n_dp, 2, quarter // 2, width), BF),
            dma((n_item,)), dma((n_item,)),
            dma((chips + 4 * n_dp,)), dma((chips + 4 * n_dp,)),
            dma((chips + 4 * n_dp,)), dma((chips + 4 * n_dp,)),
            dma((n_item,)), dma((n_item,)),
            dma((n_item,)), dma((n_item,)),
            dma, dma,
            dma((chips,)), dma((chips,)),
            dma((n_dp,)), dma((n_dp,)),
            dma((3, 2)), dma((2,)), dma((2, 2)),
            dma((3, 2)), dma((n_dp, 2)),
        ],
        compiler_params=pltpu.CompilerParams(collective_id=0, has_side_effects=True, vmem_limit_bytes=62 * 2**20),
        cost_estimate=pl.CostEstimate(flops=flops, bytes_accessed=12 * 2**20, transcendentals=n_neg * ex),
        name="loss_and_gradients",
    )(queries, item_table, pos_owner, pos_row.reshape(1, ex), negr)

    tile = min(512, rows)
    new_table, new_state = pl.pallas_call(
        step_kernel,
        grid=(rows // tile,),
        out_shape=(
            jax.ShapeDtypeStruct((rows, width), F32),
            jax.ShapeDtypeStruct((1, rows), F32),
        ),
        in_specs=[
            pl.BlockSpec((tile, width), lambda i: (i, 0)),
            pl.BlockSpec((n_dp * neg, width), lambda i: (0, 0)),
            pl.BlockSpec((n_dp, LANES), lambda i: (0, 0)),
            pl.BlockSpec((tile, width), lambda i: (i, 0)),
            pl.BlockSpec((1, tile), lambda i: (0, i)),
        ],
        out_specs=(
            pl.BlockSpec((tile, width), lambda i: (i, 0)),
            pl.BlockSpec((1, tile), lambda i: (0, i)),
        ),
        name="adagrad_step",
    )(g, negsum, negid, item_table, adagrad_state.reshape(1, rows))
    return grad, loss.reshape(ex), new_table, new_state.reshape(rows)


def solution(mesh):
    both = ("dp", "item")
    return jax.shard_map(
        functools.partial(on_device, mesh.shape["dp"], mesh.shape["item"]),
        mesh=mesh,
        in_specs=(P(both, None), P("item", None), P("item"), P(both, None), P(both), P(both)),
        out_specs=(P(both, None), P(both), P("item", None), P("item")),
        check_vma=False,
    )
```

```python
import functools

import jax
import jax.numpy as jnp
from jax import lax
from jax.experimental import pallas as pl
from jax.experimental.pallas import tpu as pltpu
from jax.sharding import PartitionSpec as P

INV_TEMP = 20.0
LEARN_RATE = 0.05
EPSILON = 1e-06
LOG2E = 1.4426950408889634
BF, F32 = jnp.bfloat16, jnp.float32
LANES = 128


def dot(a, b):
    return jnp.dot(a, b, preferred_element_type=F32)


def iota(shape, dim):
    return lax.broadcasted_iota(jnp.int32, shape, dim).astype(F32)


def eye():
    return lax.broadcasted_iota(jnp.int32, (LANES, LANES), 0) == lax.broadcasted_iota(jnp.int32, (LANES, LANES), 1)


def row_to_col(row):
    parts = []
    for k in range(row.shape[1] // LANES):
        wide = jnp.broadcast_to(row[:, k * LANES : (k + 1) * LANES], (LANES, LANES))
        parts.append(jnp.sum(jnp.where(eye(), wide, 0.0), axis=1, keepdims=True))
    return parts[0] if len(parts) == 1 else jnp.concatenate(parts, axis=0)


def col_to_row(col):
    parts = []
    for k in range(col.shape[0] // LANES):
        wide = jnp.broadcast_to(col[k * LANES : (k + 1) * LANES], (LANES, LANES))
        parts.append(jnp.sum(jnp.where(eye(), wide, 0.0), axis=0, keepdims=True))
    return parts[0] if len(parts) == 1 else jnp.concatenate(parts, axis=1)


def pick_lanes(col, first, count):
    return (col == iota((col.shape[0], count), 1) + first).astype(BF)


def pick_rows(row, first, count):
    return (row == iota((count, row.shape[1]), 0) + first).astype(BF)


OFFSETS = (
    (1, 2), (3, 2), (2, 1), (2, 3), (1, 1), (3, 3), (1, 3), (3, 1),
    (2, 2), (2, 0), (0, 2), (0, 0), (0, 1), (0, 3), (1, 0), (3, 0),
)


def main_kernel(
    n_dp, n_item,
    neg_s_ref, q_ref, table_hbm, state_ref, owner_ref, row_ref, neg_ref,
    grad_ref, loss_ref, table_out, state_out,
    table_ref, neg_f, tsend, qt, req_out, req_in, negbuf, nidbuf, found, returned, outbox, inbox, acc, pos_f, ut, tot, et, part, sib_in, red_in, red_out, y_in,
    dense_f, rs_out, relay_in, rs_in, ag,
    req_s, req_r, neg_s, neg_r, nid_s, nid_r, pc_s, pc_r, pi_s, pi_r, sn_s, sn_r, si_s, si_r, pos_s, pos_r, g_s, g_r, sib_s, sib_r, red_s, red_r, y_s, y_r,
    rs_s, relay_r, rs_r, ag_s, ag_r, load_s, store_s,
):
    ex, width = q_ref.shape
    rows = table_ref.shape[0]
    quarter = rows // n_dp
    hq = quarter // 2
    chips = n_item // 2
    cap = 3 * ex // n_item
    neg = negbuf.shape[2]
    y, me = lax.axis_index("dp"), lax.axis_index("item")
    chip, core = me // 2, lax.rem(me, 2)
    sibling = chip * 2 + 1 - core
    up, far, down = lax.rem(y + 1, n_dp), lax.rem(y + 2, n_dp), lax.rem(y + 3, n_dp)

    def copy(src, dst, send, recv, **where):
        return pltpu.make_async_remote_copy(
            src_ref=src, dst_ref=dst, send_sem=send, recv_sem=recv, device_id=where, device_id_type=pl.DeviceIdType.MESH
        )

    def load(k):
        at = pl.ds(pl.multiple_of(k * hq, hq), hq)
        return pltpu.make_async_copy(table_hbm.at[at, :], table_ref.at[at, :], load_s.at[k])

    def store(k):
        at = pl.ds(pl.multiple_of(k * hq, hq), hq)
        return pltpu.make_async_copy(table_ref.at[at, :], table_out.at[at, :], store_s.at[k])

    @pl.loop(0, 2 * n_dp)
    def _(k):
        load(k).start()

    barrier = pltpu.get_barrier_semaphore()

    @pl.loop(1, n_item)
    def _(off):
        pl.semaphore_signal(barrier, inc=1, device_id={"item": lax.rem(me + off, n_item)}, device_id_type=pl.DeviceIdType.MESH)

    @pl.loop(1, n_dp)
    def _(off):
        pl.semaphore_signal(barrier, inc=1, device_id={"dp": lax.rem(y + off, n_dp)}, device_id_type=pl.DeviceIdType.MESH)

    owner_r = owner_ref[...].astype(F32)
    row_r = row_ref[...].astype(F32)
    gid_r = owner_r * rows + row_r
    owners_r = (owner_r == iota((n_item, ex), 0)).astype(F32)
    before = (iota((LANES, LANES), 0) < iota((LANES, LANES), 1)).astype(BF)
    seen = jnp.zeros((n_item, 1), F32)
    slots = []
    for k in range(ex // LANES):
        named = owners_r[:, k * LANES : (k + 1) * LANES]
        earlier = dot(named.astype(BF), before) + seen
        slots.append(jnp.sum(earlier * named, axis=0, keepdims=True))
        seen += jnp.sum(named, axis=1, keepdims=True)
    slot_r = jnp.concatenate(slots, axis=1)
    place_r = owner_r * cap + slot_r
    high_r = jnp.floor(row_r * (1.0 / 64.0))
    low_r = row_r - 64.0 * high_r
    at_slot = slot_r == iota((LANES, ex), 0)
    both = jnp.concatenate([jnp.where(at_slot, high_r, 0.0), jnp.where(at_slot, low_r, 0.0)], axis=0).astype(BF)
    asked2 = lax.dot_general(owners_r.astype(BF), both, (((1,), (1,)), ((), ())), preferred_element_type=F32)
    asked = asked2[:, :LANES] * 64.0 + asked2[:, LANES:]
    for s in range(n_item):
        req_out[s] = asked[s : s + 1, :]

    pl.semaphore_wait(barrier, n_item - 1 + n_dp - 1)

    req_in[me] = req_out[me]

    def req_copy(peer):
        return copy(req_out.at[peer], req_in.at[me], req_s.at[peer], req_r.at[me], item=peer)

    @pl.loop(1, n_item)
    def _(off):
        req_copy(lax.rem(me + off, n_item)).start()

    @pl.loop(0, 2 * n_dp)
    def _(k):
        load(k).wait()

    for k in range(neg):
        neg_f[k : k + 1, :] = table_ref[pl.ds(neg_s_ref[k], 1), :]
    t = neg_f[...]
    mine = y * 2 + core
    negbuf[mine, chip] = (t / jnp.sqrt(jnp.sum(t * t, axis=1, keepdims=True) + EPSILON)).astype(BF)
    nidbuf[mine, chip] = jnp.concatenate([neg_ref[...].astype(F32), jnp.full((1, LANES - neg), -1.0, F32)], axis=1)

    def plane_copies(peer_chip):
        to = peer_chip * 2 + core
        return (
            copy(negbuf.at[mine, chip], negbuf.at[mine, chip], neg_s.at[peer_chip], neg_r.at[chip], item=to),
            copy(nidbuf.at[mine, chip], nidbuf.at[mine, chip], nid_s.at[peer_chip], nid_r.at[chip], item=to),
        )

    @pl.loop(1, chips)
    def _(off):
        for c in plane_copies(lax.rem(chip + off, chips)):
            c.start()

    tile = min(512, rows)

    @pl.loop(0, rows // tile)
    def _(k):
        at = pl.ds(pl.multiple_of(k * tile, tile), tile)
        t = table_ref[at, :]
        tsend[at, :] = (t / jnp.sqrt(jnp.sum(t * t, axis=1, keepdims=True) + EPSILON)).astype(BF)

    q = q_ref[...].astype(F32)
    q_norm = jnp.sqrt(jnp.sum(q * q, axis=1, keepdims=True) + EPSILON)
    acc[...] = q / q_norm
    qt[...] = jnp.transpose(acc[...]).astype(BF)

    def wait_recv(dst, send, recv, **where):
        copy(dst, dst, send, recv, **where).wait_recv()

    @pl.loop(1, n_item)
    def _(off):
        src = lax.rem(me + off, n_item)
        wait_recv(req_in.at[src], req_s.at[src], req_r.at[src], item=src)

    if chips == len(OFFSETS):
        order = [lax.rem(chip // 4 + dz, 4) * 4 + lax.rem(chip + dx, 4) for dz, dx in OFFSETS]
    else:
        order = [lax.rem(chip + d, chips) for d in range(1, chips + 1)]
    mates = [2 * c + side for c in order for side in range(2)]
    batch = min(8, n_item)
    batches = [mates[k : k + batch] for k in range(0, n_item, batch)]

    def pos_copy(peer):
        return copy(found.at[peer], returned.at[me], pos_s.at[peer], pos_r.at[me], item=peer)

    def gather(group):
        ids = jnp.concatenate([row_to_col(req_in[src])[:cap] for src in group], axis=0)
        got = jnp.zeros((batch * cap, width), F32)
        for t in range(rows // tile):
            got += dot(pick_lanes(ids, float(t * tile), tile), tsend[t * tile : (t + 1) * tile, :])
        for s, src in enumerate(group):
            found[src] = got[s * cap : (s + 1) * cap].astype(BF)

            @pl.when(src != me)
            def _():
                pos_copy(src).start()

    gather(batches[0])

    @pl.loop(1, chips)
    def _(off):
        src = lax.rem(chip + off, chips)
        wait_recv(negbuf.at[mine, src], neg_s.at[src], neg_r.at[src], item=src * 2 + core)
        wait_recv(nidbuf.at[mine, src], nid_s.at[src], nid_r.at[src], item=src * 2 + core)

    half = chips // 2

    def piece_part(d, h):
        return negbuf.at[d * 2 + core, pl.ds(h * half, half)], nidbuf.at[d * 2 + core, pl.ds(h * half, half)]

    def y_copies(d, h, way, dest):
        rows_part, ids_part = piece_part(d, h)
        return (
            copy(rows_part, rows_part, pc_s.at[way, h], pc_r.at[d, h], dp=dest),
            copy(ids_part, ids_part, pi_s.at[way, h], pi_r.at[d, h], dp=dest),
        )

    def y_wait(d, h, dest):
        for c in y_copies(d, h, 0, dest):
            c.wait_recv()

    def sib_copies(d, side):
        piece = d * 2 + side
        return (
            copy(negbuf.at[piece], negbuf.at[piece], sn_s.at[d], sn_r.at[d], item=sibling),
            copy(nidbuf.at[piece], nidbuf.at[piece], si_s.at[d], si_r.at[d], item=sibling),
        )

    def to_sibling(d):
        for c in sib_copies(d, core):
            c.start()

    def from_sibling(d):
        for c in sib_copies(d, 1 - core):
            c.wait_recv()

    def send_y(d, h, way, dest):
        for c in y_copies(d, h, way, dest):
            c.start()

    send_y(y, 0, 0, up)
    send_y(y, 1, 1, down)
    send_y(y, 1, 0, up)
    send_y(y, 0, 1, down)
    to_sibling(y)

    for group in batches[1:]:
        gather(group)

    returned[me] = found[me]

    tot[...] = jnp.zeros_like(tot)

    def pass1(piece):
        @pl.loop(0, chips // half)
        def _(h):
            first = h * half
            block = negbuf[piece, pl.ds(first, half)].reshape(half * neg, width)
            ids = jnp.concatenate(
                [
                    row_to_col(nidbuf[piece, first + z])[:neg]
                    + (((first + z) * 2 + lax.rem(piece, 2)) * rows).astype(F32)
                    for z in range(half)
                ],
                axis=0,
            )
            e = jnp.where(ids != gid_r, jnp.exp2(dot(block, qt[...]) * (INV_TEMP * LOG2E)), 0.0)
            tot[...] += jnp.sum(e.reshape(half * neg // 8, 8, ex), axis=0)
            eb = e.astype(BF)
            et[piece, pl.ds(first, half)] = eb.reshape(half, neg, ex)

    from_sibling(y)

    @pl.loop(0, 2)
    def _(side):
        pass1(y * 2 + side)

    y_wait(down, 0, down)
    send_y(down, 0, 2, up)
    y_wait(up, 1, up)
    send_y(up, 1, 2, down)
    y_wait(down, 1, down)
    to_sibling(down)
    y_wait(up, 0, up)
    to_sibling(up)

    @pl.loop(0, 2)
    def _(k):
        pass1(lax.rem(y + 1 + 2 * k, n_dp) * 2 + core)

    from_sibling(down)
    from_sibling(up)

    @pl.loop(0, 2)
    def _(k):
        pass1(lax.rem(y + 1 + 2 * k, n_dp) * 2 + 1 - core)

    y_wait(far, 0, down)
    y_wait(far, 1, up)
    to_sibling(far)
    pass1(far * 2 + core)
    from_sibling(far)
    pass1(far * 2 + 1 - core)

    @pl.loop(1, n_item)
    def _(off):
        src = lax.rem(me + off, n_item)
        wait_recv(returned.at[src], pos_s.at[src], pos_r.at[src], item=src)

    q_hat = acc[...]
    place_c = row_to_col(place_r)
    pos_e = jnp.zeros((ex, width), F32)
    for k in range(0, n_item, batch):
        pick = pick_lanes(place_c, float(k * cap), batch * cap)
        pos_e += dot(pick, returned[k : k + batch].reshape(batch * cap, width))
    pos_f[...] = pos_e
    s_pos = INV_TEMP * jnp.sum(q_hat.astype(BF).astype(F32) * pos_e, axis=1, keepdims=True)
    neg_tot = row_to_col(jnp.sum(tot[...], axis=0, keepdims=True))
    lse = jnp.log(jnp.exp(s_pos) + neg_tot)
    loss_ref[...] = col_to_row(lse - s_pos)
    coef = jnp.exp(s_pos - lse) - 1.0
    inv_tot = jnp.exp(-lse)

    g_pos = (INV_TEMP * coef * q_hat).astype(BF)

    def g_copy(peer):
        return copy(outbox.at[peer], inbox.at[me], g_s.at[peer], g_r.at[me], item=peer)

    for group in batches:
        wanted = jnp.concatenate([iota((cap, 1), 0) + (src * cap).astype(F32) for src in group], axis=0)
        rows_out = dot((place_r == wanted).astype(BF), g_pos)
        for s, src in enumerate(group):
            outbox[src] = rows_out[s * cap : (s + 1) * cap].astype(BF)

            @pl.when(src != me)
            def _():
                g_copy(src).start()

    inbox[me] = outbox[me]

    q_scaled = (q_hat.astype(BF).astype(F32) * (INV_TEMP * inv_tot)).astype(BF)

    def pass2(side):
        @pl.loop(0, n_dp)
        def _(d):
            for h in range(chips // half):
                at = slice(h * half, (h + 1) * half)
                p = dot(et[d * 2 + side, at].reshape(half * neg, ex), q_scaled)
                p = p.astype(BF).reshape(half, neg, width)
                for z in range(half):
                    part[side, h * half + z, pl.ds(pl.multiple_of(d * neg, neg), neg), :] = p[z]

    pass2(1 - core)
    to_sib = copy(part.at[1 - core], sib_in, sib_s, sib_r, item=sibling)
    to_sib.start()
    pass2(core)

    to_sib.wait_recv()

    @pl.loop(0, chips)
    def _(z):
        red_out[z] = (part[core, z].astype(F32) + sib_in[z].astype(F32)).astype(BF)

    def red_copy(peer_chip):
        return copy(red_out.at[peer_chip], red_in.at[chip], red_s.at[peer_chip], red_r.at[chip], item=peer_chip * 2 + core)

    for k, group in enumerate(batches):
        for src in group:

            @pl.when(src != me)
            def _():
                wait_recv(inbox.at[src], g_s.at[src], g_r.at[src], item=src)

        if k == len(batches) - 1:
            @pl.loop(1, chips)
            def _(off):
                red_copy(lax.rem(chip + off, chips)).start()

        ids = jnp.concatenate([req_in[src][:, :cap] for src in group], axis=1)
        came = jnp.concatenate([inbox[src] for src in group], axis=0)

        @pl.loop(0, n_dp)
        def _(d):
            at = pl.ds(pl.multiple_of(d * quarter, quarter), quarter)
            new = dot(pick_rows(ids, (d * quarter).astype(F32), quarter), came)
            if k == 0:
                dense_f[at, :] = new
            else:
                dense_f[at, :] += new

    def rs_copies():
        return (
            copy(rs_out.at[0, 0], relay_in.at[0], rs_s.at[0, 0], relay_r.at[0], dp=up),
            copy(rs_out.at[0, 1], relay_in.at[1], rs_s.at[0, 1], relay_r.at[1], dp=down),
            copy(rs_out.at[1, 0], rs_in.at[0, 0], rs_s.at[1, 0], rs_r.at[0, 0], dp=up),
            copy(rs_out.at[1, 1], rs_in.at[0, 1], rs_s.at[1, 1], rs_r.at[0, 1], dp=up),
            copy(rs_out.at[2, 0], rs_in.at[1, 0], rs_s.at[2, 0], rs_r.at[1, 0], dp=down),
            copy(rs_out.at[2, 1], rs_in.at[1, 1], rs_s.at[2, 1], rs_r.at[1, 1], dp=down),
        )

    def dense_part(d, h):
        return dense_f[pl.ds(pl.multiple_of(d * quarter + h * hq, hq), hq), :]

    far0, far1, up0, up1, down0, down1 = rs_copies()
    rs_out[0, 0] = dense_part(far, 0).astype(BF)
    far0.start()
    rs_out[0, 1] = dense_part(far, 1).astype(BF)
    far1.start()
    rs_out[1, 1] = dense_part(up, 1).astype(BF)
    up1.start()
    rs_out[2, 0] = dense_part(down, 0).astype(BF)
    down0.start()
    far0.wait_recv()
    rs_out[1, 0] = (dense_part(up, 0) + relay_in[0].astype(F32)).astype(BF)
    up0.start()
    far1.wait_recv()
    rs_out[2, 1] = (dense_part(down, 1) + relay_in[1].astype(F32)).astype(BF)
    down1.start()

    ut[...] = jnp.zeros_like(ut)

    @pl.loop(0, 2 * n_dp)
    def _(piece):
        block = negbuf[piece].reshape(chips * neg, width)
        eb = et[piece].reshape(chips * neg, ex)
        ut[...] += lax.dot_general(block, eb, (((0,), (0,)), ((), ())), preferred_element_type=F32)

    g_q = INV_TEMP * (coef * pos_f[...] + jnp.transpose(ut[...]) * inv_tot)
    grad_ref[...] = ((g_q - acc[...] * jnp.sum(acc[...] * g_q, axis=1, keepdims=True)) / q_norm).astype(BF)

    up1.wait_recv()
    up0.wait_recv()
    down0.wait_recv()
    down1.wait_recv()
    for h in range(2):
        ag[y, h] = (dense_part(y, h) + rs_in[0, h].astype(F32) + rs_in[1, h].astype(F32)).astype(BF)

    def ag_copy(slot, h, way, dest):
        return copy(ag.at[slot, h], ag.at[slot, h], ag_s.at[way, h], ag_r.at[slot, h], dp=dest)

    for h in range(2):
        ag_copy(y, h, 0, up).start()
        ag_copy(y, h, 1, down).start()
    total = red_out[chip].astype(F32)

    def add_red(off, total):
        src = lax.rem(chip + off, chips)
        wait_recv(red_in.at[src], red_s.at[src], red_r.at[src], item=src * 2 + core)
        return total + red_in[src].astype(F32)

    total = lax.fori_loop(1, chips, add_red, total)
    y_in[y] = total.astype(BF)

    def sum_copy(dest):
        return copy(y_in.at[y], y_in.at[y], y_s.at[dest], y_r.at[y], dp=dest)

    @pl.loop(1, n_dp)
    def _(off):
        sum_copy(lax.rem(y + off, n_dp)).start()

    @pl.loop(1, n_dp)
    def _(off):
        src = lax.rem(y + off, n_dp)
        wait_recv(y_in.at[src], y_s.at[src], y_r.at[src], dp=src)

    sums = y_in[0].astype(F32)
    for d in range(1, n_dp):
        sums += y_in[d].astype(F32)
    sums_high = sums.astype(BF)
    sums_low = (sums - sums_high.astype(F32)).astype(BF)
    neg_ids = jnp.concatenate([nidbuf[d * 2 + core, chip][:, :neg] for d in range(n_dp)], axis=1)

    def step(d, h):
        first = d * quarter + h * hq
        at = pl.ds(pl.multiple_of(first, hq), hq)
        pick = (neg_ids == iota((hq, n_dp * neg), 0) + first.astype(F32)).astype(BF)
        g = ag[d, h].astype(F32) + dot(pick, sums_high) + dot(pick, sums_low)
        t = table_ref[at, :]
        norm = jnp.sqrt(jnp.sum(t * t, axis=1, keepdims=True) + EPSILON)
        unit = t / norm
        g_row = (g - unit * jnp.sum(unit * g, axis=1, keepdims=True)) / norm
        mean = jnp.sum(g_row * g_row, axis=1, keepdims=True) * (1.0 / width)
        new = state_ref[:, at] + col_to_row(mean)
        state_out[:, at] = new
        table_ref[at, :] = t - LEARN_RATE * g_row / jnp.sqrt(row_to_col(new))
        store(d * 2 + h).start()

    def step_both(d):
        @pl.loop(0, 2)
        def _(h):
            step(d, h)

    step_both(y)

    wait_recv(ag.at[down, 0], ag_s.at[0, 0], ag_r.at[down, 0], dp=down)
    ag_copy(down, 0, 2, up).start()
    wait_recv(ag.at[up, 1], ag_s.at[0, 1], ag_r.at[up, 1], dp=up)
    ag_copy(up, 1, 2, down).start()

    wait_recv(ag.at[down, 1], ag_s.at[0, 1], ag_r.at[down, 1], dp=down)
    wait_recv(ag.at[up, 0], ag_s.at[0, 0], ag_r.at[up, 0], dp=up)

    @pl.loop(0, 2)
    def _(k):
        step_both(lax.rem(y + 1 + 2 * k, n_dp))

    wait_recv(ag.at[far, 0], ag_s.at[0, 0], ag_r.at[far, 0], dp=down)
    wait_recv(ag.at[far, 1], ag_s.at[0, 1], ag_r.at[far, 1], dp=up)
    step_both(far)

    @pl.loop(1, n_item)
    def _(off):
        peer = lax.rem(me + off, n_item)
        req_copy(peer).wait_send()
        pos_copy(peer).wait_send()
        g_copy(peer).wait_send()

    @pl.loop(1, chips)
    def _(off):
        peer = lax.rem(chip + off, chips)
        for c in plane_copies(peer):
            c.wait_send()
        red_copy(peer).wait_send()

    @pl.loop(1, n_dp)
    def _(off):
        sum_copy(lax.rem(y + off, n_dp)).wait_send()

    @pl.loop(0, n_dp)
    def _(d):
        for c in sib_copies(d, core):
            c.wait_send()

    for h in range(2):
        for c in (*y_copies(y, h, 0, up), *y_copies(y, h, 1, down)):
            c.wait_send()
    for c in (*y_copies(down, 0, 2, up), *y_copies(up, 1, 2, down)):
        c.wait_send()

    to_sib.wait_send()
    for c in rs_copies():
        c.wait_send()
    for h in range(2):
        ag_copy(y, h, 0, up).wait_send()
        ag_copy(y, h, 1, down).wait_send()
    ag_copy(down, 0, 2, up).wait_send()
    ag_copy(up, 1, 2, down).wait_send()

    @pl.loop(0, 2 * n_dp)
    def _(k):
        store(k).wait()


def on_device(n_dp, n_item, queries, item_table, adagrad_state, pos_owner, pos_row, neg_rows):
    ex, width = queries.shape
    rows = item_table.shape[0]
    neg = neg_rows.shape[0]
    chips = n_item // 2
    cap = 3 * ex // n_item
    quarter = rows // n_dp
    vmem, hbm = pl.BlockSpec(memory_space=pltpu.VMEM), pl.BlockSpec(memory_space=pl.ANY)
    dma = pltpu.SemaphoreType.DMA
    n_neg = 2 * n_dp * chips * neg
    flops = 2 * width * (3 * n_neg * ex + 3 * n_item * cap * (rows + ex))
    grad, loss, new_table, new_state = pl.pallas_call(
        functools.partial(main_kernel, n_dp, n_item),
        out_shape=(
            jax.ShapeDtypeStruct((ex, width), BF),
            jax.ShapeDtypeStruct((1, ex), F32),
            jax.ShapeDtypeStruct((rows, width), F32),
            jax.ShapeDtypeStruct((1, rows), F32),
        ),
        in_specs=[pl.BlockSpec(memory_space=pltpu.SMEM), vmem, hbm, vmem, vmem, vmem, vmem],
        out_specs=(vmem, vmem, hbm, vmem),
        scratch_shapes=[
            pltpu.VMEM((rows, width), F32),
            pltpu.VMEM((neg, width), F32),
            pltpu.VMEM((rows, width), BF),
            pltpu.VMEM((width, ex), BF),
            pltpu.VMEM((n_item, 1, LANES), F32),
            pltpu.VMEM((n_item, 1, LANES), F32),
            pltpu.VMEM((2 * n_dp, chips, neg, width), BF),
            pltpu.VMEM((2 * n_dp, chips, 1, LANES), F32),
            pltpu.VMEM((n_item, cap, width), BF),
            pltpu.VMEM((n_item, cap, width), BF),
            pltpu.VMEM((n_item, cap, width), BF),
            pltpu.VMEM((n_item, cap, width), BF),
            pltpu.VMEM((ex, width), F32),
            pltpu.VMEM((ex, width), F32),
            pltpu.VMEM((width, ex), F32),
            pltpu.VMEM((8, ex), F32),
            pltpu.VMEM((2 * n_dp, chips, neg, ex), BF),
            pltpu.VMEM((2, chips, n_dp * neg, width), BF),
            pltpu.VMEM((chips, n_dp * neg, width), BF),
            pltpu.VMEM((chips, n_dp * neg, width), BF),
            pltpu.VMEM((chips, n_dp * neg, width), BF),
            pltpu.VMEM((n_dp, n_dp * neg, width), BF),
            pltpu.VMEM((rows, width), F32),
            pltpu.VMEM((3, 2, quarter // 2, width), BF),
            pltpu.VMEM((2, quarter // 2, width), BF),
            pltpu.VMEM((2, 2, quarter // 2, width), BF),
            pltpu.VMEM((n_dp, 2, quarter // 2, width), BF),
            dma((n_item,)), dma((n_item,)),
            dma((chips,)), dma((chips,)),
            dma((chips,)), dma((chips,)),
            dma((3, 2)), dma((n_dp, 2)),
            dma((3, 2)), dma((n_dp, 2)),
            dma((n_dp,)), dma((n_dp,)),
            dma((n_dp,)), dma((n_dp,)),
            dma((n_item,)), dma((n_item,)),
            dma((n_item,)), dma((n_item,)),
            dma, dma,
            dma((chips,)), dma((chips,)),
            dma((n_dp,)), dma((n_dp,)),
            dma((3, 2)), dma((2,)), dma((2, 2)),
            dma((3, 2)), dma((n_dp, 2)),
            dma((2 * n_dp,)), dma((2 * n_dp,)),
        ],
        compiler_params=pltpu.CompilerParams(collective_id=0, has_side_effects=True, vmem_limit_bytes=62 * 2**20),
        cost_estimate=pl.CostEstimate(flops=flops, bytes_accessed=12 * 2**20, transcendentals=n_neg * ex),
        name="training_step",
    )(
        neg_rows, queries, item_table, adagrad_state.reshape(1, rows), pos_owner.reshape(1, ex), pos_row.reshape(1, ex),
        neg_rows.reshape(1, neg),
    )
    return grad, loss.reshape(ex), new_table, new_state.reshape(rows)


def solution(mesh):
    both = ("dp", "item")
    return jax.shard_map(
        functools.partial(on_device, mesh.shape["dp"], mesh.shape["item"]),
        mesh=mesh,
        in_specs=(P(both, None), P("item", None), P("item"), P(both, None), P(both), P(both)),
        out_specs=(P(both, None), P(both), P("item", None), P("item")),
        check_vma=False,
    )
```

```python
import functools

import jax
import jax.numpy as jnp
from jax import lax
from jax.experimental import pallas as pl
from jax.experimental.pallas import tpu as pltpu
from jax.sharding import PartitionSpec as P

INV_TEMP = 20.0
LEARN_RATE = 0.05
EPSILON = 1e-06
LOG2E = 1.4426950408889634
BF, F32 = jnp.bfloat16, jnp.float32
LANES = 128


def dot(a, b):
    return jnp.dot(a, b, preferred_element_type=F32)


def iota(shape, dim):
    return lax.broadcasted_iota(jnp.int32, shape, dim).astype(F32)


def eye():
    return lax.broadcasted_iota(jnp.int32, (LANES, LANES), 0) == lax.broadcasted_iota(jnp.int32, (LANES, LANES), 1)


def row_to_col(row):
    parts = []
    for k in range(row.shape[1] // LANES):
        wide = jnp.broadcast_to(row[:, k * LANES : (k + 1) * LANES], (LANES, LANES))
        parts.append(jnp.sum(jnp.where(eye(), wide, 0.0), axis=1, keepdims=True))
    return parts[0] if len(parts) == 1 else jnp.concatenate(parts, axis=0)


def col_to_row(col):
    parts = []
    for k in range(col.shape[0] // LANES):
        wide = jnp.broadcast_to(col[k * LANES : (k + 1) * LANES], (LANES, LANES))
        parts.append(jnp.sum(jnp.where(eye(), wide, 0.0), axis=0, keepdims=True))
    return parts[0] if len(parts) == 1 else jnp.concatenate(parts, axis=1)


def pick_lanes(col, first, count):
    return (col == iota((col.shape[0], count), 1) + first).astype(BF)


def pick_rows(row, first, count):
    return (row == iota((count, row.shape[1]), 0) + first).astype(BF)


OFFSETS = (
    (1, 2), (3, 2), (2, 1), (2, 3), (1, 1), (3, 3), (1, 3), (3, 1),
    (2, 2), (2, 0), (0, 2), (0, 0), (0, 1), (0, 3), (1, 0), (3, 0),
)


def main_kernel(
    n_dp, n_item,
    neg_s_ref, q_ref, table_hbm, state_ref, owner_ref, row_ref, neg_ref,
    grad_ref, loss_ref, table_ref, state_out,
    neg_f, tsend, qt, req_out, req_in, negbuf, nidbuf, found, returned, outbox, inbox, acc, pos_f, g_bf, ut, tot, et, part, sib_in, red_in, red_out, y_in,
    dense_f, rs_out, relay_in, rs_in, ag,
    req_s, req_r, neg_s, neg_r, nid_s, nid_r, pc_s, pc_r, pi_s, pi_r, sn_s, sn_r, si_s, si_r, pos_s, pos_r, g_s, g_r, sib_s, sib_r, red_s, red_r, y_s, y_r,
    rs_s, relay_r, rs_r, ag_s, ag_r, load_s,
):
    ex, width = q_ref.shape
    rows = table_ref.shape[0]
    quarter = rows // n_dp
    hq = quarter // 2
    chips = n_item // 2
    cap = 3 * ex // n_item
    neg = negbuf.shape[2]
    y, me = lax.axis_index("dp"), lax.axis_index("item")
    chip, core = me // 2, lax.rem(me, 2)
    sibling = chip * 2 + 1 - core
    up, far, down = lax.rem(y + 1, n_dp), lax.rem(y + 2, n_dp), lax.rem(y + 3, n_dp)

    def copy(src, dst, send, recv, **where):
        return pltpu.make_async_remote_copy(
            src_ref=src, dst_ref=dst, send_sem=send, recv_sem=recv, device_id=where, device_id_type=pl.DeviceIdType.MESH
        )

    def load(k):
        at = pl.ds(pl.multiple_of(k * hq, hq), hq)
        return pltpu.make_async_copy(table_hbm.at[at, :], table_ref.at[at, :], load_s.at[k])

    @pl.loop(0, 2 * n_dp)
    def _(k):
        load(k).start()

    barrier = pltpu.get_barrier_semaphore()

    @pl.loop(1, n_item)
    def _(off):
        pl.semaphore_signal(barrier, inc=1, device_id={"item": lax.rem(me + off, n_item)}, device_id_type=pl.DeviceIdType.MESH)

    @pl.loop(1, n_dp)
    def _(off):
        pl.semaphore_signal(barrier, inc=1, device_id={"dp": lax.rem(y + off, n_dp)}, device_id_type=pl.DeviceIdType.MESH)

    owner_r = owner_ref[...].astype(F32)
    row_r = row_ref[...].astype(F32)
    gid_r = owner_r * rows + row_r
    owners_r = (owner_r == iota((n_item, ex), 0)).astype(F32)
    before = (iota((LANES, LANES), 0) < iota((LANES, LANES), 1)).astype(BF)
    seen = jnp.zeros((n_item, 1), F32)
    slots = []
    for k in range(ex // LANES):
        named = owners_r[:, k * LANES : (k + 1) * LANES]
        earlier = dot(named.astype(BF), before) + seen
        slots.append(jnp.sum(earlier * named, axis=0, keepdims=True))
        seen += jnp.sum(named, axis=1, keepdims=True)
    slot_r = jnp.concatenate(slots, axis=1)
    place_r = owner_r * cap + slot_r
    high_r = jnp.floor(row_r * (1.0 / 64.0))
    low_r = row_r - 64.0 * high_r
    at_slot = slot_r == iota((LANES, ex), 0)
    both = jnp.concatenate([jnp.where(at_slot, high_r, 0.0), jnp.where(at_slot, low_r, 0.0)], axis=0).astype(BF)
    asked2 = lax.dot_general(owners_r.astype(BF), both, (((1,), (1,)), ((), ())), preferred_element_type=F32)
    asked = asked2[:, :LANES] * 64.0 + asked2[:, LANES:]
    for s in range(n_item):
        req_out[s] = asked[s : s + 1, :]

    pl.semaphore_wait(barrier, n_item - 1 + n_dp - 1)

    req_in[me] = req_out[me]

    def req_copy(peer):
        return copy(req_out.at[peer], req_in.at[me], req_s.at[peer], req_r.at[me], item=peer)

    @pl.loop(1, n_item)
    def _(off):
        req_copy(lax.rem(me + off, n_item)).start()

    @pl.loop(0, 2 * n_dp)
    def _(k):
        load(k).wait()

    for k in range(neg):
        neg_f[k : k + 1, :] = table_ref[pl.ds(neg_s_ref[k], 1), :]
    t = neg_f[...]
    mine = y * 2 + core
    negbuf[mine, chip] = (t / jnp.sqrt(jnp.sum(t * t, axis=1, keepdims=True) + EPSILON)).astype(BF)
    nidbuf[mine, chip] = jnp.concatenate([neg_ref[...].astype(F32), jnp.full((1, LANES - neg), -1.0, F32)], axis=1)

    def plane_copies(peer_chip):
        to = peer_chip * 2 + core
        return (
            copy(negbuf.at[mine, chip], negbuf.at[mine, chip], neg_s.at[peer_chip], neg_r.at[chip], item=to),
            copy(nidbuf.at[mine, chip], nidbuf.at[mine, chip], nid_s.at[peer_chip], nid_r.at[chip], item=to),
        )

    @pl.loop(1, chips)
    def _(off):
        for c in plane_copies(lax.rem(chip + off, chips)):
            c.start()

    tile = min(512, rows)

    @pl.loop(0, rows // tile)
    def _(k):
        at = pl.ds(pl.multiple_of(k * tile, tile), tile)
        t = table_ref[at, :]
        tsend[at, :] = (t / jnp.sqrt(jnp.sum(t * t, axis=1, keepdims=True) + EPSILON)).astype(BF)

    q = q_ref[...].astype(F32)
    q_norm = jnp.sqrt(jnp.sum(q * q, axis=1, keepdims=True) + EPSILON)
    acc[...] = q / q_norm
    qt[...] = jnp.transpose(acc[...]).astype(BF)

    def wait_recv(dst, send, recv, **where):
        copy(dst, dst, send, recv, **where).wait_recv()

    @pl.loop(1, n_item)
    def _(off):
        src = lax.rem(me + off, n_item)
        wait_recv(req_in.at[src], req_s.at[src], req_r.at[src], item=src)

    if chips == len(OFFSETS):
        order = [lax.rem(chip // 4 + dz, 4) * 4 + lax.rem(chip + dx, 4) for dz, dx in OFFSETS]
    else:
        order = [lax.rem(chip + d, chips) for d in range(1, chips + 1)]
    mates = [2 * c + side for c in order for side in range(2)]
    batch = min(8, n_item)
    batches = [mates[k : k + batch] for k in range(0, n_item, batch)]

    def pos_copy(peer):
        return copy(found.at[peer], returned.at[me], pos_s.at[peer], pos_r.at[me], item=peer)

    def gather(group):
        ids = jnp.concatenate([row_to_col(req_in[src])[:cap] for src in group], axis=0)
        got = jnp.zeros((batch * cap, width), F32)
        for t in range(rows // tile):
            got += dot(pick_lanes(ids, float(t * tile), tile), tsend[t * tile : (t + 1) * tile, :])
        for s, src in enumerate(group):
            found[src] = got[s * cap : (s + 1) * cap].astype(BF)

            @pl.when(src != me)
            def _():
                pos_copy(src).start()

    def one_of(k):
        group = batches[-1]
        for n in range(len(batches) - 2, -1, -1):
            group = [jnp.where(k == n, a, b) for a, b in zip(batches[n], group)]
        return group

    @pl.loop(0, 1)
    def _(k):
        gather(one_of(k))


    @pl.loop(1, chips)
    def _(off):
        src = lax.rem(chip + off, chips)
        wait_recv(negbuf.at[mine, src], neg_s.at[src], neg_r.at[src], item=src * 2 + core)
        wait_recv(nidbuf.at[mine, src], nid_s.at[src], nid_r.at[src], item=src * 2 + core)

    half = chips // 2

    def piece_part(d, h):
        return negbuf.at[d * 2 + core, pl.ds(h * half, half)], nidbuf.at[d * 2 + core, pl.ds(h * half, half)]

    def y_copies(d, h, way, dest):
        rows_part, ids_part = piece_part(d, h)
        return (
            copy(rows_part, rows_part, pc_s.at[way, h], pc_r.at[d, h], dp=dest),
            copy(ids_part, ids_part, pi_s.at[way, h], pi_r.at[d, h], dp=dest),
        )

    def y_wait(d, h, dest):
        for c in y_copies(d, h, 0, dest):
            c.wait_recv()

    def sib_copies(d, side):
        piece = d * 2 + side
        return (
            copy(negbuf.at[piece], negbuf.at[piece], sn_s.at[d], sn_r.at[d], item=sibling),
            copy(nidbuf.at[piece], nidbuf.at[piece], si_s.at[d], si_r.at[d], item=sibling),
        )

    def to_sibling(d):
        for c in sib_copies(d, core):
            c.start()

    def from_sibling(d):
        for c in sib_copies(d, 1 - core):
            c.wait_recv()

    def send_y(d, h, way, dest):
        for c in y_copies(d, h, way, dest):
            c.start()

    send_y(y, 0, 0, up)
    send_y(y, 1, 1, down)
    send_y(y, 1, 0, up)
    send_y(y, 0, 1, down)
    to_sibling(y)

    @pl.loop(1, len(batches))
    def _(k):
        gather(one_of(k))

    returned[me] = found[me]

    tot[...] = jnp.zeros_like(tot)

    def pass1(piece):
        @pl.loop(0, chips // half)
        def _(h):
            first = h * half
            block = negbuf[piece, pl.ds(first, half)].reshape(half * neg, width)
            ids = jnp.concatenate(
                [
                    row_to_col(nidbuf[piece, first + z])[:neg]
                    + (((first + z) * 2 + lax.rem(piece, 2)) * rows).astype(F32)
                    for z in range(half)
                ],
                axis=0,
            )
            e = jnp.where(ids != gid_r, jnp.exp2(dot(block, qt[...]) * (INV_TEMP * LOG2E)), 0.0)
            tot[...] += jnp.sum(e.reshape(half * neg // 8, 8, ex), axis=0)
            eb = e.astype(BF)
            et[piece, pl.ds(first, half)] = eb.reshape(half, neg, ex)

    from_sibling(y)

    @pl.loop(0, 2)
    def _(side):
        pass1(y * 2 + side)

    y_wait(down, 0, down)
    send_y(down, 0, 2, up)
    y_wait(up, 1, up)
    send_y(up, 1, 2, down)
    y_wait(down, 1, down)
    to_sibling(down)
    y_wait(up, 0, up)
    to_sibling(up)

    @pl.loop(0, 2)
    def _(k):
        pass1(lax.rem(y + 1 + 2 * k, n_dp) * 2 + core)

    from_sibling(down)
    from_sibling(up)

    @pl.loop(0, 2)
    def _(k):
        pass1(lax.rem(y + 1 + 2 * k, n_dp) * 2 + 1 - core)

    y_wait(far, 0, down)
    y_wait(far, 1, up)
    to_sibling(far)
    pass1(far * 2 + core)
    from_sibling(far)
    pass1(far * 2 + 1 - core)

    place_c = row_to_col(place_r)
    pos_f[...] = jnp.zeros_like(pos_f)

    def slots_of(group):
        first = lax.broadcasted_iota(jnp.int32, (1, cap), 1)
        return jnp.concatenate([first + src * cap for src in group], axis=1).astype(F32)

    @pl.loop(0, len(batches))
    def _(k):
        group = one_of(k)
        for src in group:

            @pl.when(src != me)
            def _():
                wait_recv(returned.at[src], pos_s.at[src], pos_r.at[src], item=src)

        pick = (place_c == slots_of(group)).astype(BF)
        pos_f[...] += dot(pick, jnp.concatenate([returned[src] for src in group], axis=0))

    q_hat = acc[...]
    pos_e = pos_f[...]
    s_pos = INV_TEMP * jnp.sum(q_hat.astype(BF).astype(F32) * pos_e, axis=1, keepdims=True)
    neg_tot = row_to_col(jnp.sum(tot[...], axis=0, keepdims=True))
    lse = jnp.log(jnp.exp(s_pos) + neg_tot)
    loss_ref[...] = col_to_row(lse - s_pos)
    coef = jnp.exp(s_pos - lse) - 1.0
    inv_tot = jnp.exp(-lse)

    g_bf[...] = (INV_TEMP * coef * q_hat).astype(BF)

    def g_copy(peer):
        return copy(outbox.at[peer], inbox.at[me], g_s.at[peer], g_r.at[me], item=peer)

    @pl.loop(0, len(batches))
    def _(k):
        group = one_of(k)
        wanted = jnp.concatenate([iota((cap, 1), 0) + (src * cap).astype(F32) for src in group], axis=0)
        rows_out = dot((place_r == wanted).astype(BF), g_bf[...])
        for s, src in enumerate(group):
            outbox[src] = rows_out[s * cap : (s + 1) * cap].astype(BF)

            @pl.when(src != me)
            def _():
                g_copy(src).start()

    inbox[me] = outbox[me]

    q_scaled = (q_hat.astype(BF).astype(F32) * (INV_TEMP * inv_tot)).astype(BF)

    def pass2(side):
        @pl.loop(0, n_dp)
        def _(d):
            for h in range(chips // half):
                at = slice(h * half, (h + 1) * half)
                p = dot(et[d * 2 + side, at].reshape(half * neg, ex), q_scaled)
                p = p.astype(BF).reshape(half, neg, width)
                for z in range(half):
                    part[side, h * half + z, pl.ds(pl.multiple_of(d * neg, neg), neg), :] = p[z]

    pass2(1 - core)
    to_sib = copy(part.at[1 - core], sib_in, sib_s, sib_r, item=sibling)
    to_sib.start()
    pass2(core)

    to_sib.wait_recv()

    @pl.loop(0, chips)
    def _(z):
        red_out[z] = (part[core, z].astype(F32) + sib_in[z].astype(F32)).astype(BF)

    def red_copy(peer_chip):
        return copy(red_out.at[peer_chip], red_in.at[chip], red_s.at[peer_chip], red_r.at[chip], item=peer_chip * 2 + core)

    @pl.loop(1, chips)
    def _(off):
        red_copy(lax.rem(chip + off, chips)).start()

    for k, group in enumerate(batches):
        for src in group:

            @pl.when(src != me)
            def _():
                wait_recv(inbox.at[src], g_s.at[src], g_r.at[src], item=src)

        ids = jnp.concatenate([req_in[src][:, :cap] for src in group], axis=1)
        came = jnp.concatenate([inbox[src] for src in group], axis=0)

        @pl.loop(0, n_dp)
        def _(d):
            at = pl.ds(pl.multiple_of(d * quarter, quarter), quarter)
            new = dot(pick_rows(ids, (d * quarter).astype(F32), quarter), came)
            if k == 0:
                dense_f[at, :] = new
            else:
                dense_f[at, :] += new

    def rs_copies():
        return (
            copy(rs_out.at[0, 0], relay_in.at[0], rs_s.at[0, 0], relay_r.at[0], dp=up),
            copy(rs_out.at[0, 1], relay_in.at[1], rs_s.at[0, 1], relay_r.at[1], dp=down),
            copy(rs_out.at[1, 0], rs_in.at[0, 0], rs_s.at[1, 0], rs_r.at[0, 0], dp=up),
            copy(rs_out.at[1, 1], rs_in.at[0, 1], rs_s.at[1, 1], rs_r.at[0, 1], dp=up),
            copy(rs_out.at[2, 0], rs_in.at[1, 0], rs_s.at[2, 0], rs_r.at[1, 0], dp=down),
            copy(rs_out.at[2, 1], rs_in.at[1, 1], rs_s.at[2, 1], rs_r.at[1, 1], dp=down),
        )

    def dense_part(d, h):
        return dense_f[pl.ds(pl.multiple_of(d * quarter + h * hq, hq), hq), :]

    far0, far1, up0, up1, down0, down1 = rs_copies()
    rs_out[0, 0] = dense_part(far, 0).astype(BF)
    far0.start()
    rs_out[0, 1] = dense_part(far, 1).astype(BF)
    far1.start()
    rs_out[1, 1] = dense_part(up, 1).astype(BF)
    up1.start()
    rs_out[2, 0] = dense_part(down, 0).astype(BF)
    down0.start()
    far0.wait_recv()
    rs_out[1, 0] = (dense_part(up, 0) + relay_in[0].astype(F32)).astype(BF)
    up0.start()
    far1.wait_recv()
    rs_out[2, 1] = (dense_part(down, 1) + relay_in[1].astype(F32)).astype(BF)
    down1.start()

    ut[...] = jnp.zeros_like(ut)

    @pl.loop(0, 2 * n_dp)
    def _(piece):
        block = negbuf[piece].reshape(chips * neg, width)
        eb = et[piece].reshape(chips * neg, ex)
        ut[...] += lax.dot_general(block, eb, (((0,), (0,)), ((), ())), preferred_element_type=F32)

    g_q = INV_TEMP * (coef * pos_f[...] + jnp.transpose(ut[...]) * inv_tot)
    grad_ref[...] = ((g_q - acc[...] * jnp.sum(acc[...] * g_q, axis=1, keepdims=True)) / q_norm).astype(BF)

    @pl.loop(1, n_item)
    def _(off):
        peer = lax.rem(me + off, n_item)
        req_copy(peer).wait_send()
        pos_copy(peer).wait_send()
        g_copy(peer).wait_send()

    @pl.loop(1, chips)
    def _(off):
        peer = lax.rem(chip + off, chips)
        for c in plane_copies(peer):
            c.wait_send()
        red_copy(peer).wait_send()

    @pl.loop(0, n_dp)
    def _(d):
        for c in sib_copies(d, core):
            c.wait_send()

    for h in range(2):
        for c in (*y_copies(y, h, 0, up), *y_copies(y, h, 1, down)):
            c.wait_send()
    for c in (*y_copies(down, 0, 2, up), *y_copies(up, 1, 2, down)):
        c.wait_send()

    total = red_out[chip].astype(F32)

    def add_red(off, total):
        src = lax.rem(chip + off, chips)
        wait_recv(red_in.at[src], red_s.at[src], red_r.at[src], item=src * 2 + core)
        return total + red_in[src].astype(F32)

    total = lax.fori_loop(1, chips, add_red, total)
    y_in[y] = total.astype(BF)

    def sum_copy(dest):
        return copy(y_in.at[y], y_in.at[y], y_s.at[dest], y_r.at[y], dp=dest)

    @pl.loop(1, n_dp)
    def _(off):
        sum_copy(lax.rem(y + off, n_dp)).start()

    up1.wait_recv()
    up0.wait_recv()
    down0.wait_recv()
    down1.wait_recv()
    for h in range(2):
        ag[y, h] = (dense_part(y, h) + rs_in[0, h].astype(F32) + rs_in[1, h].astype(F32)).astype(BF)

    def ag_copy(slot, h, way, dest):
        return copy(ag.at[slot, h], ag.at[slot, h], ag_s.at[way, h], ag_r.at[slot, h], dp=dest)

    for h in range(2):
        ag_copy(y, h, 0, up).start()
        ag_copy(y, h, 1, down).start()
    @pl.loop(1, n_dp)
    def _(off):
        src = lax.rem(y + off, n_dp)
        wait_recv(y_in.at[src], y_s.at[src], y_r.at[src], dp=src)

    sums = y_in[0].astype(F32)
    for d in range(1, n_dp):
        sums += y_in[d].astype(F32)
    sums_high = sums.astype(BF)
    sums_low = (sums - sums_high.astype(F32)).astype(BF)
    neg_ids = jnp.concatenate([nidbuf[d * 2 + core, chip][:, :neg] for d in range(n_dp)], axis=1)

    def step(d, h):
        first = d * quarter + h * hq
        at = pl.ds(pl.multiple_of(first, hq), hq)
        pick = (neg_ids == iota((hq, n_dp * neg), 0) + first.astype(F32)).astype(BF)
        g = ag[d, h].astype(F32) + dot(pick, sums_high) + dot(pick, sums_low)
        t = table_ref[at, :]
        norm = jnp.sqrt(jnp.sum(t * t, axis=1, keepdims=True) + EPSILON)
        unit = t / norm
        g_row = (g - unit * jnp.sum(unit * g, axis=1, keepdims=True)) / norm
        mean = jnp.sum(g_row * g_row, axis=1, keepdims=True) * (1.0 / width)
        new = state_ref[:, at] + col_to_row(mean)
        state_out[:, at] = new
        table_ref[at, :] = t - LEARN_RATE * g_row / jnp.sqrt(row_to_col(new))

    def step_both(d):
        @pl.loop(0, 2)
        def _(h):
            step(d, h)

    step_both(y)

    wait_recv(ag.at[down, 0], ag_s.at[0, 0], ag_r.at[down, 0], dp=down)
    ag_copy(down, 0, 2, up).start()
    wait_recv(ag.at[up, 1], ag_s.at[0, 1], ag_r.at[up, 1], dp=up)
    ag_copy(up, 1, 2, down).start()

    wait_recv(ag.at[down, 1], ag_s.at[0, 1], ag_r.at[down, 1], dp=down)
    wait_recv(ag.at[up, 0], ag_s.at[0, 0], ag_r.at[up, 0], dp=up)

    @pl.loop(0, 2)
    def _(k):
        step_both(lax.rem(y + 1 + 2 * k, n_dp))

    wait_recv(ag.at[far, 0], ag_s.at[0, 0], ag_r.at[far, 0], dp=down)
    wait_recv(ag.at[far, 1], ag_s.at[0, 1], ag_r.at[far, 1], dp=up)
    step_both(far)

    @pl.loop(1, n_dp)
    def _(off):
        sum_copy(lax.rem(y + off, n_dp)).wait_send()

    to_sib.wait_send()
    for c in rs_copies():
        c.wait_send()
    for h in range(2):
        ag_copy(y, h, 0, up).wait_send()
        ag_copy(y, h, 1, down).wait_send()
    ag_copy(down, 0, 2, up).wait_send()
    ag_copy(up, 1, 2, down).wait_send()


def on_device(n_dp, n_item, queries, item_table, adagrad_state, pos_owner, pos_row, neg_rows):
    ex, width = queries.shape
    rows = item_table.shape[0]
    neg = neg_rows.shape[0]
    chips = n_item // 2
    cap = 3 * ex // n_item
    quarter = rows // n_dp
    vmem, hbm = pl.BlockSpec(memory_space=pltpu.VMEM), pl.BlockSpec(memory_space=pl.ANY)
    dma = pltpu.SemaphoreType.DMA
    n_neg = 2 * n_dp * chips * neg
    flops = 2 * width * (3 * n_neg * ex + 3 * n_item * cap * (rows + ex))
    grad, loss, new_table, new_state = pl.pallas_call(
        functools.partial(main_kernel, n_dp, n_item),
        out_shape=(
            pltpu.VMEM((ex, width), BF),
            pltpu.VMEM((1, ex), F32),
            pltpu.VMEM((rows, width), F32),
            pltpu.VMEM((1, rows), F32),
        ),
        in_specs=[pl.BlockSpec(memory_space=pltpu.SMEM), vmem, hbm, vmem, vmem, vmem, vmem],
        out_specs=(vmem, vmem, vmem, vmem),
        scratch_shapes=[
            pltpu.VMEM((neg, width), F32),
            pltpu.VMEM((rows, width), BF),
            pltpu.VMEM((width, ex), BF),
            pltpu.VMEM((n_item, 1, LANES), F32),
            pltpu.VMEM((n_item, 1, LANES), F32),
            pltpu.VMEM((2 * n_dp, chips, neg, width), BF),
            pltpu.VMEM((2 * n_dp, chips, 1, LANES), F32),
            pltpu.VMEM((n_item, cap, width), BF),
            pltpu.VMEM((n_item, cap, width), BF),
            pltpu.VMEM((n_item, cap, width), BF),
            pltpu.VMEM((n_item, cap, width), BF),
            pltpu.VMEM((ex, width), F32),
            pltpu.VMEM((ex, width), F32),
            pltpu.VMEM((ex, width), BF),
            pltpu.VMEM((width, ex), F32),
            pltpu.VMEM((8, ex), F32),
            pltpu.VMEM((2 * n_dp, chips, neg, ex), BF),
            pltpu.VMEM((2, chips, n_dp * neg, width), BF),
            pltpu.VMEM((chips, n_dp * neg, width), BF),
            pltpu.VMEM((chips, n_dp * neg, width), BF),
            pltpu.VMEM((chips, n_dp * neg, width), BF),
            pltpu.VMEM((n_dp, n_dp * neg, width), BF),
            pltpu.VMEM((rows, width), F32),
            pltpu.VMEM((3, 2, quarter // 2, width), BF),
            pltpu.VMEM((2, quarter // 2, width), BF),
            pltpu.VMEM((2, 2, quarter // 2, width), BF),
            pltpu.VMEM((n_dp, 2, quarter // 2, width), BF),
            dma((n_item,)), dma((n_item,)),
            dma((chips,)), dma((chips,)),
            dma((chips,)), dma((chips,)),
            dma((3, 2)), dma((n_dp, 2)),
            dma((3, 2)), dma((n_dp, 2)),
            dma((n_dp,)), dma((n_dp,)),
            dma((n_dp,)), dma((n_dp,)),
            dma((n_item,)), dma((n_item,)),
            dma((n_item,)), dma((n_item,)),
            dma, dma,
            dma((chips,)), dma((chips,)),
            dma((n_dp,)), dma((n_dp,)),
            dma((3, 2)), dma((2,)), dma((2, 2)),
            dma((3, 2)), dma((n_dp, 2)),
            dma((2 * n_dp,)),
        ],
        compiler_params=pltpu.CompilerParams(collective_id=0, has_side_effects=True, vmem_limit_bytes=56 * 2**20),
        cost_estimate=pl.CostEstimate(flops=flops, bytes_accessed=12 * 2**20, transcendentals=n_neg * ex),
        name="training_step",
    )(
        neg_rows, queries, item_table, adagrad_state.reshape(1, rows), pos_owner.reshape(1, ex), pos_row.reshape(1, ex),
        neg_rows.reshape(1, neg),
    )
    return grad, loss.reshape(ex), new_table, new_state.reshape(rows)


def solution(mesh):
    both = ("dp", "item")
    return jax.shard_map(
        functools.partial(on_device, mesh.shape["dp"], mesh.shape["item"]),
        mesh=mesh,
        in_specs=(P(both, None), P("item", None), P("item"), P(both, None), P(both), P(both)),
        out_specs=(P(both, None), P(both), P("item", None), P("item")),
        check_vma=False,
    )
```

```python
import functools
import math

import jax
import jax.numpy as jnp
from jax import lax
from jax.experimental import pallas as pl
from jax.experimental.pallas import tpu as pltpu
from jax.sharding import PartitionSpec as P

INV_TEMP = 20.0
LEARN_RATE = 0.05
EPSILON = 1e-06
LOG2E = 1.4426950408889634
BF, F32 = jnp.bfloat16, jnp.float32
LANES = 128


def dot(a, b):
    return jnp.dot(a, b, preferred_element_type=F32)


def iota(shape, dim):
    return lax.broadcasted_iota(jnp.int32, shape, dim).astype(F32)


def eye():
    return lax.broadcasted_iota(jnp.int32, (LANES, LANES), 0) == lax.broadcasted_iota(jnp.int32, (LANES, LANES), 1)


def row_to_col(row):
    parts = []
    for k in range(row.shape[1] // LANES):
        wide = jnp.broadcast_to(row[:, k * LANES : (k + 1) * LANES], (LANES, LANES))
        parts.append(jnp.sum(jnp.where(eye(), wide, 0.0), axis=1, keepdims=True))
    return parts[0] if len(parts) == 1 else jnp.concatenate(parts, axis=0)


def col_to_row(col):
    parts = []
    for k in range(col.shape[0] // LANES):
        wide = jnp.broadcast_to(col[k * LANES : (k + 1) * LANES], (LANES, LANES))
        parts.append(jnp.sum(jnp.where(eye(), wide, 0.0), axis=0, keepdims=True))
    return parts[0] if len(parts) == 1 else jnp.concatenate(parts, axis=1)


def pick_lanes(col, first, count):
    return (col == iota((col.shape[0], count), 1) + first).astype(BF)


def pick_rows(row, first, count):
    return (row == iota((count, row.shape[1]), 0) + first).astype(BF)


OFFSETS = (
    (1, 2), (3, 2), (2, 1), (2, 3), (1, 1), (3, 3), (1, 3), (3, 1),
    (2, 2), (2, 0), (0, 2), (0, 0), (0, 1), (0, 3), (1, 0), (3, 0),
)


def main_kernel(
    n_dp, n_item,
    neg_s_ref, q_ref, table_hbm, state_ref, owner_ref, row_ref, neg_ref,
    grad_ref, loss_ref, table_ref, state_out,
    neg_f, tsend, qt, req_out, req_in, negbuf, nidbuf, found, returned, outbox, inbox, acc, pos_f, g_bf, ut, tot, et, part, sib_in, by_x, by_z, in_x, in_z, mid_x, mid_z, end_x, end_z, y_out, y_in, y_sum,
    dense_f, rs_out, relay_in, rs_in, ag,
    req_s, req_r, neg_s, neg_r, nid_s, nid_r, pc_s, pc_r, pi_s, pi_r, sn_s, sn_r, si_s, si_r, pos_s, pos_r, g_s, g_r, sib_s, sib_r, hop_s, hop_r, y_s, y_r,
    rs_s, relay_r, rs_r, ag_s, ag_r, load_s,
):
    ex, width = q_ref.shape
    rows = table_ref.shape[0]
    quarter = rows // n_dp
    hq = quarter // 2
    chips = n_item // 2
    cap = 3 * ex // n_item
    neg = negbuf.shape[2]
    y, me = lax.axis_index("dp"), lax.axis_index("item")
    chip, core = me // 2, lax.rem(me, 2)
    sibling = chip * 2 + 1 - core
    up, far, down = lax.rem(y + 1, n_dp), lax.rem(y + 2, n_dp), lax.rem(y + 3, n_dp)

    def copy(src, dst, send, recv, **where):
        return pltpu.make_async_remote_copy(
            src_ref=src, dst_ref=dst, send_sem=send, recv_sem=recv, device_id=where, device_id_type=pl.DeviceIdType.MESH
        )

    def load(k):
        at = pl.ds(pl.multiple_of(k * hq, hq), hq)
        return pltpu.make_async_copy(table_hbm.at[at, :], table_ref.at[at, :], load_s)

    @pl.loop(0, 2 * n_dp)
    def _(k):
        load(k).start()

    def wait_all(part, send=None, recv=None):
        c = copy(part, part, recv if send is None else send, send if recv is None else recv, item=sibling)
        if send is None:
            c.wait_recv()
        else:
            c.wait_send()

    barrier = pltpu.get_barrier_semaphore()

    @pl.loop(1, n_item)
    def _(off):
        pl.semaphore_signal(barrier, inc=1, device_id={"item": lax.rem(me + off, n_item)}, device_id_type=pl.DeviceIdType.MESH)

    @pl.loop(1, n_dp)
    def _(off):
        pl.semaphore_signal(barrier, inc=1, device_id={"dp": lax.rem(y + off, n_dp)}, device_id_type=pl.DeviceIdType.MESH)

    owner_r = owner_ref[...].astype(F32)
    row_r = row_ref[...].astype(F32)
    gid_r = owner_r * rows + row_r
    owners_r = (owner_r == iota((n_item, ex), 0)).astype(F32)
    before = (iota((LANES, LANES), 0) < iota((LANES, LANES), 1)).astype(BF)
    seen = jnp.zeros((n_item, 1), F32)
    slots = []
    for k in range(ex // LANES):
        named = owners_r[:, k * LANES : (k + 1) * LANES]
        earlier = dot(named.astype(BF), before) + seen
        slots.append(jnp.sum(earlier * named, axis=0, keepdims=True))
        seen += jnp.sum(named, axis=1, keepdims=True)
    slot_r = jnp.concatenate(slots, axis=1)
    place_r = owner_r * cap + slot_r
    high_r = jnp.floor(row_r * (1.0 / 64.0))
    low_r = row_r - 64.0 * high_r
    at_slot = slot_r == iota((LANES, ex), 0)
    both = jnp.concatenate([jnp.where(at_slot, high_r, 0.0), jnp.where(at_slot, low_r, 0.0)], axis=0).astype(BF)
    asked2 = lax.dot_general(owners_r.astype(BF), both, (((1,), (1,)), ((), ())), preferred_element_type=F32)
    asked = asked2[:, :LANES] * 64.0 + asked2[:, LANES:]
    for s in range(n_item):
        req_out[s] = asked[s : s + 1, :]

    pl.semaphore_wait(barrier, n_item - 1 + n_dp - 1)

    req_in[me] = req_out[me]

    def req_copy(peer):
        return copy(req_out.at[peer], req_in.at[me], req_s, req_r, item=peer)

    @pl.loop(1, n_item)
    def _(off):
        req_copy(lax.rem(me + off, n_item)).start()

    pltpu.make_async_copy(table_hbm, table_ref, load_s).wait()

    for k in range(neg):
        neg_f[k : k + 1, :] = table_ref[pl.ds(neg_s_ref[k], 1), :]
    t = neg_f[...]
    mine = y * 2 + core
    negbuf[mine, chip] = (t / jnp.sqrt(jnp.sum(t * t, axis=1, keepdims=True) + EPSILON)).astype(BF)
    nidbuf[mine, chip] = jnp.concatenate([neg_ref[...].astype(F32), jnp.full((1, LANES - neg), -1.0, F32)], axis=1)

    def plane_copies(peer_chip):
        to = peer_chip * 2 + core
        return (
            copy(negbuf.at[mine, chip], negbuf.at[mine, chip], neg_s, neg_r, item=to),
            copy(nidbuf.at[mine, chip], nidbuf.at[mine, chip], nid_s, nid_r, item=to),
        )

    @pl.loop(1, chips)
    def _(off):
        for c in plane_copies(lax.rem(chip + off, chips)):
            c.start()

    tile = min(512, rows)

    @pl.loop(0, rows // tile)
    def _(k):
        at = pl.ds(pl.multiple_of(k * tile, tile), tile)
        t = table_ref[at, :]
        tsend[at, :] = (t / jnp.sqrt(jnp.sum(t * t, axis=1, keepdims=True) + EPSILON)).astype(BF)

    q = q_ref[...].astype(F32)
    q_norm = jnp.sqrt(jnp.sum(q * q, axis=1, keepdims=True) + EPSILON)
    acc[...] = q / q_norm
    qt[...] = jnp.transpose(acc[...]).astype(BF)

    def wait_recv(dst, send, recv, **where):
        copy(dst, dst, send, recv, **where).wait_recv()

    wait_all(req_in.at[pl.ds(0, n_item - 1)], recv=req_r)

    if chips == len(OFFSETS):
        order = [lax.rem(chip // 4 + dz, 4) * 4 + lax.rem(chip + dx, 4) for dz, dx in OFFSETS]
    else:
        order = [lax.rem(chip + d, chips) for d in range(1, chips + 1)]
    mates = [2 * c + side for c in order for side in range(2)]
    batch = min(8, n_item)
    batches = [mates[k : k + batch] for k in range(0, n_item, batch)]

    def one_of(k):
        group = batches[-1]
        for n in range(len(batches) - 2, -1, -1):
            group = [jnp.where(k == n, a, b) for a, b in zip(batches[n], group)]
        return group

    own_batch = (OFFSETS.index((0, 0)) if chips == len(OFFSETS) else chips - 1) * 2 // batch

    def wait_batch(k, buffer, recv):
        @pl.when(k != own_batch)
        def _():
            wait_all(buffer.at[pl.ds(0, batch)], recv=recv.at[k])

        @pl.when(k == own_batch)
        def _():
            wait_all(buffer.at[pl.ds(0, batch - 1)], recv=recv.at[k])

    def pos_copy(peer, k):
        return copy(found.at[peer], returned.at[me], pos_s, pos_r.at[k], item=peer)

    def gather(k):
        group = one_of(k)
        ids = jnp.concatenate([row_to_col(req_in[src])[:cap] for src in group], axis=0)
        got = jnp.zeros((batch * cap, width), F32)
        for t in range(rows // tile):
            got += dot(pick_lanes(ids, float(t * tile), tile), tsend[t * tile : (t + 1) * tile, :])
        for s, src in enumerate(group):
            found[src] = got[s * cap : (s + 1) * cap].astype(BF)

            @pl.when(src != me)
            def _():
                pos_copy(src, k).start()

    @pl.loop(0, 1)
    def _(k):
        gather(k)


    wait_all(negbuf.at[mine, pl.ds(0, chips - 1)], recv=neg_r)
    wait_all(nidbuf.at[mine, pl.ds(0, chips - 1)], recv=nid_r)

    half = chips // 2

    def piece_part(d, h):
        return negbuf.at[d * 2 + core, pl.ds(h * half, half)], nidbuf.at[d * 2 + core, pl.ds(h * half, half)]

    def y_copies(d, h, dest):
        rows_part, ids_part = piece_part(d, h)
        return (
            copy(rows_part, rows_part, pc_s, pc_r.at[d, h], dp=dest),
            copy(ids_part, ids_part, pi_s, pi_r.at[d, h], dp=dest),
        )

    def y_wait(d, h, dest):
        for c in y_copies(d, h, dest):
            c.wait_recv()

    def sib_copies(d, side):
        piece = d * 2 + side
        return (
            copy(negbuf.at[piece], negbuf.at[piece], sn_s, sn_r.at[d], item=sibling),
            copy(nidbuf.at[piece], nidbuf.at[piece], si_s, si_r.at[d], item=sibling),
        )

    def to_sibling(d):
        for c in sib_copies(d, core):
            c.start()

    def from_sibling(d):
        for c in sib_copies(d, 1 - core):
            c.wait_recv()

    def send_y(d, h, dest):
        for c in y_copies(d, h, dest):
            c.start()

    send_y(y, 0, up)
    send_y(y, 1, down)
    send_y(y, 1, up)
    send_y(y, 0, down)
    to_sibling(y)

    @pl.loop(1, len(batches))
    def _(k):
        gather(k)

    returned[me] = found[me]

    tot[...] = jnp.zeros_like(tot)

    def pass1(piece):
        @pl.loop(0, chips // half)
        def _(h):
            first = h * half
            block = negbuf[piece, pl.ds(first, half)].reshape(half * neg, width)
            ids = jnp.concatenate(
                [
                    row_to_col(nidbuf[piece, first + z])[:neg]
                    + (((first + z) * 2 + lax.rem(piece, 2)) * rows).astype(F32)
                    for z in range(half)
                ],
                axis=0,
            )
            e = jnp.where(ids != gid_r, jnp.exp2(dot(block, qt[...]) * (INV_TEMP * LOG2E)), 0.0)
            tot[...] += jnp.sum(e.reshape(half * neg // 8, 8, ex), axis=0)
            eb = e.astype(BF)
            et[piece, pl.ds(first, half)] = eb.reshape(half, neg, ex)

    from_sibling(y)

    @pl.loop(0, 2)
    def _(side):
        pass1(y * 2 + side)

    y_wait(down, 0, down)
    send_y(down, 0, up)
    y_wait(up, 1, up)
    send_y(up, 1, down)
    y_wait(down, 1, down)
    to_sibling(down)
    y_wait(up, 0, up)
    to_sibling(up)

    @pl.loop(0, 2)
    def _(k):
        pass1(lax.rem(y + 1 + 2 * k, n_dp) * 2 + core)

    from_sibling(down)
    from_sibling(up)

    @pl.loop(0, 2)
    def _(k):
        pass1(lax.rem(y + 1 + 2 * k, n_dp) * 2 + 1 - core)

    y_wait(far, 0, down)
    y_wait(far, 1, up)
    to_sibling(far)
    pass1(far * 2 + core)
    from_sibling(far)
    pass1(far * 2 + 1 - core)

    place_c = row_to_col(place_r)
    pos_f[...] = jnp.zeros_like(pos_f)

    def slots_of(group):
        first = lax.broadcasted_iota(jnp.int32, (1, cap), 1)
        return jnp.concatenate([first + src * cap for src in group], axis=1).astype(F32)

    @pl.loop(0, len(batches))
    def _(k):
        group = one_of(k)
        wait_batch(k, returned, pos_r)
        pick = (place_c == slots_of(group)).astype(BF)
        pos_f[...] += dot(pick, jnp.concatenate([returned[src] for src in group], axis=0))

    q_hat = acc[...]
    pos_e = pos_f[...]
    s_pos = INV_TEMP * jnp.sum(q_hat.astype(BF).astype(F32) * pos_e, axis=1, keepdims=True)
    neg_tot = row_to_col(jnp.sum(tot[...], axis=0, keepdims=True))
    lse = jnp.log(jnp.exp(s_pos) + neg_tot)
    loss_ref[...] = col_to_row(lse - s_pos)
    coef = jnp.exp(s_pos - lse) - 1.0
    inv_tot = jnp.exp(-lse)

    g_bf[...] = (INV_TEMP * coef * q_hat).astype(BF)

    def g_copy(peer, k):
        return copy(outbox.at[peer], inbox.at[me], g_s, g_r.at[k], item=peer)

    @pl.loop(0, len(batches))
    def _(k):
        group = one_of(k)
        wanted = jnp.concatenate([iota((cap, 1), 0) + (src * cap).astype(F32) for src in group], axis=0)
        rows_out = dot((place_r == wanted).astype(BF), g_bf[...])
        for s, src in enumerate(group):
            outbox[src] = rows_out[s * cap : (s + 1) * cap].astype(BF)

            @pl.when(src != me)
            def _():
                g_copy(src, k).start()

    inbox[me] = outbox[me]

    q_scaled = (q_hat.astype(BF).astype(F32) * (INV_TEMP * inv_tot)).astype(BF)

    def pass2(side):
        @pl.loop(0, n_dp)
        def _(d):
            for h in range(chips // half):
                at = slice(h * half, (h + 1) * half)
                p = dot(et[d * 2 + side, at].reshape(half * neg, ex), q_scaled)
                p = p.astype(BF).reshape(half, neg, width)
                for z in range(half):
                    part[side, h * half + z, pl.ds(pl.multiple_of(d * neg, neg), neg), :] = p[z]

    pass2(1 - core)
    to_sib = copy(part.at[1 - core], sib_in, sib_s, sib_r, item=sibling)
    to_sib.start()
    pass2(core)

    to_sib.wait_recv()

    side = math.isqrt(chips)
    nz, nx = (side, side) if side * side == chips else (1, chips)
    my_z, my_x = chip // nx, lax.rem(chip, nx)
    hn = n_dp * neg // 2

    @pl.loop(0, nz)
    def _(z):
        @pl.loop(0, nx)
        def _(x):
            at = z * nx + x
            both = (part[core, at].astype(F32) + sib_in[at].astype(F32)).astype(BF)
            by_x[x, z] = both[:hn]
            by_z[z, x] = both[hn:]

    def at_x(x):
        return (my_z * nx + x) * 2 + core

    def at_z(z):
        return (z * nx + my_x) * 2 + core

    def first_x(x):
        return copy(by_x.at[x], in_x.at[my_x], hop_s.at[0], hop_r.at[0], item=at_x(x))

    def first_z(z):
        return copy(by_z.at[z], in_z.at[my_z], hop_s.at[1], hop_r.at[1], item=at_z(z))

    def second_z(z):
        return copy(mid_z.at[z], end_z.at[my_z], hop_s.at[2], hop_r.at[2], item=at_z(z))

    def second_x(x):
        return copy(mid_x.at[x], end_x.at[my_x], hop_s.at[3], hop_r.at[3], item=at_x(x))

    def start_others(mine_at, count, make):
        @pl.loop(1, count)
        def _(off):
            make(lax.rem(mine_at + off, count)).start()

    def wait_others(buffer, count, **sem):
        if count > 1:
            wait_all(buffer.at[pl.ds(0, count - 1)], **sem)

    start_others(my_x, nx, first_x)
    start_others(my_z, nz, first_z)
    in_x[my_x] = by_x[my_x]
    in_z[my_z] = by_z[my_z]

    def add_to_dense(group, d, fresh):
        ids = jnp.concatenate([req_in[src][:, :cap] for src in group], axis=1)
        came = jnp.concatenate([inbox[src] for src in group], axis=0)
        at = pl.ds(pl.multiple_of(d * quarter, quarter), quarter)
        new = dot(pick_rows(ids, (d * quarter).astype(F32), quarter), came)
        if fresh:
            dense_f[at, :] = new
        else:
            dense_f[at, :] += new

    def wait_inbox(k):
        wait_all(inbox.at[pl.ds(0, batch - 1 if k == own_batch else batch)], recv=g_r.at[k])

    head, tail = batches[:-2], batches[-2:]
    for k, group in enumerate(head):
        wait_inbox(k)

        @pl.loop(0, n_dp)
        def _(d):
            add_to_dense(group, d, k == 0)

    for k in range(len(head), len(batches)):
        wait_inbox(k)

    def finish(d):
        @pl.loop(0, 1)
        def _(_):
            add_to_dense([src for group in tail for src in group], d, not head)

    def rs_copies():
        return (
            copy(rs_out.at[0, 0], relay_in.at[0], rs_s, relay_r.at[0], dp=up),
            copy(rs_out.at[0, 1], relay_in.at[1], rs_s, relay_r.at[1], dp=down),
            copy(rs_out.at[1, 0], rs_in.at[0, 0], rs_s, rs_r.at[0, 0], dp=up),
            copy(rs_out.at[1, 1], rs_in.at[0, 1], rs_s, rs_r.at[0, 1], dp=up),
            copy(rs_out.at[2, 0], rs_in.at[1, 0], rs_s, rs_r.at[1, 0], dp=down),
            copy(rs_out.at[2, 1], rs_in.at[1, 1], rs_s, rs_r.at[1, 1], dp=down),
        )

    def dense_part(d, h):
        return dense_f[pl.ds(pl.multiple_of(d * quarter + h * hq, hq), hq), :]

    far0, far1, up0, up1, down0, down1 = rs_copies()
    finish(far)
    rs_out[0, 0] = dense_part(far, 0).astype(BF)
    far0.start()
    rs_out[0, 1] = dense_part(far, 1).astype(BF)
    far1.start()
    finish(up)
    rs_out[1, 1] = dense_part(up, 1).astype(BF)
    up1.start()
    finish(down)
    rs_out[2, 0] = dense_part(down, 0).astype(BF)
    down0.start()
    finish(y)
    far0.wait_recv()
    rs_out[1, 0] = (dense_part(up, 0) + relay_in[0].astype(F32)).astype(BF)
    up0.start()
    far1.wait_recv()
    rs_out[2, 1] = (dense_part(down, 1) + relay_in[1].astype(F32)).astype(BF)
    down1.start()

    wait_others(in_x, nx, recv=hop_r.at[0])
    wait_others(in_z, nz, recv=hop_r.at[1])

    def added(buffer):
        total = buffer[0].astype(F32)
        for n in range(1, buffer.shape[0]):
            total += buffer[n].astype(F32)
        return total.astype(BF)

    mid_z[...] = added(in_x)
    mid_x[...] = added(in_z)
    start_others(my_z, nz, second_z)
    start_others(my_x, nx, second_x)
    end_z[my_z] = mid_z[my_z]
    end_x[my_x] = mid_x[my_x]

    ut[...] = jnp.zeros_like(ut)

    @pl.loop(0, 2 * n_dp)
    def _(piece):
        block = negbuf[piece].reshape(chips * neg, width)
        eb = et[piece].reshape(chips * neg, ex)
        ut[...] += lax.dot_general(block, eb, (((0,), (0,)), ((), ())), preferred_element_type=F32)

    g_q = INV_TEMP * (coef * pos_f[...] + jnp.transpose(ut[...]) * inv_tot)
    grad_ref[...] = ((g_q - acc[...] * jnp.sum(acc[...] * g_q, axis=1, keepdims=True)) / q_norm).astype(BF)

    wait_all(req_out.at[pl.ds(0, n_item - 1)], send=req_s)
    wait_all(found.at[pl.ds(0, n_item - 1)], send=pos_s)
    wait_all(outbox.at[pl.ds(0, n_item - 1)], send=g_s)
    wait_all(negbuf.at[mine, pl.ds(0, chips - 1)], send=neg_s)
    wait_all(nidbuf.at[mine, pl.ds(0, chips - 1)], send=nid_s)
    wait_all(negbuf.at[pl.ds(0, 3)], send=pc_s)
    wait_all(nidbuf.at[pl.ds(0, 3)], send=pi_s)
    wait_all(negbuf.at[pl.ds(0, n_dp)], send=sn_s)
    wait_all(nidbuf.at[pl.ds(0, n_dp)], send=si_s)
    to_sib.wait_send()
    wait_others(by_x, nx, send=hop_s.at[0])
    wait_others(by_z, nz, send=hop_s.at[1])

    wait_others(end_z, nz, recv=hop_r.at[2])
    wait_others(end_x, nx, recv=hop_r.at[3])
    sums = jnp.concatenate([added(end_z), added(end_x)], axis=0)
    for d in range(n_dp):
        y_out[d] = sums[d * neg : (d + 1) * neg]
    y_in[y] = y_out[y]

    def part_copy(dest):
        return copy(y_out.at[dest], y_in.at[y], y_s.at[0], y_r.at[0], dp=dest)

    def sum_copy(dest):
        return copy(y_sum.at[y], y_sum.at[y], y_s.at[1], y_r.at[1], dp=dest)

    start_others(y, n_dp, part_copy)

    wait_others(y_in, n_dp, recv=y_r.at[0])
    y_sum[y] = added(y_in)
    start_others(y, n_dp, sum_copy)
    up1.wait_recv()
    up0.wait_recv()
    down0.wait_recv()
    down1.wait_recv()
    for h in range(2):
        ag[y, h] = (dense_part(y, h) + rs_in[0, h].astype(F32) + rs_in[1, h].astype(F32)).astype(BF)

    def ag_copy(slot, h, dest):
        return copy(ag.at[slot, h], ag.at[slot, h], ag_s, ag_r.at[slot, h], dp=dest)

    ag_copy(y, 0, up).start()
    ag_copy(y, 1, down).start()
    ag_copy(y, 1, up).start()
    ag_copy(y, 0, down).start()
    wait_others(y_sum, n_dp, recv=y_r.at[1])
    neg_sums = y_sum[...].reshape(n_dp * neg, width)
    neg_ids = jnp.concatenate([nidbuf[d * 2 + core, chip][:, :neg] for d in range(n_dp)], axis=1)

    def step(d, h):
        first = d * quarter + h * hq
        at = pl.ds(pl.multiple_of(first, hq), hq)
        pick = (neg_ids == iota((hq, n_dp * neg), 0) + first.astype(F32)).astype(BF)
        g = ag[d, h].astype(F32) + dot(pick, neg_sums)
        t = table_ref[at, :]
        norm = jnp.sqrt(jnp.sum(t * t, axis=1, keepdims=True) + EPSILON)
        unit = t / norm
        g_row = (g - unit * jnp.sum(unit * g, axis=1, keepdims=True)) / norm
        mean = jnp.sum(g_row * g_row, axis=1, keepdims=True) * (1.0 / width)
        new = state_ref[:, at] + col_to_row(mean)
        state_out[:, at] = new
        table_ref[at, :] = t - LEARN_RATE * g_row / jnp.sqrt(row_to_col(new))

    def step_both(d):
        @pl.loop(0, 2)
        def _(h):
            step(d, h)

    step_both(y)

    wait_recv(ag.at[down, 0], ag_s, ag_r.at[down, 0], dp=down)
    ag_copy(down, 0, up).start()
    wait_recv(ag.at[up, 1], ag_s, ag_r.at[up, 1], dp=up)
    ag_copy(up, 1, down).start()

    wait_recv(ag.at[down, 1], ag_s, ag_r.at[down, 1], dp=down)
    wait_recv(ag.at[up, 0], ag_s, ag_r.at[up, 0], dp=up)

    @pl.loop(0, 2)
    def _(k):
        step_both(lax.rem(y + 1 + 2 * k, n_dp))

    wait_recv(ag.at[far, 0], ag_s, ag_r.at[far, 0], dp=down)
    wait_recv(ag.at[far, 1], ag_s, ag_r.at[far, 1], dp=up)
    step_both(far)

    wait_others(mid_z, nz, send=hop_s.at[2])
    wait_others(mid_x, nx, send=hop_s.at[3])
    wait_others(y_out, n_dp, send=y_s.at[0])
    wait_others(y_sum, n_dp, send=y_s.at[1])
    wait_all(rs_out, send=rs_s)
    wait_all(ag.at[pl.ds(0, 3)], send=ag_s)


def write_kernel(*refs):
    copies = [pltpu.make_async_copy(refs[k], refs[4 + k], refs[8].at[k]) for k in range(4)]
    for c in copies:
        c.start()
    for c in copies:
        c.wait()


def on_device(n_dp, n_item, queries, item_table, adagrad_state, pos_owner, pos_row, neg_rows):
    ex, width = queries.shape
    rows = item_table.shape[0]
    neg = neg_rows.shape[0]
    chips = n_item // 2
    cap = 3 * ex // n_item
    quarter = rows // n_dp
    vmem, hbm = pl.BlockSpec(memory_space=pltpu.VMEM), pl.BlockSpec(memory_space=pl.ANY)
    dma = pltpu.SemaphoreType.DMA
    n_neg = 2 * n_dp * chips * neg
    n_batches = n_item // min(8, n_item)
    side = math.isqrt(chips)
    nz, nx = (side, side) if side * side == chips else (1, chips)
    hn = n_dp * neg // 2
    flops = 2 * width * (3 * n_neg * ex + 3 * n_item * cap * (rows + ex))
    grad, loss, new_table, new_state = pl.pallas_call(
        functools.partial(main_kernel, n_dp, n_item),
        out_shape=(
            pltpu.VMEM((ex, width), BF),
            pltpu.VMEM((1, ex), F32),
            pltpu.VMEM((rows, width), F32),
            pltpu.VMEM((1, rows), F32),
        ),
        in_specs=[pl.BlockSpec(memory_space=pltpu.SMEM), vmem, hbm, vmem, vmem, vmem, vmem],
        out_specs=(vmem, vmem, vmem, vmem),
        scratch_shapes=[
            pltpu.VMEM((neg, width), F32),
            pltpu.VMEM((rows, width), BF),
            pltpu.VMEM((width, ex), BF),
            pltpu.VMEM((n_item, 1, LANES), F32),
            pltpu.VMEM((n_item, 1, LANES), F32),
            pltpu.VMEM((2 * n_dp, chips, neg, width), BF),
            pltpu.VMEM((2 * n_dp, chips, 1, LANES), F32),
            pltpu.VMEM((n_item, cap, width), BF),
            pltpu.VMEM((n_item, cap, width), BF),
            pltpu.VMEM((n_item, cap, width), BF),
            pltpu.VMEM((n_item, cap, width), BF),
            pltpu.VMEM((ex, width), F32),
            pltpu.VMEM((ex, width), F32),
            pltpu.VMEM((ex, width), BF),
            pltpu.VMEM((width, ex), F32),
            pltpu.VMEM((8, ex), F32),
            pltpu.VMEM((2 * n_dp, chips, neg, ex), BF),
            pltpu.VMEM((2, chips, n_dp * neg, width), BF),
            pltpu.VMEM((chips, n_dp * neg, width), BF),
            pltpu.VMEM((nx, nz, hn, width), BF),
            pltpu.VMEM((nz, nx, hn, width), BF),
            pltpu.VMEM((nx, nz, hn, width), BF),
            pltpu.VMEM((nz, nx, hn, width), BF),
            pltpu.VMEM((nx, hn, width), BF),
            pltpu.VMEM((nz, hn, width), BF),
            pltpu.VMEM((nx, hn, width), BF),
            pltpu.VMEM((nz, hn, width), BF),
            pltpu.VMEM((n_dp, neg, width), BF),
            pltpu.VMEM((n_dp, neg, width), BF),
            pltpu.VMEM((n_dp, neg, width), BF),
            pltpu.VMEM((rows, width), F32),
            pltpu.VMEM((3, 2, quarter // 2, width), BF),
            pltpu.VMEM((2, quarter // 2, width), BF),
            pltpu.VMEM((2, 2, quarter // 2, width), BF),
            pltpu.VMEM((n_dp, 2, quarter // 2, width), BF),
            dma, dma,
            dma, dma,
            dma, dma,
            dma, dma((n_dp, 2)),
            dma, dma((n_dp, 2)),
            dma, dma((n_dp,)),
            dma, dma((n_dp,)),
            dma, dma((n_batches,)),
            dma, dma((n_batches,)),
            dma, dma,
            dma((4,)), dma((4,)),
            dma((2,)), dma((2,)),
            dma, dma((2,)), dma((2, 2)),
            dma, dma((n_dp, 2)),
            dma,
        ],
        compiler_params=pltpu.CompilerParams(collective_id=0, has_side_effects=True, vmem_limit_bytes=56 * 2**20),
        cost_estimate=pl.CostEstimate(flops=flops, bytes_accessed=12 * 2**20, transcendentals=n_neg * ex),
        name="training_step",
    )(
        neg_rows, queries, item_table, adagrad_state.reshape(1, rows), pos_owner.reshape(1, ex), pos_row.reshape(1, ex),
        neg_rows.reshape(1, neg),
    )

    made = [pltpu.with_memory_space_constraint(a, pltpu.VMEM) for a in (grad, loss, new_table, new_state)]
    grad, loss, new_table, new_state = pl.pallas_call(
        write_kernel,
        out_shape=[jax.ShapeDtypeStruct(a.shape, a.dtype) for a in made],
        in_specs=[vmem] * 4,
        out_specs=[hbm] * 4,
        scratch_shapes=[dma((4,))],
        compiler_params=pltpu.CompilerParams(vmem_limit_bytes=2**20),
        name="write_results",
    )(*made)
    return grad, loss.reshape(ex), new_table, new_state.reshape(rows)


def solution(mesh):
    both = ("dp", "item")
    return jax.shard_map(
        functools.partial(on_device, mesh.shape["dp"], mesh.shape["item"]),
        mesh=mesh,
        in_specs=(P(both, None), P("item", None), P("item"), P(both, None), P(both), P(both)),
        out_specs=(P(both, None), P(both), P("item", None), P("item")),
        check_vma=False,
    )
```

```python
import functools
import math

import jax
import jax.numpy as jnp
from jax import lax
from jax.experimental import pallas as pl
from jax.experimental.pallas import tpu as pltpu
from jax.sharding import PartitionSpec as P

INV_TEMP = 20.0
LEARN_RATE = 0.05
EPSILON = 1e-06
LOG2E = 1.4426950408889634
BF, F32 = jnp.bfloat16, jnp.float32
LANES = 128


def dot(a, b):
    return jnp.dot(a, b, preferred_element_type=F32)


def iota(shape, dim):
    return lax.broadcasted_iota(jnp.int32, shape, dim).astype(F32)


def eye():
    return lax.broadcasted_iota(jnp.int32, (LANES, LANES), 0) == lax.broadcasted_iota(jnp.int32, (LANES, LANES), 1)


def row_to_col(row):
    parts = []
    for k in range(row.shape[1] // LANES):
        wide = jnp.broadcast_to(row[:, k * LANES : (k + 1) * LANES], (LANES, LANES))
        parts.append(jnp.sum(jnp.where(eye(), wide, 0.0), axis=1, keepdims=True))
    return parts[0] if len(parts) == 1 else jnp.concatenate(parts, axis=0)


def col_to_row(col):
    parts = []
    for k in range(col.shape[0] // LANES):
        wide = jnp.broadcast_to(col[k * LANES : (k + 1) * LANES], (LANES, LANES))
        parts.append(jnp.sum(jnp.where(eye(), wide, 0.0), axis=0, keepdims=True))
    return parts[0] if len(parts) == 1 else jnp.concatenate(parts, axis=1)


def pick_lanes(col, first, count):
    return (col == iota((col.shape[0], count), 1) + first).astype(BF)


def pick_rows(row, first, count):
    return (row == iota((count, row.shape[1]), 0) + first).astype(BF)


OFFSETS = (
    (1, 2), (3, 2), (2, 1), (2, 3), (1, 1), (3, 3), (1, 3), (3, 1),
    (2, 2), (2, 0), (0, 2), (0, 0), (0, 1), (0, 3), (1, 0), (3, 0),
)


def main_kernel(
    n_dp, n_item,
    neg_s_ref, q_hbm, table_hbm, state_ref, owner_ref, row_ref, neg_ref,
    grad_ref, loss_ref, table_ref, state_out,
    q_ref, neg_f, tsend, qt, req_out, req_in, negbuf, nidbuf, found, returned, outbox, inbox, acc, pos_f, g_bf, ut, tot, et, part, sib_in, by_x, by_z, in_x, in_z, mid_x, mid_z, end_x, end_z, y_out, y_in, y_sum,
    dense_f, rs_out, relay_in, rs_in, ag,
    req_s, req_r, neg_s, neg_r, nid_s, nid_r, pc_s, pc_r, pi_s, pi_r, sn_s, sn_r, si_s, si_r, pos_s, pos_r, g_s, g_r, sib_s, sib_r, hop_s, hop_r, y_s, y_r,
    rs_s, relay_r, rs_r, ag_s, ag_r, load_s, load_q,
):
    ex, width = q_ref.shape
    rows = table_ref.shape[0]
    quarter = rows // n_dp
    hq = quarter // 2
    chips = n_item // 2
    cap = 3 * ex // n_item
    neg = negbuf.shape[2]
    y, me = lax.axis_index("dp"), lax.axis_index("item")
    chip, core = me // 2, lax.rem(me, 2)
    sibling = chip * 2 + 1 - core
    up, far, down = lax.rem(y + 1, n_dp), lax.rem(y + 2, n_dp), lax.rem(y + 3, n_dp)

    def copy(src, dst, send, recv, **where):
        return pltpu.make_async_remote_copy(
            src_ref=src, dst_ref=dst, send_sem=send, recv_sem=recv, device_id=where, device_id_type=pl.DeviceIdType.MESH
        )

    def load(k):
        at = pl.ds(pl.multiple_of(k * hq, hq), hq)
        return pltpu.make_async_copy(table_hbm.at[at, :], table_ref.at[at, :], load_s)

    @pl.loop(0, 2 * n_dp)
    def _(k):
        load(k).start()

    load_queries = pltpu.make_async_copy(q_hbm, q_ref, load_q)
    load_queries.start()

    def wait_all(part, send=None, recv=None):
        c = copy(part, part, recv if send is None else send, send if recv is None else recv, item=sibling)
        if send is None:
            c.wait_recv()
        else:
            c.wait_send()

    barrier = pltpu.get_barrier_semaphore()

    @pl.loop(1, n_item)
    def _(off):
        pl.semaphore_signal(barrier, inc=1, device_id={"item": lax.rem(me + off, n_item)}, device_id_type=pl.DeviceIdType.MESH)

    @pl.loop(1, n_dp)
    def _(off):
        pl.semaphore_signal(barrier, inc=1, device_id={"dp": lax.rem(y + off, n_dp)}, device_id_type=pl.DeviceIdType.MESH)

    owner_r = owner_ref[...].astype(F32)
    row_r = row_ref[...].astype(F32)
    gid_r = owner_r * rows + row_r
    owners_r = (owner_r == iota((n_item, ex), 0)).astype(F32)
    before = (iota((LANES, LANES), 0) < iota((LANES, LANES), 1)).astype(BF)
    seen = jnp.zeros((n_item, 1), F32)
    slots = []
    for k in range(ex // LANES):
        named = owners_r[:, k * LANES : (k + 1) * LANES]
        earlier = dot(named.astype(BF), before) + seen
        slots.append(jnp.sum(earlier * named, axis=0, keepdims=True))
        seen += jnp.sum(named, axis=1, keepdims=True)
    slot_r = jnp.concatenate(slots, axis=1)
    place_r = owner_r * cap + slot_r
    high_r = jnp.floor(row_r * (1.0 / 64.0))
    low_r = row_r - 64.0 * high_r
    at_slot = slot_r == iota((LANES, ex), 0)
    both = jnp.concatenate([jnp.where(at_slot, high_r, 0.0), jnp.where(at_slot, low_r, 0.0)], axis=0).astype(BF)
    asked2 = lax.dot_general(owners_r.astype(BF), both, (((1,), (1,)), ((), ())), preferred_element_type=F32)
    asked = asked2[:, :LANES] * 64.0 + asked2[:, LANES:]
    for s in range(n_item):
        req_out[s] = asked[s : s + 1, :]

    pl.semaphore_wait(barrier, n_item - 1 + n_dp - 1)

    req_in[me] = req_out[me]

    def req_copy(peer):
        return copy(req_out.at[peer], req_in.at[me], req_s, req_r, item=peer)

    @pl.loop(1, n_item)
    def _(off):
        req_copy(lax.rem(me + off, n_item)).start()

    pltpu.make_async_copy(table_hbm, table_ref, load_s).wait()

    for k in range(neg):
        neg_f[k : k + 1, :] = table_ref[pl.ds(neg_s_ref[k], 1), :]
    t = neg_f[...]
    mine = y * 2 + core
    negbuf[mine, chip] = (t / jnp.sqrt(jnp.sum(t * t, axis=1, keepdims=True) + EPSILON)).astype(BF)
    nidbuf[mine, chip] = jnp.concatenate([neg_ref[...].astype(F32), jnp.full((1, LANES - neg), -1.0, F32)], axis=1)

    def plane_copies(peer_chip):
        to = peer_chip * 2 + core
        return (
            copy(negbuf.at[mine, chip], negbuf.at[mine, chip], neg_s, neg_r, item=to),
            copy(nidbuf.at[mine, chip], nidbuf.at[mine, chip], nid_s, nid_r, item=to),
        )

    @pl.loop(1, chips)
    def _(off):
        for c in plane_copies(lax.rem(chip + off, chips)):
            c.start()

    tile = min(512, rows)

    @pl.loop(0, rows // tile)
    def _(k):
        at = pl.ds(pl.multiple_of(k * tile, tile), tile)
        t = table_ref[at, :]
        tsend[at, :] = (t / jnp.sqrt(jnp.sum(t * t, axis=1, keepdims=True) + EPSILON)).astype(BF)

    load_queries.wait()
    q = q_ref[...].astype(F32)
    q_norm = jnp.sqrt(jnp.sum(q * q, axis=1, keepdims=True) + EPSILON)
    acc[...] = q / q_norm
    qt[...] = jnp.transpose(acc[...]).astype(BF)

    def wait_recv(dst, send, recv, **where):
        copy(dst, dst, send, recv, **where).wait_recv()

    wait_all(req_in.at[pl.ds(0, n_item - 1)], recv=req_r)

    if chips == len(OFFSETS):
        order = [lax.rem(chip // 4 + dz, 4) * 4 + lax.rem(chip + dx, 4) for dz, dx in OFFSETS]
    else:
        order = [lax.rem(chip + d, chips) for d in range(1, chips + 1)]
    mates = [2 * c + side for c in order for side in range(2)]
    batch = min(8, n_item)
    batches = [mates[k : k + batch] for k in range(0, n_item, batch)]

    def one_of(k):
        group = batches[-1]
        for n in range(len(batches) - 2, -1, -1):
            group = [jnp.where(k == n, a, b) for a, b in zip(batches[n], group)]
        return group

    own_batch = (OFFSETS.index((0, 0)) if chips == len(OFFSETS) else chips - 1) * 2 // batch

    def wait_batch(k, buffer, recv):
        @pl.when(k != own_batch)
        def _():
            wait_all(buffer.at[pl.ds(0, batch)], recv=recv.at[k])

        @pl.when(k == own_batch)
        def _():
            wait_all(buffer.at[pl.ds(0, batch - 1)], recv=recv.at[k])

    def pos_copy(peer, k):
        return copy(found.at[peer], returned.at[me], pos_s, pos_r.at[k], item=peer)

    def gather(k):
        group = one_of(k)
        ids = jnp.concatenate([row_to_col(req_in[src])[:cap] for src in group], axis=0)
        got = jnp.zeros((batch * cap, width), F32)
        for t in range(rows // tile):
            got += dot(pick_lanes(ids, float(t * tile), tile), tsend[t * tile : (t + 1) * tile, :])
        for s, src in enumerate(group):
            found[src] = got[s * cap : (s + 1) * cap].astype(BF)

            @pl.when(src != me)
            def _():
                pos_copy(src, k).start()

    @pl.loop(0, 1)
    def _(k):
        gather(k)


    wait_all(negbuf.at[mine, pl.ds(0, chips - 1)], recv=neg_r)
    wait_all(nidbuf.at[mine, pl.ds(0, chips - 1)], recv=nid_r)

    half = chips // 2

    def piece_part(d, h):
        return negbuf.at[d * 2 + core, pl.ds(h * half, half)], nidbuf.at[d * 2 + core, pl.ds(h * half, half)]

    def y_copies(d, h, dest):
        rows_part, ids_part = piece_part(d, h)
        return (
            copy(rows_part, rows_part, pc_s, pc_r.at[d, h], dp=dest),
            copy(ids_part, ids_part, pi_s, pi_r.at[d, h], dp=dest),
        )

    def y_wait(d, h, dest):
        for c in y_copies(d, h, dest):
            c.wait_recv()

    def sib_copies(d, side, h):
        piece, at = d * 2 + side, pl.ds(h * half, half)
        return (
            copy(negbuf.at[piece, at], negbuf.at[piece, at], sn_s, sn_r.at[d, h], item=sibling),
            copy(nidbuf.at[piece, at], nidbuf.at[piece, at], si_s, si_r.at[d, h], item=sibling),
        )

    def to_sibling(d, h):
        for c in sib_copies(d, core, h):
            c.start()

    def from_sibling(d, h):
        for c in sib_copies(d, 1 - core, h):
            c.wait_recv()

    def send_y(d, h, dest):
        for c in y_copies(d, h, dest):
            c.start()

    send_y(y, 0, up)
    send_y(y, 1, down)
    send_y(y, 1, up)
    send_y(y, 0, down)
    to_sibling(y, 0)
    to_sibling(y, 1)

    @pl.loop(1, len(batches))
    def _(k):
        gather(k)

    returned[me] = found[me]

    tot[...] = jnp.zeros_like(tot)

    def pass1(piece, h):
        first = h * half
        block = negbuf[piece, pl.ds(first, half)].reshape(half * neg, width)
        ids = jnp.concatenate(
            [
                row_to_col(nidbuf[piece, first + z])[:neg]
                + (((first + z) * 2 + lax.rem(piece, 2)) * rows).astype(F32)
                for z in range(half)
            ],
            axis=0,
        )
        e = jnp.where(ids != gid_r, jnp.exp2(dot(block, qt[...]) * (INV_TEMP * LOG2E)), 0.0)
        tot[...] += jnp.sum(e.reshape(half * neg // 8, 8, ex), axis=0)
        eb = e.astype(BF)
        et[piece, pl.ds(first, half)] = eb.reshape(half, neg, ex)

    from_sibling(y, 0)
    from_sibling(y, 1)

    @pl.loop(0, 4)
    def _(k):
        pass1(y * 2 + k // 2, lax.rem(k, 2))

    def near(side, first):
        @pl.loop(0, 2)
        def _(k):
            pass1(lax.rem(y + 3 - 2 * k, n_dp) * 2 + side, first + k - 2 * first * k)

    y_wait(down, 0, down)
    send_y(down, 0, up)
    to_sibling(down, 0)
    y_wait(up, 1, up)
    send_y(up, 1, down)
    to_sibling(up, 1)
    near(core, 0)
    from_sibling(down, 0)
    from_sibling(up, 1)
    near(1 - core, 0)

    y_wait(down, 1, down)
    to_sibling(down, 1)
    y_wait(up, 0, up)
    to_sibling(up, 0)
    near(core, 1)
    from_sibling(down, 1)
    from_sibling(up, 0)
    near(1 - core, 1)

    y_wait(far, 0, down)
    to_sibling(far, 0)
    y_wait(far, 1, up)
    to_sibling(far, 1)

    def pass1_far(side):
        @pl.loop(0, 2)
        def _(h):
            pass1(far * 2 + side, h)

    pass1_far(core)
    from_sibling(far, 0)
    from_sibling(far, 1)
    pass1_far(1 - core)

    place_c = row_to_col(place_r)
    pos_f[...] = jnp.zeros_like(pos_f)

    def slots_of(group):
        first = lax.broadcasted_iota(jnp.int32, (1, cap), 1)
        return jnp.concatenate([first + src * cap for src in group], axis=1).astype(F32)

    def place(first, end):
        @pl.loop(first, end)
        def _(k):
            group = one_of(k)
            wait_batch(k, returned, pos_r)
            pick = (place_c == slots_of(group)).astype(BF)
            pos_f[...] += dot(pick, jnp.concatenate([returned[src] for src in group], axis=0))

    place(0, len(batches))
    q_hat = acc[...]
    pos_e = pos_f[...]
    s_pos = INV_TEMP * jnp.sum(q_hat.astype(BF).astype(F32) * pos_e, axis=1, keepdims=True)
    neg_tot = row_to_col(jnp.sum(tot[...], axis=0, keepdims=True))
    lse = jnp.log(jnp.exp(s_pos) + neg_tot)
    loss_ref[...] = col_to_row(lse - s_pos)
    coef = jnp.exp(s_pos - lse) - 1.0
    inv_tot = jnp.exp(-lse)

    g_bf[...] = (INV_TEMP * coef * q_hat).astype(BF)

    def g_copy(peer, k):
        return copy(outbox.at[peer], inbox.at[me], g_s, g_r.at[k], item=peer)

    @pl.loop(0, len(batches))
    def _(k):
        group = one_of(k)
        wanted = jnp.concatenate([iota((cap, 1), 0) + (src * cap).astype(F32) for src in group], axis=0)
        rows_out = dot((place_r == wanted).astype(BF), g_bf[...])
        for s, src in enumerate(group):
            outbox[src] = rows_out[s * cap : (s + 1) * cap].astype(BF)

            @pl.when(src != me)
            def _():
                g_copy(src, k).start()

    inbox[me] = outbox[me]

    q_scaled = (q_hat.astype(BF).astype(F32) * (INV_TEMP * inv_tot)).astype(BF)

    def pass2(side):
        @pl.loop(0, n_dp)
        def _(d):
            for h in range(chips // half):
                at = slice(h * half, (h + 1) * half)
                p = dot(et[d * 2 + side, at].reshape(half * neg, ex), q_scaled)
                p = p.astype(BF).reshape(half, neg, width)
                for z in range(half):
                    part[side, h * half + z, pl.ds(pl.multiple_of(d * neg, neg), neg), :] = p[z]

    pass2(1 - core)
    to_sib = copy(part.at[1 - core], sib_in, sib_s, sib_r, item=sibling)
    to_sib.start()
    pass2(core)

    to_sib.wait_recv()

    side = math.isqrt(chips)
    nz, nx = (side, side) if side * side == chips else (1, chips)
    my_z, my_x = chip // nx, lax.rem(chip, nx)
    hn = n_dp * neg // 2

    @pl.loop(0, nz)
    def _(z):
        @pl.loop(0, nx)
        def _(x):
            at = z * nx + x
            both = (part[core, at].astype(F32) + sib_in[at].astype(F32)).astype(BF)
            by_x[x, z] = both[:hn]
            by_z[z, x] = both[hn:]

    def at_x(x):
        return (my_z * nx + x) * 2 + core

    def at_z(z):
        return (z * nx + my_x) * 2 + core

    def first_x(x):
        return copy(by_x.at[x], in_x.at[my_x], hop_s.at[0], hop_r.at[0], item=at_x(x))

    def first_z(z):
        return copy(by_z.at[z], in_z.at[my_z], hop_s.at[1], hop_r.at[1], item=at_z(z))

    def second_z(z):
        return copy(mid_z.at[z], end_z.at[my_z], hop_s.at[2], hop_r.at[2], item=at_z(z))

    def second_x(x):
        return copy(mid_x.at[x], end_x.at[my_x], hop_s.at[3], hop_r.at[3], item=at_x(x))

    def start_others(mine_at, count, make):
        @pl.loop(1, count)
        def _(off):
            make(lax.rem(mine_at + off, count)).start()

    def wait_others(buffer, count, **sem):
        if count > 1:
            wait_all(buffer.at[pl.ds(0, count - 1)], **sem)

    start_others(my_x, nx, first_x)
    start_others(my_z, nz, first_z)
    in_x[my_x] = by_x[my_x]
    in_z[my_z] = by_z[my_z]

    def add_to_dense(group, d, fresh):
        ids = jnp.concatenate([req_in[src][:, :cap] for src in group], axis=1)
        came = jnp.concatenate([inbox[src] for src in group], axis=0)
        at = pl.ds(pl.multiple_of(d * quarter, quarter), quarter)
        new = dot(pick_rows(ids, (d * quarter).astype(F32), quarter), came)
        if fresh:
            dense_f[at, :] = new
        else:
            dense_f[at, :] += new

    def wait_inbox(k):
        wait_all(inbox.at[pl.ds(0, batch - 1 if k == own_batch else batch)], recv=g_r.at[k])

    head, tail = batches[:-2], batches[-2:]
    for k, group in enumerate(head):
        wait_inbox(k)

        @pl.loop(0, n_dp)
        def _(d):
            add_to_dense(group, d, k == 0)

    for k in range(len(head), len(batches)):
        wait_inbox(k)

    def rs_copies():
        return (
            copy(rs_out.at[0, 0], relay_in.at[0], rs_s, relay_r.at[0], dp=up),
            copy(rs_out.at[0, 1], relay_in.at[1], rs_s, relay_r.at[1], dp=down),
            copy(rs_out.at[1, 0], rs_in.at[0, 0], rs_s, rs_r.at[0, 0], dp=up),
            copy(rs_out.at[1, 1], rs_in.at[0, 1], rs_s, rs_r.at[0, 1], dp=up),
            copy(rs_out.at[2, 0], rs_in.at[1, 0], rs_s, rs_r.at[1, 0], dp=down),
            copy(rs_out.at[2, 1], rs_in.at[1, 1], rs_s, rs_r.at[1, 1], dp=down),
        )

    def dense_part(d, h):
        return dense_f[pl.ds(pl.multiple_of(d * quarter + h * hq, hq), hq), :]

    far0, far1, up0, up1, down0, down1 = rs_copies()
    tail_group = [src for group in tail for src in group]

    @pl.loop(0, n_dp)
    def _(k):
        step_k = jnp.where(k == 0, 2, jnp.where(k == 1, 1, jnp.where(k == 2, 3, 0)))
        add_to_dense(tail_group, lax.rem(y + step_k, n_dp), not head)

        @pl.when(k == 0)
        def _():
            rs_out[0, 0] = dense_part(far, 0).astype(BF)
            far0.start()
            rs_out[0, 1] = dense_part(far, 1).astype(BF)
            far1.start()

        @pl.when(k == 1)
        def _():
            rs_out[1, 1] = dense_part(up, 1).astype(BF)
            up1.start()

        @pl.when(k == 2)
        def _():
            rs_out[2, 0] = dense_part(down, 0).astype(BF)
            down0.start()

    far0.wait_recv()
    rs_out[1, 0] = (dense_part(up, 0) + relay_in[0].astype(F32)).astype(BF)
    up0.start()
    far1.wait_recv()
    rs_out[2, 1] = (dense_part(down, 1) + relay_in[1].astype(F32)).astype(BF)
    down1.start()

    wait_others(in_x, nx, recv=hop_r.at[0])
    wait_others(in_z, nz, recv=hop_r.at[1])

    def added(buffer):
        total = buffer[0].astype(F32)
        for n in range(1, buffer.shape[0]):
            total += buffer[n].astype(F32)
        return total.astype(BF)

    mid_z[...] = added(in_x)
    mid_x[...] = added(in_z)
    start_others(my_z, nz, second_z)
    start_others(my_x, nx, second_x)
    end_z[my_z] = mid_z[my_z]
    end_x[my_x] = mid_x[my_x]

    ut[...] = jnp.zeros_like(ut)

    @pl.loop(0, 2 * n_dp)
    def _(piece):
        block = negbuf[piece].reshape(chips * neg, width)
        eb = et[piece].reshape(chips * neg, ex)
        ut[...] += lax.dot_general(block, eb, (((0,), (0,)), ((), ())), preferred_element_type=F32)

    g_q = INV_TEMP * (coef * pos_f[...] + jnp.transpose(ut[...]) * inv_tot)
    grad_ref[...] = ((g_q - acc[...] * jnp.sum(acc[...] * g_q, axis=1, keepdims=True)) / q_norm).astype(BF)

    wait_all(req_out.at[pl.ds(0, n_item - 1)], send=req_s)
    wait_all(found.at[pl.ds(0, n_item - 1)], send=pos_s)
    wait_all(outbox.at[pl.ds(0, n_item - 1)], send=g_s)
    wait_all(negbuf.at[mine, pl.ds(0, chips - 1)], send=neg_s)
    wait_all(nidbuf.at[mine, pl.ds(0, chips - 1)], send=nid_s)
    wait_all(negbuf.at[pl.ds(0, 3)], send=pc_s)
    wait_all(nidbuf.at[pl.ds(0, 3)], send=pi_s)
    wait_all(negbuf.at[pl.ds(0, n_dp)], send=sn_s)
    wait_all(nidbuf.at[pl.ds(0, n_dp)], send=si_s)
    to_sib.wait_send()
    wait_others(by_x, nx, send=hop_s.at[0])
    wait_others(by_z, nz, send=hop_s.at[1])

    wait_others(end_z, nz, recv=hop_r.at[2])
    wait_others(end_x, nx, recv=hop_r.at[3])
    sums = jnp.concatenate([added(end_z), added(end_x)], axis=0)
    for d in range(n_dp):
        y_out[d] = sums[d * neg : (d + 1) * neg]
    y_in[y] = y_out[y]

    def part_copy(dest):
        return copy(y_out.at[dest], y_in.at[y], y_s.at[0], y_r.at[0], dp=dest)

    def sum_copy(dest):
        return copy(y_sum.at[y], y_sum.at[y], y_s.at[1], y_r.at[1], dp=dest)

    start_others(y, n_dp, part_copy)

    wait_others(y_in, n_dp, recv=y_r.at[0])
    y_sum[y] = added(y_in)
    start_others(y, n_dp, sum_copy)
    up1.wait_recv()
    up0.wait_recv()
    down0.wait_recv()
    down1.wait_recv()
    for h in range(2):
        ag[y, h] = (dense_part(y, h) + rs_in[0, h].astype(F32) + rs_in[1, h].astype(F32)).astype(BF)

    def ag_copy(slot, h, dest):
        return copy(ag.at[slot, h], ag.at[slot, h], ag_s, ag_r.at[slot, h], dp=dest)

    ag_copy(y, 0, up).start()
    ag_copy(y, 1, down).start()
    ag_copy(y, 1, up).start()
    ag_copy(y, 0, down).start()
    wait_others(y_sum, n_dp, recv=y_r.at[1])
    neg_sums = y_sum[...].reshape(n_dp * neg, width)
    neg_ids = jnp.concatenate([nidbuf[d * 2 + core, chip][:, :neg] for d in range(n_dp)], axis=1)

    def step(d, h):
        first = d * quarter + h * hq
        at = pl.ds(pl.multiple_of(first, hq), hq)
        pick = (neg_ids == iota((hq, n_dp * neg), 0) + first.astype(F32)).astype(BF)
        g = ag[d, h].astype(F32) + dot(pick, neg_sums)
        t = table_ref[at, :]
        norm = jnp.sqrt(jnp.sum(t * t, axis=1, keepdims=True) + EPSILON)
        unit = t / norm
        g_row = (g - unit * jnp.sum(unit * g, axis=1, keepdims=True)) / norm
        mean = jnp.sum(g_row * g_row, axis=1, keepdims=True) * (1.0 / width)
        new = state_ref[:, at] + col_to_row(mean)
        state_out[:, at] = new
        table_ref[at, :] = t - LEARN_RATE * g_row / jnp.sqrt(row_to_col(new))

    def step_both(d):
        @pl.loop(0, 2)
        def _(h):
            step(d, h)

    step_both(y)

    wait_recv(ag.at[down, 0], ag_s, ag_r.at[down, 0], dp=down)
    ag_copy(down, 0, up).start()
    wait_recv(ag.at[up, 1], ag_s, ag_r.at[up, 1], dp=up)
    ag_copy(up, 1, down).start()

    wait_recv(ag.at[down, 1], ag_s, ag_r.at[down, 1], dp=down)
    wait_recv(ag.at[up, 0], ag_s, ag_r.at[up, 0], dp=up)

    @pl.loop(0, 2)
    def _(k):
        step_both(lax.rem(y + 1 + 2 * k, n_dp))

    wait_recv(ag.at[far, 0], ag_s, ag_r.at[far, 0], dp=down)
    wait_recv(ag.at[far, 1], ag_s, ag_r.at[far, 1], dp=up)
    step_both(far)

    wait_others(mid_z, nz, send=hop_s.at[2])
    wait_others(mid_x, nx, send=hop_s.at[3])
    wait_others(y_out, n_dp, send=y_s.at[0])
    wait_others(y_sum, n_dp, send=y_s.at[1])
    wait_all(rs_out, send=rs_s)
    wait_all(ag.at[pl.ds(0, 3)], send=ag_s)


def write_kernel(grad_v, loss_v, table_v, state_v, grad, loss, table, state, sems):
    parts = sems.shape[0] - 3
    rows = table.shape[0] // parts
    pairs = [(table_v.at[pl.ds(k * rows, rows), :], table.at[pl.ds(k * rows, rows), :]) for k in range(parts)]
    pairs += [(grad_v, grad), (state_v, state), (loss_v, loss)]
    copies = [pltpu.make_async_copy(src, dst, sems.at[k]) for k, (src, dst) in enumerate(pairs)]
    for c in copies:
        c.start()
    for c in copies:
        c.wait()


def on_device(n_dp, n_item, queries, item_table, adagrad_state, pos_owner, pos_row, neg_rows):
    ex, width = queries.shape
    rows = item_table.shape[0]
    neg = neg_rows.shape[0]
    chips = n_item // 2
    cap = 3 * ex // n_item
    quarter = rows // n_dp
    vmem, hbm = pl.BlockSpec(memory_space=pltpu.VMEM), pl.BlockSpec(memory_space=pl.ANY)
    dma = pltpu.SemaphoreType.DMA
    n_neg = 2 * n_dp * chips * neg
    n_batches = n_item // min(8, n_item)
    side = math.isqrt(chips)
    nz, nx = (side, side) if side * side == chips else (1, chips)
    hn = n_dp * neg // 2
    flops = 2 * width * (3 * n_neg * ex + 3 * n_item * cap * (rows + ex))
    grad, loss, new_table, new_state = pl.pallas_call(
        functools.partial(main_kernel, n_dp, n_item),
        out_shape=(
            pltpu.VMEM((ex, width), BF),
            pltpu.VMEM((1, ex), F32),
            pltpu.VMEM((rows, width), F32),
            pltpu.VMEM((1, rows), F32),
        ),
        in_specs=[pl.BlockSpec(memory_space=pltpu.SMEM), hbm, hbm, vmem, vmem, vmem, vmem],
        out_specs=(vmem, vmem, vmem, vmem),
        scratch_shapes=[
            pltpu.VMEM((ex, width), BF),
            pltpu.VMEM((neg, width), F32),
            pltpu.VMEM((rows, width), BF),
            pltpu.VMEM((width, ex), BF),
            pltpu.VMEM((n_item, 1, LANES), F32),
            pltpu.VMEM((n_item, 1, LANES), F32),
            pltpu.VMEM((2 * n_dp, chips, neg, width), BF),
            pltpu.VMEM((2 * n_dp, chips, 1, LANES), F32),
            pltpu.VMEM((n_item, cap, width), BF),
            pltpu.VMEM((n_item, cap, width), BF),
            pltpu.VMEM((n_item, cap, width), BF),
            pltpu.VMEM((n_item, cap, width), BF),
            pltpu.VMEM((ex, width), F32),
            pltpu.VMEM((ex, width), F32),
            pltpu.VMEM((ex, width), BF),
            pltpu.VMEM((width, ex), F32),
            pltpu.VMEM((8, ex), F32),
            pltpu.VMEM((2 * n_dp, chips, neg, ex), BF),
            pltpu.VMEM((2, chips, n_dp * neg, width), BF),
            pltpu.VMEM((chips, n_dp * neg, width), BF),
            pltpu.VMEM((nx, nz, hn, width), BF),
            pltpu.VMEM((nz, nx, hn, width), BF),
            pltpu.VMEM((nx, nz, hn, width), BF),
            pltpu.VMEM((nz, nx, hn, width), BF),
            pltpu.VMEM((nx, hn, width), BF),
            pltpu.VMEM((nz, hn, width), BF),
            pltpu.VMEM((nx, hn, width), BF),
            pltpu.VMEM((nz, hn, width), BF),
            pltpu.VMEM((n_dp, neg, width), BF),
            pltpu.VMEM((n_dp, neg, width), BF),
            pltpu.VMEM((n_dp, neg, width), BF),
            pltpu.VMEM((rows, width), F32),
            pltpu.VMEM((3, 2, quarter // 2, width), BF),
            pltpu.VMEM((2, quarter // 2, width), BF),
            pltpu.VMEM((2, 2, quarter // 2, width), BF),
            pltpu.VMEM((n_dp, 2, quarter // 2, width), BF),
            dma, dma,
            dma, dma,
            dma, dma,
            dma, dma((n_dp, 2)),
            dma, dma((n_dp, 2)),
            dma, dma((n_dp, 2)),
            dma, dma((n_dp, 2)),
            dma, dma((n_batches,)),
            dma, dma((n_batches,)),
            dma, dma,
            dma((4,)), dma((4,)),
            dma((2,)), dma((2,)),
            dma, dma((2,)), dma((2, 2)),
            dma, dma((n_dp, 2)),
            dma, dma,
        ],
        compiler_params=pltpu.CompilerParams(collective_id=0, has_side_effects=True, vmem_limit_bytes=56 * 2**20),
        cost_estimate=pl.CostEstimate(flops=flops, bytes_accessed=12 * 2**20, transcendentals=n_neg * ex),
        name="training_step",
    )(
        neg_rows, queries, item_table, adagrad_state.reshape(1, rows), pos_owner.reshape(1, ex), pos_row.reshape(1, ex),
        neg_rows.reshape(1, neg),
    )

    made = [pltpu.with_memory_space_constraint(a, pltpu.VMEM) for a in (grad, loss, new_table, new_state)]
    grad, loss, new_table, new_state = pl.pallas_call(
        write_kernel,
        out_shape=[jax.ShapeDtypeStruct(a.shape, a.dtype) for a in made],
        in_specs=[vmem] * 4,
        out_specs=[hbm] * 4,
        scratch_shapes=[dma((11,))],
        compiler_params=pltpu.CompilerParams(vmem_limit_bytes=2**20),
        name="write_results",
    )(*made)
    return grad, loss.reshape(ex), new_table, new_state.reshape(rows)


def solution(mesh):
    both = ("dp", "item")
    return jax.shard_map(
        functools.partial(on_device, mesh.shape["dp"], mesh.shape["item"]),
        mesh=mesh,
        in_specs=(P(both, None), P("item", None), P("item"), P(both, None), P(both), P(both)),
        out_specs=(P(both, None), P(both), P("item", None), P("item")),
        check_vma=False,
    )
```

```python
import functools
import math

import jax
import jax.numpy as jnp
from jax import lax
from jax.experimental import pallas as pl
from jax.experimental.pallas import tpu as pltpu
from jax.sharding import PartitionSpec as P

INV_TEMP = 20.0
LEARN_RATE = 0.05
EPSILON = 1e-06
LOG2E = 1.4426950408889634
BF, F32 = jnp.bfloat16, jnp.float32
LANES = 128


def dot(a, b):
    return jnp.dot(a, b, preferred_element_type=F32)


def iota(shape, dim):
    return lax.broadcasted_iota(jnp.int32, shape, dim).astype(F32)


def eye():
    return lax.broadcasted_iota(jnp.int32, (LANES, LANES), 0) == lax.broadcasted_iota(jnp.int32, (LANES, LANES), 1)


def row_to_col(row):
    parts = []
    for k in range(row.shape[1] // LANES):
        wide = jnp.broadcast_to(row[:, k * LANES : (k + 1) * LANES], (LANES, LANES))
        parts.append(jnp.sum(jnp.where(eye(), wide, 0.0), axis=1, keepdims=True))
    return parts[0] if len(parts) == 1 else jnp.concatenate(parts, axis=0)


def col_to_row(col):
    parts = []
    for k in range(col.shape[0] // LANES):
        wide = jnp.broadcast_to(col[k * LANES : (k + 1) * LANES], (LANES, LANES))
        parts.append(jnp.sum(jnp.where(eye(), wide, 0.0), axis=0, keepdims=True))
    return parts[0] if len(parts) == 1 else jnp.concatenate(parts, axis=1)


def pick_lanes(col, first, count):
    return (col == iota((col.shape[0], count), 1) + first).astype(BF)


def pick_rows(row, first, count):
    return (row == iota((count, row.shape[1]), 0) + first).astype(BF)


OFFSETS = (
    (1, 2), (3, 2), (2, 1), (2, 3), (1, 1), (3, 3), (1, 3), (3, 1),
    (2, 2), (2, 0), (0, 2), (0, 0), (0, 1), (0, 3), (1, 0), (3, 0),
)


def main_kernel(
    n_dp, n_item,
    neg_s_ref, q_hbm, table_hbm, state_ref, owner_ref, row_ref, neg_ref,
    grad_ref, loss_ref, table_ref, state_out,
    q_ref, neg_f, tsend, qt, req_out, req_in, negbuf, nidbuf, found, returned, outbox, inbox, acc, pos_f, g_bf, ut, tot, et, part, sib_in, by_x, by_z, in_x, in_z, mid_x, mid_z, end_x, end_z, y_out, y_in, y_sum,
    dense_f, rs_out, relay_in, rs_in, ag,
    req_s, req_r, neg_s, neg_r, nid_s, nid_r, pc_s, pc_r, pi_s, pi_r, sn_s, sn_r, si_s, si_r, pos_s, pos_r, g_s, g_r, sib_s, sib_r, hop_s, hop_r, y_s, y_r,
    rs_s, relay_r, rs_r, ag_s, ag_r, load_s, load_q,
):
    ex, width = q_ref.shape
    rows = table_ref.shape[0]
    quarter = rows // n_dp
    hq = quarter // 2
    chips = n_item // 2
    cap = 3 * ex // n_item
    neg = negbuf.shape[2]
    y, me = lax.axis_index("dp"), lax.axis_index("item")
    chip, core = me // 2, lax.rem(me, 2)
    sibling = chip * 2 + 1 - core
    up, far, down = lax.rem(y + 1, n_dp), lax.rem(y + 2, n_dp), lax.rem(y + 3, n_dp)

    def copy(src, dst, send, recv, **where):
        return pltpu.make_async_remote_copy(
            src_ref=src, dst_ref=dst, send_sem=send, recv_sem=recv, device_id=where, device_id_type=pl.DeviceIdType.MESH
        )

    def load(k):
        at = pl.ds(pl.multiple_of(k * hq, hq), hq)
        return pltpu.make_async_copy(table_hbm.at[at, :], table_ref.at[at, :], load_s)

    @pl.loop(0, 2 * n_dp)
    def _(k):
        load(k).start()

    load_queries = pltpu.make_async_copy(q_hbm, q_ref, load_q)
    load_queries.start()

    def wait_all(part, send=None, recv=None):
        c = copy(part, part, recv if send is None else send, send if recv is None else recv, item=sibling)
        if send is None:
            c.wait_recv()
        else:
            c.wait_send()

    barrier = pltpu.get_barrier_semaphore()

    @pl.loop(1, n_item)
    def _(off):
        pl.semaphore_signal(barrier, inc=1, device_id={"item": lax.rem(me + off, n_item)}, device_id_type=pl.DeviceIdType.MESH)

    @pl.loop(1, n_dp)
    def _(off):
        pl.semaphore_signal(barrier, inc=1, device_id={"dp": lax.rem(y + off, n_dp)}, device_id_type=pl.DeviceIdType.MESH)

    owner_r = owner_ref[...].astype(F32)
    row_r = row_ref[...].astype(F32)
    gid_r = owner_r * rows + row_r
    owners_r = (owner_r == iota((n_item, ex), 0)).astype(F32)
    before = (iota((LANES, LANES), 0) < iota((LANES, LANES), 1)).astype(BF)
    seen = jnp.zeros((n_item, 1), F32)
    slots = []
    for k in range(ex // LANES):
        named = owners_r[:, k * LANES : (k + 1) * LANES]
        earlier = dot(named.astype(BF), before) + seen
        slots.append(jnp.sum(earlier * named, axis=0, keepdims=True))
        seen += jnp.sum(named, axis=1, keepdims=True)
    slot_r = jnp.concatenate(slots, axis=1)
    place_r = owner_r * cap + slot_r
    high_r = jnp.floor(row_r * (1.0 / 64.0))
    low_r = row_r - 64.0 * high_r
    at_slot = slot_r == iota((LANES, ex), 0)
    both = jnp.concatenate([jnp.where(at_slot, high_r, 0.0), jnp.where(at_slot, low_r, 0.0)], axis=0).astype(BF)
    asked2 = lax.dot_general(owners_r.astype(BF), both, (((1,), (1,)), ((), ())), preferred_element_type=F32)
    asked = asked2[:, :LANES] * 64.0 + asked2[:, LANES:]
    for s in range(n_item):
        req_out[s] = asked[s : s + 1, :]

    pl.semaphore_wait(barrier, n_item - 1 + n_dp - 1)

    req_in[me] = req_out[me]

    def req_copy(peer):
        return copy(req_out.at[peer], req_in.at[me], req_s, req_r, item=peer)

    @pl.loop(1, n_item)
    def _(off):
        req_copy(lax.rem(me + off, n_item)).start()

    pltpu.make_async_copy(table_hbm, table_ref, load_s).wait()

    for k in range(neg):
        neg_f[k : k + 1, :] = table_ref[pl.ds(neg_s_ref[k], 1), :]
    t = neg_f[...]
    mine = y * 2 + core
    negbuf[mine, chip] = (t / jnp.sqrt(jnp.sum(t * t, axis=1, keepdims=True) + EPSILON)).astype(BF)
    nidbuf[mine, chip] = jnp.concatenate([neg_ref[...].astype(F32), jnp.full((1, LANES - neg), -1.0, F32)], axis=1)

    def plane_copies(peer_chip):
        to = peer_chip * 2 + core
        return (
            copy(negbuf.at[mine, chip], negbuf.at[mine, chip], neg_s, neg_r, item=to),
            copy(nidbuf.at[mine, chip], nidbuf.at[mine, chip], nid_s, nid_r, item=to),
        )

    @pl.loop(1, chips)
    def _(off):
        for c in plane_copies(lax.rem(chip + off, chips)):
            c.start()

    tile = min(512, rows)

    @pl.loop(0, rows // tile)
    def _(k):
        at = pl.ds(pl.multiple_of(k * tile, tile), tile)
        t = table_ref[at, :]
        tsend[at, :] = (t / jnp.sqrt(jnp.sum(t * t, axis=1, keepdims=True) + EPSILON)).astype(BF)

    load_queries.wait()
    q = q_ref[...].astype(F32)
    q_norm = jnp.sqrt(jnp.sum(q * q, axis=1, keepdims=True) + EPSILON)
    acc[...] = q / q_norm
    qt[...] = jnp.transpose(acc[...]).astype(BF)

    def wait_recv(dst, send, recv, **where):
        copy(dst, dst, send, recv, **where).wait_recv()

    wait_all(req_in.at[pl.ds(0, n_item - 1)], recv=req_r)

    if chips == len(OFFSETS):
        order = [lax.rem(chip // 4 + dz, 4) * 4 + lax.rem(chip + dx, 4) for dz, dx in OFFSETS]
    else:
        order = [lax.rem(chip + d, chips) for d in range(1, chips + 1)]
    mates = [2 * c + side for c in order for side in range(2)]
    batch = min(8, n_item)
    batches = [mates[k : k + batch] for k in range(0, n_item, batch)]

    def one_of(k):
        group = batches[-1]
        for n in range(len(batches) - 2, -1, -1):
            group = [jnp.where(k == n, a, b) for a, b in zip(batches[n], group)]
        return group

    own_batch = (OFFSETS.index((0, 0)) if chips == len(OFFSETS) else chips - 1) * 2 // batch

    def wait_batch(k, buffer, recv):
        @pl.when(k != own_batch)
        def _():
            wait_all(buffer.at[pl.ds(0, batch)], recv=recv.at[k])

        @pl.when(k == own_batch)
        def _():
            wait_all(buffer.at[pl.ds(0, batch - 1)], recv=recv.at[k])

    def pos_copy(peer, k):
        return copy(found.at[peer], returned.at[me], pos_s, pos_r.at[k], item=peer)

    def gather(k):
        group = one_of(k)
        ids = jnp.concatenate([row_to_col(req_in[src])[:cap] for src in group], axis=0)
        got = jnp.zeros((batch * cap, width), F32)
        for t in range(rows // tile):
            got += dot(pick_lanes(ids, float(t * tile), tile), tsend[t * tile : (t + 1) * tile, :])
        for s, src in enumerate(group):
            found[src] = got[s * cap : (s + 1) * cap].astype(BF)

            @pl.when(src != me)
            def _():
                pos_copy(src, k).start()

    @pl.loop(0, 1)
    def _(k):
        gather(k)


    wait_all(negbuf.at[mine, pl.ds(0, chips - 1)], recv=neg_r)
    wait_all(nidbuf.at[mine, pl.ds(0, chips - 1)], recv=nid_r)

    half = chips // 2

    def piece_part(d, h):
        return negbuf.at[d * 2 + core, pl.ds(h * half, half)], nidbuf.at[d * 2 + core, pl.ds(h * half, half)]

    def y_copies(d, h, dest):
        rows_part, ids_part = piece_part(d, h)
        return (
            copy(rows_part, rows_part, pc_s, pc_r.at[d, h], dp=dest),
            copy(ids_part, ids_part, pi_s, pi_r.at[d, h], dp=dest),
        )

    def y_wait(d, h, dest):
        for c in y_copies(d, h, dest):
            c.wait_recv()

    def sib_copies(d, side, h):
        piece, at = d * 2 + side, pl.ds(h * half, half)
        return (
            copy(negbuf.at[piece, at], negbuf.at[piece, at], sn_s, sn_r.at[d, h], item=sibling),
            copy(nidbuf.at[piece, at], nidbuf.at[piece, at], si_s, si_r.at[d, h], item=sibling),
        )

    def to_sibling(d, h):
        for c in sib_copies(d, core, h):
            c.start()

    def from_sibling(d, h):
        for c in sib_copies(d, 1 - core, h):
            c.wait_recv()

    def send_y(d, h, dest):
        for c in y_copies(d, h, dest):
            c.start()

    send_y(y, 0, up)
    send_y(y, 1, down)
    send_y(y, 1, up)
    send_y(y, 0, down)
    to_sibling(y, 0)
    to_sibling(y, 1)

    @pl.loop(1, len(batches))
    def _(k):
        gather(k)

    returned[me] = found[me]

    tot[...] = jnp.zeros_like(tot)

    def pass1(piece, h):
        first = h * half
        block = negbuf[piece, pl.ds(first, half)].reshape(half * neg, width)
        ids = jnp.concatenate(
            [
                row_to_col(nidbuf[piece, first + z])[:neg]
                + (((first + z) * 2 + lax.rem(piece, 2)) * rows).astype(F32)
                for z in range(half)
            ],
            axis=0,
        )
        e = jnp.where(ids != gid_r, jnp.exp2(dot(block, qt[...]) * (INV_TEMP * LOG2E)), 0.0)
        tot[...] += jnp.sum(e.reshape(half * neg // 8, 8, ex), axis=0)
        eb = e.astype(BF)
        et[piece, pl.ds(first, half)] = eb.reshape(half, neg, ex)

    from_sibling(y, 0)
    from_sibling(y, 1)

    @pl.loop(0, 4)
    def _(k):
        pass1(y * 2 + k // 2, lax.rem(k, 2))

    def near(side, first):
        @pl.loop(0, 2)
        def _(k):
            pass1(lax.rem(y + 3 - 2 * k, n_dp) * 2 + side, first + k - 2 * first * k)

    y_wait(down, 0, down)
    send_y(down, 0, up)
    to_sibling(down, 0)
    y_wait(up, 1, up)
    send_y(up, 1, down)
    to_sibling(up, 1)
    near(core, 0)
    from_sibling(down, 0)
    from_sibling(up, 1)
    near(1 - core, 0)

    y_wait(down, 1, down)
    to_sibling(down, 1)
    y_wait(up, 0, up)
    to_sibling(up, 0)
    near(core, 1)
    from_sibling(down, 1)
    from_sibling(up, 0)
    near(1 - core, 1)

    y_wait(far, 0, down)
    to_sibling(far, 0)
    y_wait(far, 1, up)
    to_sibling(far, 1)

    def pass1_far(side):
        @pl.loop(0, 2)
        def _(h):
            pass1(far * 2 + side, h)

    pass1_far(core)
    from_sibling(far, 0)
    from_sibling(far, 1)
    pass1_far(1 - core)

    place_c = row_to_col(place_r)
    pos_f[...] = jnp.zeros_like(pos_f)

    def slots_of(group):
        first = lax.broadcasted_iota(jnp.int32, (1, cap), 1)
        return jnp.concatenate([first + src * cap for src in group], axis=1).astype(F32)

    def place(first, end):
        @pl.loop(first, end)
        def _(k):
            group = one_of(k)
            wait_batch(k, returned, pos_r)
            pick = (place_c == slots_of(group)).astype(BF)
            pos_f[...] += dot(pick, jnp.concatenate([returned[src] for src in group], axis=0))

    place(0, len(batches))
    q_hat = acc[...]
    pos_e = pos_f[...]
    s_pos = INV_TEMP * jnp.sum(q_hat.astype(BF).astype(F32) * pos_e, axis=1, keepdims=True)
    neg_tot = row_to_col(jnp.sum(tot[...], axis=0, keepdims=True))
    lse = jnp.log(jnp.exp(s_pos) + neg_tot)
    loss_ref[...] = col_to_row(lse - s_pos)
    coef = jnp.exp(s_pos - lse) - 1.0
    inv_tot = jnp.exp(-lse)

    fw = width // 2
    g_bf[...] = (INV_TEMP * coef * q_hat).astype(BF)

    def g_copy(f, peer, k):
        return copy(outbox.at[f, peer], inbox.at[f, me], g_s.at[f], g_r.at[f, k], item=peer)

    @pl.loop(0, len(batches))
    def _(k):
        group = one_of(k)
        wanted = jnp.concatenate([iota((cap, 1), 0) + (src * cap).astype(F32) for src in group], axis=0)
        rows_out = dot((place_r == wanted).astype(BF), g_bf[...])
        for s, src in enumerate(group):
            for f in range(2):
                outbox[f, src] = rows_out[s * cap : (s + 1) * cap, f * fw : (f + 1) * fw].astype(BF)

            @pl.when(src != me)
            def _():
                g_copy(0, src, k).start()

    @pl.loop(0, len(batches))
    def _(k):
        for src in one_of(k):

            @pl.when(src != me)
            def _():
                g_copy(1, src, k).start()

    inbox[0, me] = outbox[0, me]
    inbox[1, me] = outbox[1, me]

    q_scaled = (q_hat.astype(BF).astype(F32) * (INV_TEMP * inv_tot)).astype(BF)

    def pass2(side):
        @pl.loop(0, n_dp)
        def _(d):
            for h in range(chips // half):
                at = slice(h * half, (h + 1) * half)
                p = dot(et[d * 2 + side, at].reshape(half * neg, ex), q_scaled)
                p = p.astype(BF).reshape(half, neg, width)
                for z in range(half):
                    part[side, h * half + z, pl.ds(pl.multiple_of(d * neg, neg), neg), :] = p[z]

    pass2(1 - core)
    to_sib = copy(part.at[1 - core], sib_in, sib_s, sib_r, item=sibling)
    to_sib.start()
    pass2(core)

    to_sib.wait_recv()

    side = math.isqrt(chips)
    nz, nx = (side, side) if side * side == chips else (1, chips)
    my_z, my_x = chip // nx, lax.rem(chip, nx)
    hn = n_dp * neg // 2

    @pl.loop(0, nz)
    def _(z):
        @pl.loop(0, nx)
        def _(x):
            at = z * nx + x
            both = (part[core, at].astype(F32) + sib_in[at].astype(F32)).astype(BF)
            by_x[x, z] = both[:hn]
            by_z[z, x] = both[hn:]

    def at_x(x):
        return (my_z * nx + x) * 2 + core

    def at_z(z):
        return (z * nx + my_x) * 2 + core

    def first_x(x):
        return copy(by_x.at[x], in_x.at[my_x], hop_s.at[0], hop_r.at[0], item=at_x(x))

    def first_z(z):
        return copy(by_z.at[z], in_z.at[my_z], hop_s.at[1], hop_r.at[1], item=at_z(z))

    def second_z(z):
        return copy(mid_z.at[z], end_z.at[my_z], hop_s.at[2], hop_r.at[2], item=at_z(z))

    def second_x(x):
        return copy(mid_x.at[x], end_x.at[my_x], hop_s.at[3], hop_r.at[3], item=at_x(x))

    def start_others(mine_at, count, make):
        @pl.loop(1, count)
        def _(off):
            make(lax.rem(mine_at + off, count)).start()

    def wait_others(buffer, count, **sem):
        if count > 1:
            wait_all(buffer.at[pl.ds(0, count - 1)], **sem)

    start_others(my_x, nx, first_x)
    start_others(my_z, nz, first_z)
    in_x[my_x] = by_x[my_x]
    in_z[my_z] = by_z[my_z]

    def wait_inbox(f):
        for k in range(len(batches)):
            wait_all(inbox.at[f, pl.ds(0, batch - 1 if k == own_batch else batch)], recv=g_r.at[f, k])

    def quarter_sum(f, d):
        total = jnp.zeros((quarter, fw), F32)
        for k in range(0, n_item, batch):
            ids = jnp.concatenate([req_in[src][:, :cap] for src in range(k, k + batch)], axis=1)
            came = inbox[f, k : k + batch].reshape(batch * cap, fw)
            total += dot(pick_rows(ids, (d * quarter).astype(F32), quarter), came)
        dense_f[f, pl.ds(pl.multiple_of(d * quarter, quarter), quarter), :] = total

    def rs_copy(f, block, h):
        if block == 0:
            return copy(rs_out.at[f, 0, h], relay_in.at[f, h], rs_s, relay_r.at[f, h], dp=(up, down)[h])
        return copy(rs_out.at[f, block, h], rs_in.at[f, block - 1, h], rs_s, rs_r.at[f, block - 1, h], dp=(up, down)[block - 1])

    def dense_part(f, d, h):
        return dense_f[f, pl.ds(pl.multiple_of(d * quarter + h * hq, hq), hq), :]

    def sum_and_send(f):
        @pl.loop(0, n_dp)
        def _(k):
            step_k = jnp.where(k == 0, 2, jnp.where(k == 1, 1, jnp.where(k == 2, 3, 0)))
            quarter_sum(f, lax.rem(y + step_k, n_dp))

            @pl.when(k == 0)
            def _():
                rs_out[f, 0, 0] = dense_part(f, far, 0).astype(BF)
                rs_copy(f, 0, 0).start()
                rs_out[f, 0, 1] = dense_part(f, far, 1).astype(BF)
                rs_copy(f, 0, 1).start()

            @pl.when(k == 1)
            def _():
                rs_out[f, 1, 1] = dense_part(f, up, 1).astype(BF)
                rs_copy(f, 1, 1).start()

            @pl.when(k == 2)
            def _():
                rs_out[f, 2, 0] = dense_part(f, down, 0).astype(BF)
                rs_copy(f, 2, 0).start()

    def relay(f):
        rs_copy(f, 0, 0).wait_recv()
        rs_out[f, 1, 0] = (dense_part(f, up, 0) + relay_in[f, 0].astype(F32)).astype(BF)
        rs_copy(f, 1, 0).start()
        rs_copy(f, 0, 1).wait_recv()
        rs_out[f, 2, 1] = (dense_part(f, down, 1) + relay_in[f, 1].astype(F32)).astype(BF)
        rs_copy(f, 2, 1).start()

    wait_inbox(0)
    sum_and_send(0)
    relay(0)
    wait_inbox(1)
    sum_and_send(1)
    relay(1)

    wait_others(in_x, nx, recv=hop_r.at[0])
    wait_others(in_z, nz, recv=hop_r.at[1])

    def added(buffer):
        total = buffer[0].astype(F32)
        for n in range(1, buffer.shape[0]):
            total += buffer[n].astype(F32)
        return total.astype(BF)

    mid_z[...] = added(in_x)
    mid_x[...] = added(in_z)
    start_others(my_z, nz, second_z)
    start_others(my_x, nx, second_x)
    end_z[my_z] = mid_z[my_z]
    end_x[my_x] = mid_x[my_x]

    wait_all(req_out.at[pl.ds(0, n_item - 1)], send=req_s)
    wait_all(found.at[pl.ds(0, n_item - 1)], send=pos_s)
    for f in range(2):
        wait_all(outbox.at[f, pl.ds(0, n_item - 1)], send=g_s.at[f])
    wait_all(negbuf.at[mine, pl.ds(0, chips - 1)], send=neg_s)
    wait_all(nidbuf.at[mine, pl.ds(0, chips - 1)], send=nid_s)
    wait_all(negbuf.at[pl.ds(0, 3)], send=pc_s)
    wait_all(nidbuf.at[pl.ds(0, 3)], send=pi_s)
    wait_all(negbuf.at[pl.ds(0, n_dp)], send=sn_s)
    wait_all(nidbuf.at[pl.ds(0, n_dp)], send=si_s)
    to_sib.wait_send()
    wait_others(by_x, nx, send=hop_s.at[0])
    wait_others(by_z, nz, send=hop_s.at[1])

    for f in range(2):
        for block in (1, 2):
            for h in range(2):
                rs_copy(f, block, h).wait_recv()
    for h in range(2):
        both = [dense_part(f, y, h) + rs_in[f, 0, h].astype(F32) + rs_in[f, 1, h].astype(F32) for f in range(2)]
        ag[y, h] = jnp.concatenate(both, axis=1).astype(BF)

    def ag_copy(slot, h, dest):
        return copy(ag.at[slot, h], ag.at[slot, h], ag_s, ag_r.at[slot, h], dp=dest)

    ag_copy(y, 0, up).start()
    ag_copy(y, 1, down).start()

    wait_others(end_z, nz, recv=hop_r.at[2])
    wait_others(end_x, nx, recv=hop_r.at[3])
    sums = jnp.concatenate([added(end_z), added(end_x)], axis=0)
    for d in range(n_dp):
        y_out[d] = sums[d * neg : (d + 1) * neg]
    y_in[y] = y_out[y]

    def part_copy(dest):
        return copy(y_out.at[dest], y_in.at[y], y_s.at[0], y_r.at[0], dp=dest)

    def sum_copy(dest):
        return copy(y_sum.at[y], y_sum.at[y], y_s.at[1], y_r.at[1], dp=dest)

    start_others(y, n_dp, part_copy)

    ag_copy(y, 1, up).start()
    ag_copy(y, 0, down).start()

    wait_others(y_in, n_dp, recv=y_r.at[0])
    y_sum[y] = added(y_in)
    start_others(y, n_dp, sum_copy)

    wait_recv(ag.at[down, 0], ag_s, ag_r.at[down, 0], dp=down)
    ag_copy(down, 0, up).start()
    wait_recv(ag.at[up, 1], ag_s, ag_r.at[up, 1], dp=up)
    ag_copy(up, 1, down).start()

    ut[...] = jnp.zeros_like(ut)

    @pl.loop(0, 2 * n_dp)
    def _(piece):
        block = negbuf[piece].reshape(chips * neg, width)
        eb = et[piece].reshape(chips * neg, ex)
        ut[...] += lax.dot_general(block, eb, (((0,), (0,)), ((), ())), preferred_element_type=F32)

    g_q = INV_TEMP * (coef * pos_f[...] + jnp.transpose(ut[...]) * inv_tot)
    grad_ref[...] = ((g_q - acc[...] * jnp.sum(acc[...] * g_q, axis=1, keepdims=True)) / q_norm).astype(BF)

    wait_others(y_sum, n_dp, recv=y_r.at[1])
    neg_sums = y_sum[...].reshape(n_dp * neg, width)
    neg_ids = jnp.concatenate([nidbuf[d * 2 + core, chip][:, :neg] for d in range(n_dp)], axis=1)

    def step(d, h):
        first = d * quarter + h * hq
        at = pl.ds(pl.multiple_of(first, hq), hq)
        pick = (neg_ids == iota((hq, n_dp * neg), 0) + first.astype(F32)).astype(BF)
        g = ag[d, h].astype(F32) + dot(pick, neg_sums)
        t = table_ref[at, :]
        norm = jnp.sqrt(jnp.sum(t * t, axis=1, keepdims=True) + EPSILON)
        unit = t / norm
        g_row = (g - unit * jnp.sum(unit * g, axis=1, keepdims=True)) / norm
        mean = jnp.sum(g_row * g_row, axis=1, keepdims=True) * (1.0 / width)
        new = state_ref[:, at] + col_to_row(mean)
        state_out[:, at] = new
        table_ref[at, :] = t - LEARN_RATE * g_row / jnp.sqrt(row_to_col(new))

    def step_both(d):
        @pl.loop(0, 2)
        def _(h):
            step(d, h)

    step_both(y)

    wait_recv(ag.at[down, 1], ag_s, ag_r.at[down, 1], dp=down)
    wait_recv(ag.at[up, 0], ag_s, ag_r.at[up, 0], dp=up)

    @pl.loop(0, 2)
    def _(k):
        step_both(lax.rem(y + 1 + 2 * k, n_dp))

    wait_recv(ag.at[far, 0], ag_s, ag_r.at[far, 0], dp=down)
    wait_recv(ag.at[far, 1], ag_s, ag_r.at[far, 1], dp=up)
    step_both(far)

    wait_others(mid_z, nz, send=hop_s.at[2])
    wait_others(mid_x, nx, send=hop_s.at[3])
    wait_others(y_out, n_dp, send=y_s.at[0])
    wait_others(y_sum, n_dp, send=y_s.at[1])
    wait_all(rs_out, send=rs_s)
    wait_all(ag.at[pl.ds(0, 3)], send=ag_s)


def write_kernel(grad_v, loss_v, table_v, state_v, grad, loss, table, state, sems):
    parts = sems.shape[0] - 3
    rows = table.shape[0] // parts
    pairs = [(table_v.at[pl.ds(k * rows, rows), :], table.at[pl.ds(k * rows, rows), :]) for k in range(parts)]
    pairs += [(grad_v, grad), (state_v, state), (loss_v, loss)]
    copies = [pltpu.make_async_copy(src, dst, sems.at[k]) for k, (src, dst) in enumerate(pairs)]
    for c in copies:
        c.start()
    for c in copies:
        c.wait()


def on_device(n_dp, n_item, queries, item_table, adagrad_state, pos_owner, pos_row, neg_rows):
    ex, width = queries.shape
    rows = item_table.shape[0]
    neg = neg_rows.shape[0]
    chips = n_item // 2
    cap = 3 * ex // n_item
    quarter = rows // n_dp
    vmem, hbm = pl.BlockSpec(memory_space=pltpu.VMEM), pl.BlockSpec(memory_space=pl.ANY)
    dma = pltpu.SemaphoreType.DMA
    n_neg = 2 * n_dp * chips * neg
    n_batches = n_item // min(8, n_item)
    side = math.isqrt(chips)
    nz, nx = (side, side) if side * side == chips else (1, chips)
    hn = n_dp * neg // 2
    flops = 2 * width * (3 * n_neg * ex + 3 * n_item * cap * (rows + ex))
    grad, loss, new_table, new_state = pl.pallas_call(
        functools.partial(main_kernel, n_dp, n_item),
        out_shape=(
            pltpu.VMEM((ex, width), BF),
            pltpu.VMEM((1, ex), F32),
            pltpu.VMEM((rows, width), F32),
            pltpu.VMEM((1, rows), F32),
        ),
        in_specs=[pl.BlockSpec(memory_space=pltpu.SMEM), hbm, hbm, vmem, vmem, vmem, vmem],
        out_specs=(vmem, vmem, vmem, vmem),
        scratch_shapes=[
            pltpu.VMEM((ex, width), BF),
            pltpu.VMEM((neg, width), F32),
            pltpu.VMEM((rows, width), BF),
            pltpu.VMEM((width, ex), BF),
            pltpu.VMEM((n_item, 1, LANES), F32),
            pltpu.VMEM((n_item, 1, LANES), F32),
            pltpu.VMEM((2 * n_dp, chips, neg, width), BF),
            pltpu.VMEM((2 * n_dp, chips, 1, LANES), F32),
            pltpu.VMEM((n_item, cap, width), BF),
            pltpu.VMEM((n_item, cap, width), BF),
            pltpu.VMEM((2, n_item, cap, width // 2), BF),
            pltpu.VMEM((2, n_item, cap, width // 2), BF),
            pltpu.VMEM((ex, width), F32),
            pltpu.VMEM((ex, width), F32),
            pltpu.VMEM((ex, width), BF),
            pltpu.VMEM((width, ex), F32),
            pltpu.VMEM((8, ex), F32),
            pltpu.VMEM((2 * n_dp, chips, neg, ex), BF),
            pltpu.VMEM((2, chips, n_dp * neg, width), BF),
            pltpu.VMEM((chips, n_dp * neg, width), BF),
            pltpu.VMEM((nx, nz, hn, width), BF),
            pltpu.VMEM((nz, nx, hn, width), BF),
            pltpu.VMEM((nx, nz, hn, width), BF),
            pltpu.VMEM((nz, nx, hn, width), BF),
            pltpu.VMEM((nx, hn, width), BF),
            pltpu.VMEM((nz, hn, width), BF),
            pltpu.VMEM((nx, hn, width), BF),
            pltpu.VMEM((nz, hn, width), BF),
            pltpu.VMEM((n_dp, neg, width), BF),
            pltpu.VMEM((n_dp, neg, width), BF),
            pltpu.VMEM((n_dp, neg, width), BF),
            pltpu.VMEM((2, rows, width // 2), F32),
            pltpu.VMEM((2, 3, 2, quarter // 2, width // 2), BF),
            pltpu.VMEM((2, 2, quarter // 2, width // 2), BF),
            pltpu.VMEM((2, 2, 2, quarter // 2, width // 2), BF),
            pltpu.VMEM((n_dp, 2, quarter // 2, width), BF),
            dma, dma,
            dma, dma,
            dma, dma,
            dma, dma((n_dp, 2)),
            dma, dma((n_dp, 2)),
            dma, dma((n_dp, 2)),
            dma, dma((n_dp, 2)),
            dma, dma((n_batches,)),
            dma((2,)), dma((2, n_batches)),
            dma, dma,
            dma((4,)), dma((4,)),
            dma((2,)), dma((2,)),
            dma, dma((2, 2)), dma((2, 2, 2)),
            dma, dma((n_dp, 2)),
            dma, dma,
        ],
        compiler_params=pltpu.CompilerParams(collective_id=0, has_side_effects=True, vmem_limit_bytes=56 * 2**20),
        cost_estimate=pl.CostEstimate(flops=flops, bytes_accessed=12 * 2**20, transcendentals=n_neg * ex),
        name="training_step",
    )(
        neg_rows, queries, item_table, adagrad_state.reshape(1, rows), pos_owner.reshape(1, ex), pos_row.reshape(1, ex),
        neg_rows.reshape(1, neg),
    )

    made = [pltpu.with_memory_space_constraint(a, pltpu.VMEM) for a in (grad, loss, new_table, new_state)]
    grad, loss, new_table, new_state = pl.pallas_call(
        write_kernel,
        out_shape=[jax.ShapeDtypeStruct(a.shape, a.dtype) for a in made],
        in_specs=[vmem] * 4,
        out_specs=[hbm] * 4,
        scratch_shapes=[dma((11,))],
        compiler_params=pltpu.CompilerParams(vmem_limit_bytes=2**20),
        name="write_results",
    )(*made)
    return grad, loss.reshape(ex), new_table, new_state.reshape(rows)


def solution(mesh):
    both = ("dp", "item")
    return jax.shard_map(
        functools.partial(on_device, mesh.shape["dp"], mesh.shape["item"]),
        mesh=mesh,
        in_specs=(P(both, None), P("item", None), P("item"), P(both, None), P(both), P(both)),
        out_specs=(P(both, None), P(both), P("item", None), P("item")),
        check_vma=False,
    )
```

```python
import functools
import math

import jax
import jax.numpy as jnp
from jax import lax
from jax.experimental import pallas as pl
from jax.experimental.pallas import tpu as pltpu
from jax.sharding import PartitionSpec as P

INV_TEMP = 20.0
LEARN_RATE = 0.05
EPSILON = 1e-06
LOG2E = 1.4426950408889634
BF, F32 = jnp.bfloat16, jnp.float32
LANES = 128


def dot(a, b):
    return jnp.dot(a, b, preferred_element_type=F32)


def iota(shape, dim):
    return lax.broadcasted_iota(jnp.int32, shape, dim).astype(F32)


def eye():
    return lax.broadcasted_iota(jnp.int32, (LANES, LANES), 0) == lax.broadcasted_iota(jnp.int32, (LANES, LANES), 1)


def row_to_col(row):
    parts = []
    for k in range(row.shape[1] // LANES):
        wide = jnp.broadcast_to(row[:, k * LANES : (k + 1) * LANES], (LANES, LANES))
        parts.append(jnp.sum(jnp.where(eye(), wide, 0.0), axis=1, keepdims=True))
    return parts[0] if len(parts) == 1 else jnp.concatenate(parts, axis=0)


def col_to_row(col):
    parts = []
    for k in range(col.shape[0] // LANES):
        wide = jnp.broadcast_to(col[k * LANES : (k + 1) * LANES], (LANES, LANES))
        parts.append(jnp.sum(jnp.where(eye(), wide, 0.0), axis=0, keepdims=True))
    return parts[0] if len(parts) == 1 else jnp.concatenate(parts, axis=1)


def pick_lanes(col, first, count):
    return (col == iota((col.shape[0], count), 1) + first).astype(BF)


def pick_rows(row, first, count):
    return (row == iota((count, row.shape[1]), 0) + first).astype(BF)


OFFSETS = (
    (1, 2), (3, 2), (2, 1), (2, 3), (1, 1), (3, 3), (1, 3), (3, 1),
    (2, 2), (2, 0), (0, 2), (0, 0), (0, 1), (0, 3), (1, 0), (3, 0),
)


def main_kernel(
    n_dp, n_item,
    neg_s_ref, q_hbm, table_hbm, state_ref, owner_ref, row_ref, neg_ref,
    grad_ref, loss_ref, table_ref, state_out,
    q_ref, neg_f, tsend, qt, req_out, req_in, negbuf, nidbuf, found, returned, outbox, inbox, acc, pos_f, g_bf, ut, tot, et, part, sib_in, by_x, by_z, in_x, in_z, mid_x, mid_z, end_x, end_z, y_out, y_in, y_sum,
    dense_f, rs_out, relay_in, rs_in, ag,
    req_s, req_r, neg_s, neg_r, nid_s, nid_r, pc_s, pc_r, pi_s, pi_r, sn_s, sn_r, si_s, si_r, pos_s, pos_r, g_s, g_r, sib_s, sib_r, hop_s, hop_r, y_s, y_r,
    rs_s, relay_r, rs_r, ag_s, ag_r, load_s, load_q,
):
    ex, width = q_ref.shape
    rows = table_ref.shape[0]
    quarter = rows // n_dp
    hq = quarter // 2
    chips = n_item // 2
    cap = 3 * ex // n_item
    neg = negbuf.shape[2]
    y, me = lax.axis_index("dp"), lax.axis_index("item")
    chip, core = me // 2, lax.rem(me, 2)
    sibling = chip * 2 + 1 - core
    up, far, down = lax.rem(y + 1, n_dp), lax.rem(y + 2, n_dp), lax.rem(y + 3, n_dp)

    def copy(src, dst, send, recv, **where):
        return pltpu.make_async_remote_copy(
            src_ref=src, dst_ref=dst, send_sem=send, recv_sem=recv, device_id=where, device_id_type=pl.DeviceIdType.MESH
        )

    def load(k):
        at = pl.ds(pl.multiple_of(k * hq, hq), hq)
        return pltpu.make_async_copy(table_hbm.at[at, :], table_ref.at[at, :], load_s)

    @pl.loop(0, 2 * n_dp)
    def _(k):
        load(k).start()

    load_queries = pltpu.make_async_copy(q_hbm, q_ref, load_q)
    load_queries.start()

    def wait_all(part, send=None, recv=None):
        c = copy(part, part, recv if send is None else send, send if recv is None else recv, item=sibling)
        if send is None:
            c.wait_recv()
        else:
            c.wait_send()

    barrier = pltpu.get_barrier_semaphore()

    @pl.loop(1, n_item)
    def _(off):
        pl.semaphore_signal(barrier, inc=1, device_id={"item": lax.rem(me + off, n_item)}, device_id_type=pl.DeviceIdType.MESH)

    @pl.loop(1, n_dp)
    def _(off):
        pl.semaphore_signal(barrier, inc=1, device_id={"dp": lax.rem(y + off, n_dp)}, device_id_type=pl.DeviceIdType.MESH)

    owner_r = owner_ref[...].astype(F32)
    row_r = row_ref[...].astype(F32)
    gid_r = owner_r * rows + row_r
    owners_r = (owner_r == iota((n_item, ex), 0)).astype(F32)
    before = (iota((LANES, LANES), 0) < iota((LANES, LANES), 1)).astype(BF)
    seen = jnp.zeros((n_item, 1), F32)
    slots = []
    for k in range(ex // LANES):
        named = owners_r[:, k * LANES : (k + 1) * LANES]
        earlier = dot(named.astype(BF), before) + seen
        slots.append(jnp.sum(earlier * named, axis=0, keepdims=True))
        seen += jnp.sum(named, axis=1, keepdims=True)
    slot_r = jnp.concatenate(slots, axis=1)
    place_r = owner_r * cap + slot_r
    high_r = jnp.floor(row_r * (1.0 / 64.0))
    low_r = row_r - 64.0 * high_r
    at_slot = slot_r == iota((LANES, ex), 0)
    both = jnp.concatenate([jnp.where(at_slot, high_r, 0.0), jnp.where(at_slot, low_r, 0.0)], axis=0).astype(BF)
    asked2 = lax.dot_general(owners_r.astype(BF), both, (((1,), (1,)), ((), ())), preferred_element_type=F32)
    asked = asked2[:, :LANES] * 64.0 + asked2[:, LANES:]
    for s in range(n_item):
        req_out[s] = asked[s : s + 1, :]

    pl.semaphore_wait(barrier, n_item - 1 + n_dp - 1)

    req_in[me] = req_out[me]

    def req_copy(peer):
        return copy(req_out.at[peer], req_in.at[me], req_s, req_r, item=peer)

    @pl.loop(1, n_item)
    def _(off):
        req_copy(lax.rem(me + off, n_item)).start()

    pltpu.make_async_copy(table_hbm, table_ref, load_s).wait()

    for k in range(neg):
        neg_f[k : k + 1, :] = table_ref[pl.ds(neg_s_ref[k], 1), :]
    t = neg_f[...]
    mine = y * 2 + core
    negbuf[mine, chip] = (t / jnp.sqrt(jnp.sum(t * t, axis=1, keepdims=True) + EPSILON)).astype(BF)
    nidbuf[mine, chip] = jnp.concatenate([neg_ref[...].astype(F32), jnp.full((1, LANES - neg), -1.0, F32)], axis=1)

    def plane_copies(peer_chip):
        to = peer_chip * 2 + core
        return (
            copy(negbuf.at[mine, chip], negbuf.at[mine, chip], neg_s, neg_r, item=to),
            copy(nidbuf.at[mine, chip], nidbuf.at[mine, chip], nid_s, nid_r, item=to),
        )

    @pl.loop(1, chips)
    def _(off):
        for c in plane_copies(lax.rem(chip + off, chips)):
            c.start()

    tile = min(512, rows)

    @pl.loop(0, rows // tile)
    def _(k):
        at = pl.ds(pl.multiple_of(k * tile, tile), tile)
        t = table_ref[at, :]
        tsend[at, :] = (t / jnp.sqrt(jnp.sum(t * t, axis=1, keepdims=True) + EPSILON)).astype(BF)

    load_queries.wait()
    q = q_ref[...].astype(F32)
    q_norm = jnp.sqrt(jnp.sum(q * q, axis=1, keepdims=True) + EPSILON)
    acc[...] = q / q_norm
    qt[...] = jnp.transpose(acc[...]).astype(BF)

    def wait_recv(dst, send, recv, **where):
        copy(dst, dst, send, recv, **where).wait_recv()

    wait_all(req_in.at[pl.ds(0, n_item - 1)], recv=req_r)

    if chips == len(OFFSETS):
        order = [lax.rem(chip // 4 + dz, 4) * 4 + lax.rem(chip + dx, 4) for dz, dx in OFFSETS]
    else:
        order = [lax.rem(chip + d, chips) for d in range(1, chips + 1)]
    mates = [2 * c + side for c in order for side in range(2)]
    batch = min(8, n_item)
    batches = [mates[k : k + batch] for k in range(0, n_item, batch)]

    def one_of(k):
        group = batches[-1]
        for n in range(len(batches) - 2, -1, -1):
            group = [jnp.where(k == n, a, b) for a, b in zip(batches[n], group)]
        return group

    own_batch = (OFFSETS.index((0, 0)) if chips == len(OFFSETS) else chips - 1) * 2 // batch

    def wait_batch(k, buffer, recv):
        @pl.when(k != own_batch)
        def _():
            wait_all(buffer.at[pl.ds(0, batch)], recv=recv.at[k])

        @pl.when(k == own_batch)
        def _():
            wait_all(buffer.at[pl.ds(0, batch - 1)], recv=recv.at[k])

    def pos_copy(peer, k):
        return copy(found.at[peer], returned.at[me], pos_s, pos_r.at[k], item=peer)

    def gather(k):
        group = one_of(k)
        ids = jnp.concatenate([row_to_col(req_in[src])[:cap] for src in group], axis=0)
        got = jnp.zeros((batch * cap, width), F32)
        for t in range(rows // tile):
            got += dot(pick_lanes(ids, float(t * tile), tile), tsend[t * tile : (t + 1) * tile, :])
        for s, src in enumerate(group):
            found[src] = got[s * cap : (s + 1) * cap].astype(BF)

            @pl.when(src != me)
            def _():
                pos_copy(src, k).start()

    @pl.loop(0, 1)
    def _(k):
        gather(k)


    wait_all(negbuf.at[mine, pl.ds(0, chips - 1)], recv=neg_r)
    wait_all(nidbuf.at[mine, pl.ds(0, chips - 1)], recv=nid_r)

    half = chips // 2

    def piece_part(d, h):
        return negbuf.at[d * 2 + core, pl.ds(h * half, half)], nidbuf.at[d * 2 + core, pl.ds(h * half, half)]

    def y_copies(d, h, dest):
        rows_part, ids_part = piece_part(d, h)
        return (
            copy(rows_part, rows_part, pc_s, pc_r.at[d, h], dp=dest),
            copy(ids_part, ids_part, pi_s, pi_r.at[d, h], dp=dest),
        )

    def y_wait(d, h, dest):
        for c in y_copies(d, h, dest):
            c.wait_recv()

    def sib_copies(d, side, h):
        piece, at = d * 2 + side, pl.ds(h * half, half)
        return (
            copy(negbuf.at[piece, at], negbuf.at[piece, at], sn_s, sn_r.at[d, h], item=sibling),
            copy(nidbuf.at[piece, at], nidbuf.at[piece, at], si_s, si_r.at[d, h], item=sibling),
        )

    def to_sibling(d, h):
        for c in sib_copies(d, core, h):
            c.start()

    def from_sibling(d, h):
        for c in sib_copies(d, 1 - core, h):
            c.wait_recv()

    def send_y(d, h, dest):
        for c in y_copies(d, h, dest):
            c.start()

    send_y(y, 0, up)
    send_y(y, 1, down)
    send_y(y, 1, up)
    send_y(y, 0, down)
    to_sibling(y, 0)
    to_sibling(y, 1)

    @pl.loop(1, len(batches))
    def _(k):
        gather(k)

    returned[me] = found[me]

    tot[...] = jnp.zeros_like(tot)

    def pass1(piece, h):
        first = h * half
        block = negbuf[piece, pl.ds(first, half)].reshape(half * neg, width)
        ids = jnp.concatenate(
            [
                row_to_col(nidbuf[piece, first + z])[:neg]
                + (((first + z) * 2 + lax.rem(piece, 2)) * rows).astype(F32)
                for z in range(half)
            ],
            axis=0,
        )
        e = jnp.where(ids != gid_r, jnp.exp2(dot(block, qt[...]) * (INV_TEMP * LOG2E)), 0.0)
        tot[...] += jnp.sum(e.reshape(half * neg // 8, 8, ex), axis=0)
        eb = e.astype(BF)
        et[piece, pl.ds(first, half)] = eb.reshape(half, neg, ex)

    from_sibling(y, 0)
    from_sibling(y, 1)

    @pl.loop(0, 4)
    def _(k):
        pass1(y * 2 + k // 2, lax.rem(k, 2))

    def near(side, first):
        @pl.loop(0, 2)
        def _(k):
            pass1(lax.rem(y + 3 - 2 * k, n_dp) * 2 + side, first + k - 2 * first * k)

    y_wait(down, 0, down)
    send_y(down, 0, up)
    to_sibling(down, 0)
    y_wait(up, 1, up)
    send_y(up, 1, down)
    to_sibling(up, 1)
    near(core, 0)
    from_sibling(down, 0)
    from_sibling(up, 1)
    near(1 - core, 0)

    y_wait(down, 1, down)
    to_sibling(down, 1)
    y_wait(up, 0, up)
    to_sibling(up, 0)
    near(core, 1)
    from_sibling(down, 1)
    from_sibling(up, 0)
    near(1 - core, 1)

    y_wait(far, 0, down)
    to_sibling(far, 0)
    y_wait(far, 1, up)
    to_sibling(far, 1)

    def pass1_far(side):
        @pl.loop(0, 2)
        def _(h):
            pass1(far * 2 + side, h)

    pass1_far(core)
    from_sibling(far, 0)
    from_sibling(far, 1)
    pass1_far(1 - core)

    place_c = row_to_col(place_r)
    pos_f[...] = jnp.zeros_like(pos_f)

    def slots_of(group):
        first = lax.broadcasted_iota(jnp.int32, (1, cap), 1)
        return jnp.concatenate([first + src * cap for src in group], axis=1).astype(F32)

    def place(first, end):
        @pl.loop(first, end)
        def _(k):
            group = one_of(k)
            wait_batch(k, returned, pos_r)
            pick = (place_c == slots_of(group)).astype(BF)
            pos_f[...] += dot(pick, jnp.concatenate([returned[src] for src in group], axis=0))

    place(0, len(batches))
    q_hat = acc[...]
    pos_e = pos_f[...]
    s_pos = INV_TEMP * jnp.sum(q_hat.astype(BF).astype(F32) * pos_e, axis=1, keepdims=True)
    neg_tot = row_to_col(jnp.sum(tot[...], axis=0, keepdims=True))
    lse = jnp.log(jnp.exp(s_pos) + neg_tot)
    loss_ref[...] = col_to_row(lse - s_pos)
    coef = jnp.exp(s_pos - lse) - 1.0
    inv_tot = jnp.exp(-lse)

    fw = width // 2
    g_bf[...] = (INV_TEMP * coef * q_hat).astype(BF)

    def g_copy(f, peer, k):
        return copy(outbox.at[f, peer], inbox.at[f, me], g_s.at[f], g_r.at[f, k], item=peer)

    @pl.loop(0, len(batches))
    def _(k):
        group = one_of(k)
        wanted = jnp.concatenate([iota((cap, 1), 0) + (src * cap).astype(F32) for src in group], axis=0)
        rows_out = dot((place_r == wanted).astype(BF), g_bf[...])
        for s, src in enumerate(group):
            for f in range(2):
                outbox[f, src] = rows_out[s * cap : (s + 1) * cap, f * fw : (f + 1) * fw].astype(BF)

            @pl.when(src != me)
            def _():
                g_copy(0, src, k).start()

    inbox[0, me] = outbox[0, me]
    inbox[1, me] = outbox[1, me]

    q_scaled = (q_hat.astype(BF).astype(F32) * (INV_TEMP * inv_tot)).astype(BF)

    def pass2(side):
        @pl.loop(0, n_dp)
        def _(d):
            for h in range(chips // half):
                at = slice(h * half, (h + 1) * half)
                p = dot(et[d * 2 + side, at].reshape(half * neg, ex), q_scaled)
                p = p.astype(BF).reshape(half, neg, width)
                for z in range(half):
                    part[side, h * half + z, pl.ds(pl.multiple_of(d * neg, neg), neg), :] = p[z]

    pass2(1 - core)
    to_sib = copy(part.at[1 - core], sib_in, sib_s, sib_r, item=sibling)
    to_sib.start()
    pass2(core)

    @pl.loop(0, len(batches))
    def _(k):
        for src in one_of(k):

            @pl.when(src != me)
            def _():
                g_copy(1, src, k).start()


    to_sib.wait_recv()

    side = math.isqrt(chips)
    nz, nx = (side, side) if side * side == chips else (1, chips)
    my_z, my_x = chip // nx, lax.rem(chip, nx)
    hn = n_dp * neg // 2

    @pl.loop(0, nz)
    def _(z):
        @pl.loop(0, nx)
        def _(x):
            at = z * nx + x
            both = (part[core, at].astype(F32) + sib_in[at].astype(F32)).astype(BF)
            by_x[x, z] = both[:hn]
            by_z[z, x] = both[hn:]

    def at_x(x):
        return (my_z * nx + x) * 2 + core

    def at_z(z):
        return (z * nx + my_x) * 2 + core

    def first_x(x):
        return copy(by_x.at[x], in_x.at[my_x], hop_s.at[0], hop_r.at[0], item=at_x(x))

    def first_z(z):
        return copy(by_z.at[z], in_z.at[my_z], hop_s.at[1], hop_r.at[1], item=at_z(z))

    def second_z(z):
        return copy(mid_z.at[z], end_z.at[my_z], hop_s.at[2], hop_r.at[2], item=at_z(z))

    def second_x(x):
        return copy(mid_x.at[x], end_x.at[my_x], hop_s.at[3], hop_r.at[3], item=at_x(x))

    def start_others(mine_at, count, make):
        @pl.loop(1, count)
        def _(off):
            make(lax.rem(mine_at + off, count)).start()

    def wait_others(buffer, count, **sem):
        if count > 1:
            wait_all(buffer.at[pl.ds(0, count - 1)], **sem)

    start_others(my_x, nx, first_x)
    start_others(my_z, nz, first_z)
    in_x[my_x] = by_x[my_x]
    in_z[my_z] = by_z[my_z]

    def wait_inbox(f):
        for k in range(len(batches)):
            wait_all(inbox.at[f, pl.ds(0, batch - 1 if k == own_batch else batch)], recv=g_r.at[f, k])

    def quarter_sum(f, d):
        total = jnp.zeros((quarter, fw), F32)
        for k in range(0, n_item, batch):
            ids = jnp.concatenate([req_in[src][:, :cap] for src in range(k, k + batch)], axis=1)
            came = inbox[f, k : k + batch].reshape(batch * cap, fw)
            total += dot(pick_rows(ids, (d * quarter).astype(F32), quarter), came)
        dense_f[f, pl.ds(pl.multiple_of(d * quarter, quarter), quarter), :] = total

    def rs_copy(f, block, h):
        if block == 0:
            return copy(rs_out.at[f, 0, h], relay_in.at[f, h], rs_s, relay_r.at[f, h], dp=(up, down)[h])
        return copy(rs_out.at[f, block, h], rs_in.at[f, block - 1, h], rs_s, rs_r.at[f, block - 1, h], dp=(up, down)[block - 1])

    def dense_part(f, d, h):
        return dense_f[f, pl.ds(pl.multiple_of(d * quarter + h * hq, hq), hq), :]

    def sum_and_send(f):
        @pl.loop(0, n_dp)
        def _(k):
            step_k = jnp.where(k == 0, 2, jnp.where(k == 1, 1, jnp.where(k == 2, 3, 0)))
            quarter_sum(f, lax.rem(y + step_k, n_dp))

            @pl.when(k == 0)
            def _():
                rs_out[f, 0, 0] = dense_part(f, far, 0).astype(BF)
                rs_copy(f, 0, 0).start()
                rs_out[f, 0, 1] = dense_part(f, far, 1).astype(BF)
                rs_copy(f, 0, 1).start()

            @pl.when(k == 1)
            def _():
                rs_out[f, 1, 1] = dense_part(f, up, 1).astype(BF)
                rs_copy(f, 1, 1).start()

            @pl.when(k == 2)
            def _():
                rs_out[f, 2, 0] = dense_part(f, down, 0).astype(BF)
                rs_copy(f, 2, 0).start()

    def relay(f):
        rs_copy(f, 0, 0).wait_recv()
        rs_out[f, 1, 0] = (dense_part(f, up, 0) + relay_in[f, 0].astype(F32)).astype(BF)
        rs_copy(f, 1, 0).start()
        rs_copy(f, 0, 1).wait_recv()
        rs_out[f, 2, 1] = (dense_part(f, down, 1) + relay_in[f, 1].astype(F32)).astype(BF)
        rs_copy(f, 2, 1).start()

    wait_inbox(0)
    sum_and_send(0)
    relay(0)
    wait_inbox(1)
    sum_and_send(1)
    relay(1)

    wait_others(in_x, nx, recv=hop_r.at[0])
    wait_others(in_z, nz, recv=hop_r.at[1])

    def added(buffer):
        total = buffer[0].astype(F32)
        for n in range(1, buffer.shape[0]):
            total += buffer[n].astype(F32)
        return total.astype(BF)

    mid_z[...] = added(in_x)
    mid_x[...] = added(in_z)
    start_others(my_z, nz, second_z)
    start_others(my_x, nx, second_x)
    end_z[my_z] = mid_z[my_z]
    end_x[my_x] = mid_x[my_x]

    wait_all(req_out.at[pl.ds(0, n_item - 1)], send=req_s)
    wait_all(found.at[pl.ds(0, n_item - 1)], send=pos_s)
    for f in range(2):
        wait_all(outbox.at[f, pl.ds(0, n_item - 1)], send=g_s.at[f])
    wait_all(negbuf.at[mine, pl.ds(0, chips - 1)], send=neg_s)
    wait_all(nidbuf.at[mine, pl.ds(0, chips - 1)], send=nid_s)
    wait_all(negbuf.at[pl.ds(0, 3)], send=pc_s)
    wait_all(nidbuf.at[pl.ds(0, 3)], send=pi_s)
    wait_all(negbuf.at[pl.ds(0, n_dp)], send=sn_s)
    wait_all(nidbuf.at[pl.ds(0, n_dp)], send=si_s)
    to_sib.wait_send()
    wait_others(by_x, nx, send=hop_s.at[0])
    wait_others(by_z, nz, send=hop_s.at[1])

    for f in range(2):
        for block in (1, 2):
            for h in range(2):
                rs_copy(f, block, h).wait_recv()
    for h in range(2):
        both = [dense_part(f, y, h) + rs_in[f, 0, h].astype(F32) + rs_in[f, 1, h].astype(F32) for f in range(2)]
        ag[y, h] = jnp.concatenate(both, axis=1).astype(BF)

    def ag_copy(slot, h, dest):
        return copy(ag.at[slot, h], ag.at[slot, h], ag_s, ag_r.at[slot, h], dp=dest)

    ag_copy(y, 0, up).start()
    ag_copy(y, 1, down).start()

    wait_others(end_z, nz, recv=hop_r.at[2])
    wait_others(end_x, nx, recv=hop_r.at[3])
    sums = jnp.concatenate([added(end_z), added(end_x)], axis=0)
    for d in range(n_dp):
        y_out[d] = sums[d * neg : (d + 1) * neg]
    y_in[y] = y_out[y]

    def part_copy(dest):
        return copy(y_out.at[dest], y_in.at[y], y_s.at[0], y_r.at[0], dp=dest)

    def sum_copy(dest):
        return copy(y_sum.at[y], y_sum.at[y], y_s.at[1], y_r.at[1], dp=dest)

    start_others(y, n_dp, part_copy)

    ag_copy(y, 1, up).start()
    ag_copy(y, 0, down).start()

    wait_others(y_in, n_dp, recv=y_r.at[0])
    y_sum[y] = added(y_in)
    start_others(y, n_dp, sum_copy)

    wait_recv(ag.at[down, 0], ag_s, ag_r.at[down, 0], dp=down)
    ag_copy(down, 0, up).start()
    wait_recv(ag.at[up, 1], ag_s, ag_r.at[up, 1], dp=up)
    ag_copy(up, 1, down).start()

    ut[...] = jnp.zeros_like(ut)

    @pl.loop(0, 2 * n_dp)
    def _(piece):
        block = negbuf[piece].reshape(chips * neg, width)
        eb = et[piece].reshape(chips * neg, ex)
        ut[...] += lax.dot_general(block, eb, (((0,), (0,)), ((), ())), preferred_element_type=F32)

    g_q = INV_TEMP * (coef * pos_f[...] + jnp.transpose(ut[...]) * inv_tot)
    grad_ref[...] = ((g_q - acc[...] * jnp.sum(acc[...] * g_q, axis=1, keepdims=True)) / q_norm).astype(BF)

    wait_others(y_sum, n_dp, recv=y_r.at[1])
    neg_sums = y_sum[...].reshape(n_dp * neg, width)
    neg_ids = jnp.concatenate([nidbuf[d * 2 + core, chip][:, :neg] for d in range(n_dp)], axis=1)

    def step(d, h):
        first = d * quarter + h * hq
        at = pl.ds(pl.multiple_of(first, hq), hq)
        pick = (neg_ids == iota((hq, n_dp * neg), 0) + first.astype(F32)).astype(BF)
        g = ag[d, h].astype(F32) + dot(pick, neg_sums)
        t = table_ref[at, :]
        norm = jnp.sqrt(jnp.sum(t * t, axis=1, keepdims=True) + EPSILON)
        unit = t / norm
        g_row = (g - unit * jnp.sum(unit * g, axis=1, keepdims=True)) / norm
        mean = jnp.sum(g_row * g_row, axis=1, keepdims=True) * (1.0 / width)
        new = state_ref[:, at] + col_to_row(mean)
        state_out[:, at] = new
        table_ref[at, :] = t - LEARN_RATE * g_row / jnp.sqrt(row_to_col(new))

    def step_both(d):
        @pl.loop(0, 2)
        def _(h):
            step(d, h)

    step_both(y)

    wait_recv(ag.at[down, 1], ag_s, ag_r.at[down, 1], dp=down)
    wait_recv(ag.at[up, 0], ag_s, ag_r.at[up, 0], dp=up)

    @pl.loop(0, 2)
    def _(k):
        step_both(lax.rem(y + 1 + 2 * k, n_dp))

    wait_recv(ag.at[far, 0], ag_s, ag_r.at[far, 0], dp=down)
    wait_recv(ag.at[far, 1], ag_s, ag_r.at[far, 1], dp=up)
    step_both(far)

    wait_others(mid_z, nz, send=hop_s.at[2])
    wait_others(mid_x, nx, send=hop_s.at[3])
    wait_others(y_out, n_dp, send=y_s.at[0])
    wait_others(y_sum, n_dp, send=y_s.at[1])
    wait_all(rs_out, send=rs_s)
    wait_all(ag.at[pl.ds(0, 3)], send=ag_s)


def write_kernel(grad_v, loss_v, table_v, state_v, grad, loss, table, state, sems):
    parts = sems.shape[0] - 3
    rows = table.shape[0] // parts
    pairs = [(table_v.at[pl.ds(k * rows, rows), :], table.at[pl.ds(k * rows, rows), :]) for k in range(parts)]
    pairs += [(grad_v, grad), (state_v, state), (loss_v, loss)]
    copies = [pltpu.make_async_copy(src, dst, sems.at[k]) for k, (src, dst) in enumerate(pairs)]
    for c in copies:
        c.start()
    for c in copies:
        c.wait()


def on_device(n_dp, n_item, queries, item_table, adagrad_state, pos_owner, pos_row, neg_rows):
    ex, width = queries.shape
    rows = item_table.shape[0]
    neg = neg_rows.shape[0]
    chips = n_item // 2
    cap = 3 * ex // n_item
    quarter = rows // n_dp
    vmem, hbm = pl.BlockSpec(memory_space=pltpu.VMEM), pl.BlockSpec(memory_space=pl.ANY)
    dma = pltpu.SemaphoreType.DMA
    n_neg = 2 * n_dp * chips * neg
    n_batches = n_item // min(8, n_item)
    side = math.isqrt(chips)
    nz, nx = (side, side) if side * side == chips else (1, chips)
    hn = n_dp * neg // 2
    flops = 2 * width * (3 * n_neg * ex + 3 * n_item * cap * (rows + ex))
    grad, loss, new_table, new_state = pl.pallas_call(
        functools.partial(main_kernel, n_dp, n_item),
        out_shape=(
            pltpu.VMEM((ex, width), BF),
            pltpu.VMEM((1, ex), F32),
            pltpu.VMEM((rows, width), F32),
            pltpu.VMEM((1, rows), F32),
        ),
        in_specs=[pl.BlockSpec(memory_space=pltpu.SMEM), hbm, hbm, vmem, vmem, vmem, vmem],
        out_specs=(vmem, vmem, vmem, vmem),
        scratch_shapes=[
            pltpu.VMEM((ex, width), BF),
            pltpu.VMEM((neg, width), F32),
            pltpu.VMEM((rows, width), BF),
            pltpu.VMEM((width, ex), BF),
            pltpu.VMEM((n_item, 1, LANES), F32),
            pltpu.VMEM((n_item, 1, LANES), F32),
            pltpu.VMEM((2 * n_dp, chips, neg, width), BF),
            pltpu.VMEM((2 * n_dp, chips, 1, LANES), F32),
            pltpu.VMEM((n_item, cap, width), BF),
            pltpu.VMEM((n_item, cap, width), BF),
            pltpu.VMEM((2, n_item, cap, width // 2), BF),
            pltpu.VMEM((2, n_item, cap, width // 2), BF),
            pltpu.VMEM((ex, width), F32),
            pltpu.VMEM((ex, width), F32),
            pltpu.VMEM((ex, width), BF),
            pltpu.VMEM((width, ex), F32),
            pltpu.VMEM((8, ex), F32),
            pltpu.VMEM((2 * n_dp, chips, neg, ex), BF),
            pltpu.VMEM((2, chips, n_dp * neg, width), BF),
            pltpu.VMEM((chips, n_dp * neg, width), BF),
            pltpu.VMEM((nx, nz, hn, width), BF),
            pltpu.VMEM((nz, nx, hn, width), BF),
            pltpu.VMEM((nx, nz, hn, width), BF),
            pltpu.VMEM((nz, nx, hn, width), BF),
            pltpu.VMEM((nx, hn, width), BF),
            pltpu.VMEM((nz, hn, width), BF),
            pltpu.VMEM((nx, hn, width), BF),
            pltpu.VMEM((nz, hn, width), BF),
            pltpu.VMEM((n_dp, neg, width), BF),
            pltpu.VMEM((n_dp, neg, width), BF),
            pltpu.VMEM((n_dp, neg, width), BF),
            pltpu.VMEM((2, rows, width // 2), F32),
            pltpu.VMEM((2, 3, 2, quarter // 2, width // 2), BF),
            pltpu.VMEM((2, 2, quarter // 2, width // 2), BF),
            pltpu.VMEM((2, 2, 2, quarter // 2, width // 2), BF),
            pltpu.VMEM((n_dp, 2, quarter // 2, width), BF),
            dma, dma,
            dma, dma,
            dma, dma,
            dma, dma((n_dp, 2)),
            dma, dma((n_dp, 2)),
            dma, dma((n_dp, 2)),
            dma, dma((n_dp, 2)),
            dma, dma((n_batches,)),
            dma((2,)), dma((2, n_batches)),
            dma, dma,
            dma((4,)), dma((4,)),
            dma((2,)), dma((2,)),
            dma, dma((2, 2)), dma((2, 2, 2)),
            dma, dma((n_dp, 2)),
            dma, dma,
        ],
        compiler_params=pltpu.CompilerParams(collective_id=0, has_side_effects=True, vmem_limit_bytes=56 * 2**20),
        cost_estimate=pl.CostEstimate(flops=flops, bytes_accessed=12 * 2**20, transcendentals=n_neg * ex),
        name="training_step",
    )(
        neg_rows, queries, item_table, adagrad_state.reshape(1, rows), pos_owner.reshape(1, ex), pos_row.reshape(1, ex),
        neg_rows.reshape(1, neg),
    )

    made = [pltpu.with_memory_space_constraint(a, pltpu.VMEM) for a in (grad, loss, new_table, new_state)]
    grad, loss, new_table, new_state = pl.pallas_call(
        write_kernel,
        out_shape=[jax.ShapeDtypeStruct(a.shape, a.dtype) for a in made],
        in_specs=[vmem] * 4,
        out_specs=[hbm] * 4,
        scratch_shapes=[dma((11,))],
        compiler_params=pltpu.CompilerParams(vmem_limit_bytes=2**20),
        name="write_results",
    )(*made)
    return grad, loss.reshape(ex), new_table, new_state.reshape(rows)


def solution(mesh):
    both = ("dp", "item")
    return jax.shard_map(
        functools.partial(on_device, mesh.shape["dp"], mesh.shape["item"]),
        mesh=mesh,
        in_specs=(P(both, None), P("item", None), P("item"), P(both, None), P(both), P(both)),
        out_specs=(P(both, None), P(both), P("item", None), P("item")),
        check_vma=False,
    )
```
